32 devices in a mesh: dp: 8 (over z, x), tensor: 4 (over y, core).
Axes of the slice: x: 2, y: 2, z: 4, core: 2. Of those that a mesh axis runs over, the one named last changes fastest.
Arguments:
- tokens: bfloat16 [24576, 768], P('dp'), may hold values from -6 to 6
- buckets: int32 [24], P('dp'), may hold values from 0 to 8
- norm1_gain: bfloat16 [768], replicated, may hold values from 0.099609375 to 1.8984375
- norm1_bias: bfloat16 [768], replicated, may hold values from -3 to 3
- qkv_weight: bfloat16 [3, 768, 768], P(None, None, 'tensor'), may hold values from -0.21875 to 0.21875
- qkv_bias: bfloat16 [2, 768], P(None, 'tensor'), may hold values from -3 to 3
- out_weight: bfloat16 [768, 768], P('tensor'), may hold values from -0.21875 to 0.21875
- out_bias: bfloat16 [768], replicated, may hold values from -3 to 3
- norm2_gain: bfloat16 [768], replicated, may hold values from 0.099609375 to 1.8984375
- norm2_bias: bfloat16 [768], replicated, may hold values from -3 to 3
- up_weight: bfloat16 [768, 3072], P(None, 'tensor'), may hold values from -0.21875 to 0.21875
- up_bias: bfloat16 [3072], P('tensor'), may hold values from -3 to 3
- down_weight: bfloat16 [3072, 768], P('tensor'), may hold values from -0.109375 to 0.109375
- down_bias: bfloat16 [768], replicated, may hold values from -3 to 3
- cotangent: bfloat16 [24576, 768], P('dp'), may hold values from -6 to 6
Outputs:
- layer_out: bfloat16 [24576, 768], P(('dp', 'tensor'))
- input_grad: bfloat16 [24576, 768], P(('dp', 'tensor'))
- norm1_gain_grad: float32 [768], replicated
- norm1_bias_grad: float32 [768], replicated
- qkv_weight_grad: float32 [3, 768, 768], P(None, 'dp', 'tensor')
- qkv_bias_grad: float32 [2, 768], P(None, 'tensor')
- out_weight_grad: float32 [768, 768], P('tensor', 'dp')
- out_bias_grad: float32 [768], replicated
- norm2_gain_grad: float32 [768], replicated
- norm2_bias_grad: float32 [768], replicated
- up_weight_grad: float32 [768, 3072], P('dp', 'tensor')
- up_bias_grad: float32 [3072], P('tensor')
- down_weight_grad: float32 [3072, 768], P('tensor', 'dp')
- down_bias_grad: float32 [768], replicated
The draws below stay inside these ranges and needn't reach their ends.
Inputs may be any that keep to these rules, and one draw needn't show every extreme that they name: `buckets`: bucket id of each image, naming its grid of patches as in the reference program.
All inputs are finite; a program needn't handle non-finite values.
Results may differ from the reference program's by a relative error of at most 0.018.
Values may be sent and summed in bfloat16 or wider, within the bound.
A program may use at most 256 MiB of HBM per device.

```python
from functools import partial
import jax
import jax.numpy as jnp
from jax import lax

D = 768
HEADS = 12
DH = 64
FF = 3072
IMG_LEN = 1024
IMG_DEV = 3
TOK_DEV = 3072
IMAGES = 24
TOKENS = 24576
N_DP = 8


def set_ends(values, rng, smallest, largest):
    extent = values.shape
    place = [jax.random.randint(jax.random.fold_in(rng, axis), (), 0, extent[axis]) for axis in range(len(extent))]
    values = values.at[tuple(place)].set(smallest)
    longest = extent.index(max(extent))
    place[longest] = (place[longest] + 1) % extent[longest]
    return values.at[tuple(place)].set(largest)


def with_spikes(entries, own_key, source, target, parts, factor):
    owner, partner = [(jnp.arange(entries.shape[position]) // (entries.shape[position] // parts)).reshape([-1 if axis == position else 1 for axis in range(entries.ndim)]) for position in (source, target)]
    chosen = jax.random.permutation(own_key, parts)[partner]
    strong = (owner == chosen) | (owner == (partner + parts // 2) % parts)
    return jnp.where(strong, factor * entries, entries)


def block_levels(stream_key, dims, split, low, top_value):
    gain, own = 1.0, jax.random.fold_in(stream_key, 6)
    for dim, blocks in split:
        steps = jnp.exp(jax.random.uniform(jax.random.fold_in(own, dim), (blocks,), jnp.float32, low / len(split), top_value / len(split)))
        gain = gain * jnp.repeat(steps, dims[dim] // blocks).reshape([-1 if axis == dim else 1 for axis in range(len(dims))])
    return gain


def scatter_about(stream_key, dims, scale, reach, pieces=(), kind=jnp.bfloat16):
    loudness = block_levels(stream_key, dims, pieces, -0.22, 0.18) if pieces else 1.0
    values = jax.random.normal(stream_key, dims, jnp.float32) * scale * loudness
    return jnp.minimum(jnp.maximum(values, -reach), reach).astype(kind)


def heavy_noise(rng, extent, scale, limit, split, heavy, held_as=jnp.bfloat16):
    values = scale * jax.random.normal(rng, extent, jnp.float32)
    if split:
        values = values * block_levels(rng, extent, split, -0.22, 0.18)
    return jnp.clip(with_spikes(values, jax.random.fold_in(rng, 3), *heavy), -limit, limit).astype(held_as)


def setup_inputs(seed: int = 0) -> dict:
    key_of = jax.random.split(jax.random.key(seed), 16)
    return {
        "tokens": scatter_about(key_of[0], (TOKENS, D), 1.0, 6.0, ((0, 8),)),
        "buckets": set_ends(jax.random.randint(key_of[1], (IMAGES,), 0, 9), jax.random.fold_in(key_of[1], 1), 0, 8).astype(jnp.int32),
        "norm1_gain": jnp.clip(1.0 + 0.18 * jax.random.normal(key_of[2], (D,), jnp.float32), 0.099609375, 1.8984375).astype(jnp.bfloat16),
        "norm1_bias": scatter_about(key_of[3], (D,), 0.5, 3.0),
        "qkv_weight": scatter_about(key_of[4], (3, D, D), D ** -0.5, 0.21875, ((2, 4),)),
        "qkv_bias": scatter_about(key_of[5], (2, D), 0.5, 3.0, ((1, 4),)),
        "out_weight": scatter_about(key_of[6], (D, D), D ** -0.5, 0.21875, ((0, 4),)),
        "out_bias": scatter_about(key_of[7], (D,), 0.5, 3.0),
        "norm2_gain": jnp.clip(1.0 + 0.18 * jax.random.normal(key_of[8], (D,), jnp.float32), 0.099609375, 1.8984375).astype(jnp.bfloat16),
        "norm2_bias": scatter_about(key_of[9], (D,), 0.5, 3.0),
        "up_weight": scatter_about(key_of[10], (D, FF), D ** -0.5, 0.21875, ((1, 4),)),
        "up_bias": scatter_about(key_of[11], (FF,), 0.5, 3.0, ((0, 4),)),
        "down_weight": scatter_about(key_of[12], (FF, D), FF ** -0.5, 0.109375, ((0, 4),)),
        "down_bias": scatter_about(key_of[13], (D,), 0.5, 3.0),
        "cotangent": heavy_noise(key_of[14], (TOKENS, D), 1.0, 6.0, ((0, 8),), (0, 1, 8, 2.0)),
    }


@jax.custom_vjp
def low(v):
    return lax.optimization_barrier(v.astype(jnp.bfloat16)).astype(jnp.float32)

@jax.custom_vjp
def low_back(v):
    return v

def low_keep(v):
    return (low(v), None)

def low_pass(kept, grad):
    return (grad,)

def back_keep(v):
    return (v, None)

def back_low(kept, grad):
    return (low(grad),)
low.defvjp(low_keep, low_pass)
low_back.defvjp(back_keep, back_low)
NORM_EPSILON = 1e-06
GRID_SIXTEENTHS = (16, 15, 15, 12, 12, 8, 8, 6, 6)
NEG_FILL = -1e+30

def product(left, right):
    return jnp.dot(left, right, precision=lax.Precision.HIGHEST, preferred_element_type=jnp.float32)

def normalize(values, gain_row, shift_row):
    centre = lax.optimization_barrier(jnp.mean(values, axis=-1, keepdims=True))
    centred = values - centre
    spread = lax.optimization_barrier(jnp.mean(centred * centred, axis=-1, keepdims=True))
    return centred * lax.rsqrt(spread + NORM_EPSILON) * gain_row + shift_row

def both_ways(values):
    return low(low_back(values))

def grid_lengths(buckets):
    table_row = jnp.asarray(GRID_SIXTEENTHS, dtype=jnp.int32)
    chosen = (buckets[:, None] == jnp.arange(len(GRID_SIXTEENTHS), dtype=jnp.int32)[None, :]).astype(jnp.int32)
    return IMG_LEN * lax.optimization_barrier(jnp.sum(chosen * table_row[None, :], axis=1)) // 16

def attend(image_item):
    queries, key_rows, value_rows, length = image_item
    scores = jnp.einsum('qhd,khd->hqk', queries, key_rows, precision=lax.Precision.HIGHEST) * DH ** (-0.5)
    key_mask = jnp.arange(IMG_LEN, dtype=jnp.int32) < length
    scores = low_back(jnp.where(key_mask[None, None, :], scores, NEG_FILL))
    prob_rows = low(jax.nn.softmax(scores, axis=-1))
    return jnp.einsum('hqk,khd->qhd', prob_rows, value_rows, precision=lax.Precision.HIGHEST)

def forward(lengths, block, gain_one, shift_one, qkv_weight, qkv_bias, out_weight, out_bias, gain_two, shift_two, up_weight, up_bias, down_weight, down_bias):
    normed_one = low(normalize(block, gain_one, shift_one))
    queries = both_ways(product(normed_one, qkv_weight[0]) + qkv_bias[0])
    key_rows = both_ways(product(normed_one, qkv_weight[1]))
    value_rows = both_ways(product(normed_one, qkv_weight[2]) + qkv_bias[1])
    per_image = (IMG_DEV, IMG_LEN, HEADS, DH)
    mixed_rows = lax.map(jax.checkpoint(attend), (queries.reshape(per_image), key_rows.reshape(per_image), value_rows.reshape(per_image), lengths))
    mixed_rows = both_ways(mixed_rows.reshape(TOK_DEV, D))
    hidden_one = block + low_back(product(mixed_rows, out_weight)) + out_bias
    normed_two = low(normalize(hidden_one, gain_two, shift_two))
    upper = low_back(product(normed_two, up_weight) + up_bias)
    active = low(jax.nn.gelu(upper, approximate=True))
    return hidden_one + low_back(product(active, down_weight)) + down_bias

def reference(tokens, buckets, norm1_gain, norm1_bias, qkv_weight, qkv_bias, out_weight, out_bias, norm2_gain, norm2_bias, up_weight, up_bias, down_weight, down_bias, cotangent):
    params = [p.astype(jnp.float32) for p in (norm1_gain, norm1_bias, qkv_weight, qkv_bias, out_weight, out_bias, norm2_gain, norm2_bias, up_weight, up_bias, down_weight, down_bias)]
    lengths = grid_lengths(buckets).reshape(N_DP, IMG_DEV)
    blocks = tokens.astype(jnp.float32).reshape(N_DP, TOK_DEV, D)
    cot_blocks = cotangent.astype(jnp.float32).reshape(N_DP, TOK_DEV, D)

    def step(totals, block_item):
        block, cot_block, block_lengths = block_item
        result, back = jax.vjp(partial(forward, block_lengths), block, *params)
        grads = back(cot_block)
        totals = [t + g for t, g in zip(totals, grads[1:])]
        return (totals, (result.astype(jnp.bfloat16), grads[0].astype(jnp.bfloat16)))
    initial = [jnp.zeros(p.shape, jnp.float32) for p in params]
    totals, (outputs, input_grads) = lax.scan(step, initial, (blocks, cot_blocks, lengths))
    return (outputs.reshape(TOKENS, D), input_grads.reshape(TOKENS, D), totals[0], totals[1], totals[2], totals[3], totals[4], totals[5], totals[6], totals[7], totals[8], totals[9], totals[10], totals[11])
```

```python
import functools

import jax
import jax.numpy as jnp
from jax import lax
from jax.experimental import pallas as pl
from jax.experimental.pallas import tpu as pltpu
from jax.sharding import PartitionSpec as P

DH = 64
NORM_EPSILON = 1e-06
GRID_SIXTEENTHS = (16, 15, 15, 12, 12, 8, 8, 6, 6)
GELU_SCALE = 0.7978845608028654
GELU_CUBE = 0.044715
VMEM = 60 << 20
NN = (((1,), (0,)), ((), ()))
NT = (((1,), (1,)), ((), ()))
TN = (((0,), (0,)), ((), ()))
bf16 = jnp.bfloat16
f32 = jnp.float32
ANY = pl.BlockSpec(memory_space=pl.ANY)


def dot(left, right, dims=NN):
    return lax.dot_general(left, right, dims, preferred_element_type=f32)


def lanes(rows, width):
    return lax.broadcasted_iota(jnp.int32, (rows, width), 1)


def live_lengths(image_len):
    return sorted({image_len * s // 16 for s in GRID_SIXTEENTHS})


def live_length(bucket, image_len):
    length = jnp.int32(0)
    for index, sixteenths in enumerate(GRID_SIXTEENTHS):
        length = jnp.where(bucket == index, image_len * sixteenths // 16, length)
    return length


def cost(flops, nbytes, transcendentals=0):
    return pl.CostEstimate(flops=flops, bytes_accessed=nbytes, transcendentals=transcendentals)


def split3(values):
    high = values.astype(bf16).astype(f32)
    middle = (values - high).astype(bf16).astype(f32)
    return high, middle, values - high - middle


def unit_rows(values):
    centred = values - jnp.mean(values, axis=-1, keepdims=True)
    spread = jnp.mean(centred * centred, axis=-1, keepdims=True)
    inverse = lax.rsqrt(spread + NORM_EPSILON)
    return centred * inverse, inverse


def norm_back(grad, gain, unit, inverse):
    scaled = grad * gain
    mean_one = jnp.mean(scaled, axis=-1, keepdims=True)
    mean_two = jnp.mean(scaled * unit, axis=-1, keepdims=True)
    return inverse * (scaled - mean_one - unit * mean_two)


def project_kernel(x_ref, gain_ref, shift_ref, w_ref, bias_ref, q_ref, k_ref, v_ref):
    unit, _ = unit_rows(x_ref[...].astype(f32))
    normed = (unit * gain_ref[...].astype(f32) + shift_ref[...].astype(f32)).astype(bf16)
    bias = bias_ref[...].astype(f32)
    q_ref[...] = (dot(normed, w_ref[0]) + bias[0:1]).astype(bf16)
    k_ref[...] = dot(normed, w_ref[1]).astype(bf16)
    v_ref[...] = (dot(normed, w_ref[2]) + bias[1:2]).astype(bf16)


def project(tokens, gain, shift, weight, bias):
    rows, width = tokens.shape
    cols = weight.shape[2]
    block = 512
    out = pl.BlockSpec((block, cols), lambda i: (i, 0))
    whole = lambda shape: pl.BlockSpec(shape, lambda i: (0,) * len(shape))
    return pl.pallas_call(
        project_kernel,
        grid=(rows // block,),
        in_specs=[
            pl.BlockSpec((block, width), lambda i: (i, 0)),
            whole((1, width)),
            whole((1, width)),
            whole(weight.shape),
            whole(bias.shape),
        ],
        out_specs=[out] * 3,
        out_shape=[jax.ShapeDtypeStruct((rows, cols), bf16)] * 3,
        compiler_params=pltpu.CompilerParams(vmem_limit_bytes=VMEM),
        cost_estimate=cost(6 * rows * width * cols, 2 * rows * (width + 3 * cols)),
        name="project",
    )(tokens, gain, shift, weight, bias)


def attend_kernel(bucket_ref, q_ref, k_ref, v_ref, o_ref, qx_ref, kx, vt, *, block):
    image_len, cols = q_ref.shape
    heads = cols // DH
    length = live_length(bucket_ref[pl.program_id(0)], image_len)
    for live in live_lengths(image_len):

        @pl.when(length == live)
        def _():
            scaled = k_ref[0:live, :] * jnp.asarray(0.125, bf16)
            flipped = jnp.transpose(v_ref[0:live, :])
            lane = lanes(live, 128)
            for h in range(heads):
                if h < 2:
                    keep = (lane < DH) if h == 0 else (lane >= DH)
                    kx[h, 0:live, :] = jnp.where(keep, scaled[:, 0:128], jnp.zeros((), bf16))
                else:
                    kx[h, 0:live, 0:DH] = scaled[:, 128:192]
                vt[h, 0:DH, 0:live] = flipped[DH * h : DH * (h + 1)]
                vt[h, DH:128, 0:live] = jnp.ones((DH, live), bf16)

            def scores(h, start):
                if h < 2:
                    return dot(kx[h, 0:live, :], q_ref[start : start + block, 0:128], NT)
                return dot(kx[h, 0:live, 0:DH], q_ref[start : start + block, 128:192], NT)

            parts = {}

            def finish(h, start, score):
                top = jnp.max(score, axis=0, keepdims=True)
                weights = jnp.exp(score - top).astype(bf16)
                mixed = dot(vt[h, :, 0:live], weights)
                total = mixed[DH : DH + 1]
                parts[h] = (mixed[:DH] * (1.0 / total), split3(-(top + jnp.log(total))))
                if h == heads - 1:
                    stack = [parts[i][0] for i in range(heads)]
                    stack += [parts[i][1][j] for i in range(heads) for j in range(3)]
                    stack += [jnp.zeros((DH - 3 * heads, block), f32)]
                    turned = jnp.transpose(jnp.concatenate(stack, axis=0).astype(bf16))
                    here = slice(start, start + block)
                    o_ref[here, :] = turned[:, 0:cols]
                    qx_ref[here, :] = jnp.concatenate([q_ref[here, :], turned[:, cols:]], axis=1)

            items = [(h, s) for s in range(0, image_len, block) for h in range(heads)]
            score = scores(*items[0])
            for index, item in enumerate(items):
                following = scores(*items[index + 1]) if index + 1 < len(items) else None
                finish(*item, score)
                score = following


def attend(buckets, q, k, v):
    rows, cols = q.shape
    images = buckets.shape[0]
    image_len = rows // images
    heads = cols // DH
    spec = pl.BlockSpec((image_len, cols), lambda i, b: (i, 0))
    return pl.pallas_call(
        functools.partial(attend_kernel, block=512),
        grid_spec=pltpu.PrefetchScalarGridSpec(
            num_scalar_prefetch=1,
            grid=(images,),
            in_specs=[spec] * 3,
            out_specs=[spec, pl.BlockSpec((image_len, 256), lambda i, b: (i, 0))],
            scratch_shapes=[
                pltpu.VMEM((heads, image_len, 128), bf16),
                pltpu.VMEM((heads, 128, image_len), bf16),
            ],
        ),
        out_shape=[
            jax.ShapeDtypeStruct((rows, cols), bf16),
            jax.ShapeDtypeStruct((rows, 256), bf16),
        ],
        compiler_params=pltpu.CompilerParams(vmem_limit_bytes=VMEM),
        cost_estimate=cost(16 * rows * image_len * cols, 12 * rows * cols, rows * image_len * heads),
        name="attend",
    )(buckets, q, k, v)


def attend_back_kernel(
    bucket_ref, qx_ref, k_ref, v_ref, o_ref, do_ref, dq_ref, dk_ref, dv_ref,
    dox, dot_t, q_t, kx, vx, k_t, *, block,
):
    image_len, cols = o_ref.shape
    heads = cols // DH
    length = live_length(bucket_ref[pl.program_id(0)], image_len)
    product = do_ref[...].astype(f32) * o_ref[...].astype(f32)
    high = product.astype(bf16)
    low = (product - high.astype(f32)).astype(bf16)
    row = lax.broadcasted_iota(jnp.int32, (cols, DH), 0)
    lane = lanes(cols, DH)
    pick = jnp.where(row // DH == lane // 3, 1.0, 0.0).astype(bf16)
    inner = split3(-(dot(high, pick) + dot(low, pick)))
    lane = lanes(image_len, DH)
    which = lane % 3
    inner = jnp.where(which == 0, inner[0], jnp.where(which == 1, inner[1], inner[2]))
    inner = jnp.where(lane < 3 * heads, inner, 0.0).astype(bf16)
    extended = jnp.concatenate([do_ref[...], inner], axis=1)
    dox[...] = extended
    dot_t[...] = jnp.transpose(extended)
    q_t[...] = jnp.transpose(qx_ref[...])
    for live in live_lengths(image_len):

        @pl.when(length == live)
        def _():
            if live < image_len:
                blank = jnp.zeros((image_len - live, cols), bf16)
                dk_ref[live:image_len, :] = blank
                dv_ref[live:image_len, :] = blank
            lane = lanes(live, cols)
            side = lanes(live, DH)
            scaled = k_ref[0:live, :] * jnp.asarray(0.125, bf16)
            values = v_ref[0:live, :]
            k_t[0:cols, 0:live] = jnp.transpose(scaled)
            zero = jnp.zeros((), bf16)
            for h in range(heads):
                keep = (lane >= DH * h) & (lane < DH * (h + 1))
                ones = jnp.where((side >= 3 * h) & (side < 3 * h + 3), 1.0, 0.0).astype(bf16)
                kx[h, 0:live, :] = jnp.concatenate([jnp.where(keep, scaled, zero), ones], axis=1)
                vx[h, 0:live, :] = jnp.concatenate([jnp.where(keep, values, zero), ones], axis=1)
            parts, grad_q = {}, {}
            for start in range(0, live, block):
                end = min(live, start + block)
                for h in range(heads):
                    probs = jnp.exp(dot(kx[h, start:end, :], qx_ref[...], NT))
                    grad_probs = dot(vx[h, start:end, :], dox[...], NT)
                    grad_scores = (probs * grad_probs).astype(bf16)
                    pair = slice(0, 128) if h < 2 else slice(128, 256)
                    own = slice(DH * (h % 2), DH * (h % 2) + DH)
                    grad_v = dot(dot_t[pair, :], probs.astype(bf16), NT)[own]
                    grad_k = dot(q_t[pair, :], grad_scores, NT)[own]
                    parts[h] = (grad_v, grad_k)
                    step = dot(k_t[pair, start:end], grad_scores)[own]
                    grad_q[h] = step if start == 0 else grad_q[h] + step
                grad_v = jnp.concatenate([parts[h][0] for h in range(heads)], axis=0)
                grad_k = jnp.concatenate([parts[h][1] for h in range(heads)], axis=0) * 0.125
                dv_ref[start:end, :] = jnp.transpose(grad_v.astype(bf16))
                dk_ref[start:end, :] = jnp.transpose(grad_k.astype(bf16))
            whole = jnp.concatenate([grad_q[h] for h in range(heads)], axis=0)
            dq_ref[...] = jnp.transpose(whole.astype(bf16))


def attend_back(buckets, qx, k, v, o, grad_o):
    rows, cols = o.shape
    images = buckets.shape[0]
    image_len = rows // images
    heads = cols // DH
    spec = pl.BlockSpec((image_len, cols), lambda i, b: (i, 0))
    return pl.pallas_call(
        functools.partial(attend_back_kernel, block=256),
        grid_spec=pltpu.PrefetchScalarGridSpec(
            num_scalar_prefetch=1,
            grid=(images,),
            in_specs=[pl.BlockSpec((image_len, 256), lambda i, b: (i, 0))] + [spec] * 4,
            out_specs=[spec] * 3,
            scratch_shapes=[
                pltpu.VMEM((image_len, 256), bf16),
                pltpu.VMEM((256, image_len), bf16),
                pltpu.VMEM((256, image_len), bf16),
                pltpu.VMEM((heads, image_len, 256), bf16),
                pltpu.VMEM((heads, image_len, 256), bf16),
                pltpu.VMEM((256, image_len), bf16),
            ],
        ),
        out_shape=[jax.ShapeDtypeStruct((rows, cols), bf16)] * 3,
        compiler_params=pltpu.CompilerParams(vmem_limit_bytes=VMEM),
        cost_estimate=cost(40 * rows * image_len * cols, 16 * rows * cols, rows * image_len * heads),
        name="attend_back",
    )(buckets, qx, k, v, o, grad_o)


def rows_kernel(*refs, parts):
    it = iter(refs)
    take = lambda count: [next(it) for _ in range(count)]
    x_ref, g_ref, out_bias, gain_ref, shift_ref, down_bias, up_bias = take(7)
    o_in, wo_in, up_in, down_in = take(parts), take(parts), take(parts), take(parts)
    y_ref, dh_ref, grads_ref, wo_grad_ref, small_ref, up_small_ref = take(6)
    do_refs = take(parts)
    up_w, down_w, hidden, normed, mixed, back, sems = take(7)
    part = pl.program_id(0)
    copies = []
    for r in range(parts):
        copies.append(pltpu.make_async_copy(up_in[r], up_w.at[r], sems.at[0, r]))
        copies.append(pltpu.make_async_copy(down_in[r], down_w.at[r], sems.at[1, r]))
    gain = gain_ref[...].astype(f32)

    @pl.when(part == 0)
    def _():
        for copy in copies:
            copy.start()
        attended = dot(o_in[0][...], wo_in[0][...])
        for r in range(1, parts):
            attended += dot(o_in[r][...], wo_in[r][...])
        h1 = x_ref[...].astype(f32) + attended + out_bias[...].astype(f32)
        hidden[...] = h1
        unit, _ = unit_rows(h1)
        normed[...] = (unit * gain + shift_ref[...].astype(f32)).astype(bf16)

    for r in range(parts):

        @pl.when(part == r)
        def _():
            copies[2 * r].wait()
            copies[2 * r + 1].wait()

    g = g_ref[...]
    c = normed[...]
    width = up_w.shape[2]
    step = width // 2
    for start in range(0, width, step):
        cols = slice(start, start + step)
        u = dot(c, up_w[part, :, cols]) + up_bias[0, :, cols].astype(f32)
        square = u * u
        scaled = u * GELU_SCALE
        gate = 0.5 + 0.5 * jnp.tanh(scaled * (1.0 + GELU_CUBE * square))
        z = (u * gate).astype(bf16)
        slope = gate + 2.0 * gate * (1.0 - gate) * scaled * (1.0 + (3.0 * GELU_CUBE) * square)
        dz = dot(g, down_w[part, cols, :], NT)
        wide = dz * slope
        du = wide.astype(bf16)
        up_small_ref[0, :, cols] = jnp.sum(du.astype(f32), axis=0, keepdims=True)
        forward = dot(z, down_w[part, cols, :])
        backward = dot(du, up_w[part, :, cols], NT)
        if start == 0:

            @pl.when(part == 0)
            def _():
                mixed[...] = forward
                back[...] = backward

            @pl.when(part > 0)
            def _():
                mixed[...] += forward
                back[...] += backward
        else:
            mixed[...] += forward
            back[...] += backward
        grads_ref[0, :, cols] = dot(g, z, TN).astype(bf16)
        grads_ref[0, :, slice(width + start, width + start + step)] = dot(c, du, TN).astype(bf16)

    @pl.when(part == parts - 1)
    def _():
        h1 = hidden[...]
        y_ref[...] = (h1 + mixed[...] + down_bias[...].astype(f32)).astype(bf16)
        unit, inverse = unit_rows(h1)
        dc = back[...]
        wide_g = g.astype(f32)
        dh = wide_g + norm_back(dc, gain, unit, inverse)
        dh_ref[...] = dh
        e = dh.astype(bf16)
        sums = [dc * unit, dc, dh, wide_g]
        for index, values in enumerate(sums):
            small_ref[index : index + 1, :] = jnp.sum(values, axis=0, keepdims=True)
        small_ref[len(sums) :, :] = jnp.zeros_like(small_ref[len(sums) :, :])
        for r in range(parts):
            do_refs[r][...] = dot(e, wo_in[r][...], NT).astype(bf16)
            wo_grad_ref[r] = dot(e, o_in[r][...], TN).astype(bf16)


def own_rows(x, g, out_bias, gain, shift, down_bias, up_bias, o_parts, wo_parts, up_parts, down_parts):
    parts = len(o_parts)
    rows, width = x.shape
    cols = o_parts[0].shape[1]
    hid = up_parts[0].shape[1]
    fixed = lambda shape: pl.BlockSpec(shape, lambda r: (0,) * len(shape))
    row = fixed((1, width))
    out_shape = [
        jax.ShapeDtypeStruct((rows, width), bf16),
        jax.ShapeDtypeStruct((rows, width), f32),
        jax.ShapeDtypeStruct((parts, width, 2 * hid), bf16),
        jax.ShapeDtypeStruct((parts, width, cols), bf16),
        jax.ShapeDtypeStruct((8, width), f32),
        jax.ShapeDtypeStruct((parts, 1, hid), f32),
    ] + [jax.ShapeDtypeStruct((rows, cols), bf16)] * parts
    return pl.pallas_call(
        functools.partial(rows_kernel, parts=parts),
        grid=(parts,),
        in_specs=[fixed((rows, width))] * 2
        + [row] * 4
        + [pl.BlockSpec((1, 1, hid), lambda r: (r, 0, 0))]
        + [fixed((rows, cols))] * parts
        + [fixed((cols, width))] * parts
        + [ANY] * (2 * parts),
        out_specs=[
            fixed((rows, width)),
            fixed((rows, width)),
            pl.BlockSpec((1, width, 2 * hid), lambda r: (r, 0, 0)),
            fixed((parts, width, cols)),
            fixed((8, width)),
            pl.BlockSpec((1, 1, hid), lambda r: (r, 0, 0)),
        ]
        + [fixed((rows, cols))] * parts,
        out_shape=out_shape,
        scratch_shapes=[
            pltpu.VMEM((parts, width, hid), bf16),
            pltpu.VMEM((parts, hid, width), bf16),
            pltpu.VMEM((rows, width), f32),
            pltpu.VMEM((rows, width), bf16),
            pltpu.VMEM((rows, width), f32),
            pltpu.VMEM((rows, width), f32),
            pltpu.SemaphoreType.DMA((2, parts)),
        ],
        compiler_params=pltpu.CompilerParams(vmem_limit_bytes=VMEM),
        cost_estimate=cost(12 * rows * width * hid * parts, 8 * parts * width * hid, rows * hid * parts),
        name="own_rows",
    )(x, g, out_bias, gain, shift, down_bias, up_bias, *o_parts, *wo_parts, *up_parts, *down_parts)


def project_back_kernel(
    x_ref, gain_ref, shift_ref, w_ref, dq_ref, dk_ref, dv_ref,
    da_ref, dw_ref, small_ref, bias_ref, total, sums, bias_sums,
):
    image = pl.program_id(0)
    last = pl.num_programs(0) - 1
    unit, _ = unit_rows(x_ref[...].astype(f32))
    normed = (unit * gain_ref[...].astype(f32) + shift_ref[...].astype(f32)).astype(bf16)
    grads = [dq_ref[...], dk_ref[...], dv_ref[...]]
    da = dot(grads[0], w_ref[0], NT) + dot(grads[1], w_ref[1], NT) + dot(grads[2], w_ref[2], NT)
    da_ref[...] = da.astype(bf16)

    @pl.when(image == 0)
    def _():
        total[...] = jnp.zeros_like(total)
        sums[...] = jnp.zeros_like(sums)
        bias_sums[...] = jnp.zeros_like(bias_sums)

    for j in range(3):
        total[j] += dot(normed, grads[j], TN)
    sums[0:1, :] += jnp.sum(da * unit, axis=0, keepdims=True)
    sums[1:2, :] += jnp.sum(da, axis=0, keepdims=True)
    bias_sums[0:1, :] += jnp.sum(grads[0].astype(f32), axis=0, keepdims=True)
    bias_sums[1:2, :] += jnp.sum(grads[2].astype(f32), axis=0, keepdims=True)

    @pl.when(image == last)
    def _():
        dw_ref[...] = total[...].astype(bf16)
        small_ref[...] = sums[...]
        bias_ref[...] = bias_sums[...]


def project_back(tokens, gain, shift, weight, dq, dk, dv, images):
    rows, width = tokens.shape
    cols = dq.shape[1]
    block = rows // images
    fixed = lambda shape: pl.BlockSpec(shape, lambda i: (0,) * len(shape))
    by_rows = lambda w: pl.BlockSpec((block, w), lambda i: (i, 0))
    return pl.pallas_call(
        project_back_kernel,
        grid=(images,),
        in_specs=[by_rows(width), fixed((1, width)), fixed((1, width)), fixed(weight.shape)]
        + [by_rows(cols)] * 3,
        out_specs=[by_rows(width), fixed(weight.shape), fixed((8, width)), fixed((8, cols))],
        out_shape=[
            jax.ShapeDtypeStruct((rows, width), bf16),
            jax.ShapeDtypeStruct(weight.shape, bf16),
            jax.ShapeDtypeStruct((8, width), f32),
            jax.ShapeDtypeStruct((8, cols), f32),
        ],
        scratch_shapes=[
            pltpu.VMEM(weight.shape, f32),
            pltpu.VMEM((8, width), f32),
            pltpu.VMEM((8, cols), f32),
        ],
        compiler_params=pltpu.CompilerParams(vmem_limit_bytes=VMEM),
        cost_estimate=cost(12 * rows * width * cols, 2 * rows * (2 * width + 3 * cols)),
        name="project_back",
    )(tokens, gain, shift, weight, dq, dk, dv)


def input_kernel(x_ref, gain_ref, mine_ref, other_ref, dh_ref, out_ref):
    unit, inverse = unit_rows(x_ref[...].astype(f32))
    da = mine_ref[...].astype(f32) + other_ref[...].astype(f32)
    gain = gain_ref[...].astype(f32)
    out_ref[...] = (dh_ref[...] + norm_back(da, gain, unit, inverse)).astype(bf16)


def input_back(x, gain, mine, other, dh):
    rows, width = x.shape
    block = rows // 4
    by_rows = pl.BlockSpec((block, width), lambda i: (i, 0))
    return pl.pallas_call(
        input_kernel,
        grid=(rows // block,),
        in_specs=[by_rows, pl.BlockSpec((1, width), lambda i: (0, 0)), by_rows, by_rows, by_rows],
        out_specs=by_rows,
        out_shape=jax.ShapeDtypeStruct((rows, width), bf16),
        compiler_params=pltpu.CompilerParams(vmem_limit_bytes=VMEM),
        cost_estimate=cost(20 * rows * width, 12 * rows * width),
        name="input_back",
    )(x, gain, mine, other, dh)


def on_device(
    dp_size, tokens, buckets, norm1_gain, norm1_bias, qkv_weight, qkv_bias, out_weight, out_bias,
    norm2_gain, norm2_bias, up_weight, up_bias, down_weight, down_bias, cotangent,
):
    parts = 4
    dp_bits = dp_size.bit_length() - 1
    me = lax.axis_index("tensor")
    group = lax.axis_index("dp")
    token_rows, width = tokens.shape
    share = token_rows // parts

    def over_tensor(values, mask):
        return lax.ppermute(values, "tensor", [(i, i ^ mask) for i in range(parts)])

    def over_dp(values, mask):
        return lax.ppermute(values, "dp", [(i, i ^ mask) for i in range(dp_size)])

    def block_of(values, index):
        return lax.dynamic_slice_in_dim(values, index * share, share, 0)

    def add(left, right):
        return (left.astype(f32) + right.astype(f32)).astype(bf16)

    def gather(shard):
        half = shard.shape[0] // 2
        bit = group & 1
        near = over_tensor(lax.dynamic_slice_in_dim(shard, bit * half, half, 0), 2)
        far = over_dp(near, 1)
        first = jnp.where(bit == 0, near, far)
        second = jnp.where(bit == 0, far, near)
        whole = jnp.concatenate([first, second], axis=0)
        return [shard, over_tensor(shard, 1), whole, over_tensor(whole, 1)]

    row = lambda v: v.reshape(1, -1)
    wo_parts = gather(out_weight)
    up_parts = gather(up_weight)
    down_parts = gather(down_weight)
    bias_parts = [up_bias] + [over_tensor(up_bias, r) for r in range(1, parts)]

    q, k, v = project(tokens, row(norm1_gain), row(norm1_bias), qkv_weight, qkv_bias)
    o, qx = attend(buckets, q, k, v)
    o_parts = [block_of(o, me)] + [over_tensor(block_of(o, me ^ r), r) for r in range(1, parts)]

    x_own = block_of(tokens, me)
    g_own = block_of(cotangent, me)
    layer_out, dh, grads, wo_grads, small, up_small, *do_parts = own_rows(
        x_own, g_own, row(out_bias), row(norm2_gain), row(norm2_bias), row(down_bias),
        jnp.stack(bias_parts)[:, None, :], o_parts, wo_parts, up_parts, down_parts,
    )

    got = jnp.stack([do_parts[0]] + [over_tensor(do_parts[r], r) for r in range(1, parts)])
    grad_o = jnp.concatenate(
        [lax.dynamic_index_in_dim(got, me ^ j, 0, keepdims=False) for j in range(parts)], axis=0
    )
    dq, dk, dv = attend_back(buckets, qx, k, v, o, grad_o)
    da, grad_qkv, small_one, bias_sums = project_back(
        tokens, row(norm1_gain), row(norm1_bias), qkv_weight, dq, dk, dv, buckets.shape[0]
    )

    def scatter_dp(values, mid=None):
        blocks = values.reshape(dp_size, width // dp_size, -1)
        for bit in range(dp_bits):
            blocks = blocks.reshape(-1, 2, *blocks.shape[-2:])
            mine = (group >> bit) & 1
            keep = lax.dynamic_index_in_dim(blocks, mine, 1, keepdims=False)
            send = lax.dynamic_index_in_dim(blocks, 1 - mine, 1, keepdims=False)
            blocks = add(keep, over_dp(send, 1 << bit))
            if bit == 0 and mid is not None:
                blocks = mid(blocks)
        return blocks.reshape(width // dp_size, -1)

    own_pack = []
    for r in range(parts):
        own_pack.append(jnp.concatenate([grads[r], wo_grads[r]], axis=1))
    mine = add(own_pack[0], over_tensor(own_pack[1], 1))
    theirs = add(own_pack[2], over_tensor(own_pack[3], 1))
    span = mine.shape[1]
    both = jnp.concatenate([mine, theirs], axis=1)

    def cross(blocks):
        return add(blocks[..., :span], over_tensor(blocks[..., span:], 2))

    packed = scatter_dp(both, cross).astype(f32)
    hid = up_weight.shape[1]
    grad_down = packed[:, :hid].T
    grad_up = packed[:, hid : 2 * hid]
    grad_out = packed[:, 2 * hid :].T
    qkv_cols = qkv_weight.shape[2]
    flat = jnp.concatenate([grad_qkv[j] for j in range(3)], axis=1)
    flat = scatter_dp(flat).astype(f32)
    grad_qkv_weight = jnp.stack([flat[:, j * qkv_cols : (j + 1) * qkv_cols] for j in range(3)])

    ours = add(block_of(da, me), over_tensor(block_of(da, me ^ 1), 1))
    cross_rows = add(block_of(da, me ^ 2), over_tensor(block_of(da, me ^ 3), 1))
    input_grad = input_back(x_own, row(norm1_gain), ours, over_tensor(cross_rows, 2), dh)

    up_all = jnp.concatenate(
        [lax.dynamic_index_in_dim(up_small, me ^ j, 0, keepdims=False) for j in range(parts)], axis=1
    )

    def total_all(values, also=None):
        for mask in (1, 2):
            values = values + over_tensor(values, mask)
        if also is not None:
            values = jnp.concatenate([values, also], axis=1)
        for bit in range(dp_bits):
            values = values + over_dp(values, 1 << bit)
        return values

    early = total_all(jnp.concatenate([small[j : j + 1] for j in range(4)] + [up_all], axis=1))[0]
    late = total_all(
        jnp.concatenate([small_one[0:1], small_one[1:2]], axis=1),
        jnp.concatenate([bias_sums[0:1], bias_sums[1:2]], axis=1),
    )[0]
    piece = lambda v, i: v[i * width : (i + 1) * width]
    grad_up_bias = lax.dynamic_slice_in_dim(early, 4 * width + me * hid, hid, 0)
    grad_qkv_bias = late[2 * width :].reshape(2, qkv_cols)
    return (
        layer_out,
        input_grad,
        piece(late, 0),
        piece(late, 1),
        grad_qkv_weight,
        grad_qkv_bias,
        grad_out,
        piece(early, 2),
        piece(early, 0),
        piece(early, 1),
        grad_up,
        grad_up_bias,
        grad_down,
        piece(early, 3),
    )


def solution(mesh):
    return jax.shard_map(
        functools.partial(on_device, mesh.shape["dp"]),
        mesh=mesh,
        in_specs=(
            P("dp", None),
            P("dp"),
            P(),
            P(),
            P(None, None, "tensor"),
            P(None, "tensor"),
            P("tensor", None),
            P(),
            P(),
            P(),
            P(None, "tensor"),
            P("tensor"),
            P("tensor", None),
            P(),
            P("dp", None),
        ),
        out_specs=(
            P(("dp", "tensor"), None),
            P(("dp", "tensor"), None),
            P(),
            P(),
            P(None, "dp", "tensor"),
            P(None, "tensor"),
            P("tensor", "dp"),
            P(),
            P(),
            P(),
            P("dp", "tensor"),
            P("tensor"),
            P("tensor", "dp"),
            P(),
        ),
        check_vma=False,
    )
```

```python
import functools

import jax
import jax.numpy as jnp
from jax import lax
from jax.experimental import pallas as pl
from jax.experimental.pallas import tpu as pltpu
from jax.sharding import PartitionSpec as P

DH = 64
NORM_EPSILON = 1e-06
GRID_SIXTEENTHS = (16, 15, 15, 12, 12, 8, 8, 6, 6)
GELU_SCALE = 0.7978845608028654
GELU_CUBE = 0.044715
VMEM = 60 << 20
NN = (((1,), (0,)), ((), ()))
NT = (((1,), (1,)), ((), ()))
TN = (((0,), (0,)), ((), ()))
bf16 = jnp.bfloat16
f32 = jnp.float32
ANY = pl.BlockSpec(memory_space=pl.ANY)


def dot(left, right, dims=NN):
    return lax.dot_general(left, right, dims, preferred_element_type=f32)


def lanes(rows, width):
    return lax.broadcasted_iota(jnp.int32, (rows, width), 1)


def live_lengths(image_len):
    return sorted({image_len * s // 16 for s in GRID_SIXTEENTHS})


def live_length(bucket, image_len):
    length = jnp.int32(0)
    for index, sixteenths in enumerate(GRID_SIXTEENTHS):
        length = jnp.where(bucket == index, image_len * sixteenths // 16, length)
    return length


def cost(flops, nbytes, transcendentals=0):
    return pl.CostEstimate(flops=flops, bytes_accessed=nbytes, transcendentals=transcendentals)


def split3(values):
    high = values.astype(bf16).astype(f32)
    middle = (values - high).astype(bf16).astype(f32)
    return high, middle, values - high - middle


def unit_rows(values):
    centred = values - jnp.mean(values, axis=-1, keepdims=True)
    spread = jnp.mean(centred * centred, axis=-1, keepdims=True)
    inverse = lax.rsqrt(spread + NORM_EPSILON)
    return centred * inverse, inverse


def norm_back(grad, gain, unit, inverse):
    scaled = grad * gain
    mean_one = jnp.mean(scaled, axis=-1, keepdims=True)
    mean_two = jnp.mean(scaled * unit, axis=-1, keepdims=True)
    return inverse * (scaled - mean_one - unit * mean_two)


def project_kernel(x_ref, vec_ref, w_ref, bias_ref, out_ref, bound_ref, w_all):
    cols = w_ref.shape[2]

    @pl.when(pl.program_id(0) == 0)
    def _():
        w_all[...] = jnp.concatenate([w_ref[1], w_ref[2], w_ref[0]], axis=1)

    gain, shift = vec_ref[0:1, :].astype(f32), vec_ref[1:2, :].astype(f32)
    bias = bias_ref[...].astype(f32)
    bias = jnp.concatenate([jnp.zeros((1, cols), f32), bias[1:2], bias[0:1]], axis=1)
    rows, step = x_ref.shape[0], 128
    row = lax.broadcasted_iota(jnp.int32, (3 * cols, 128), 0)
    pick = jnp.where(row // DH == lanes(3 * cols, 128), 1.0, 0.0).astype(bf16)

    def normed(start):
        unit, _ = unit_rows(x_ref[start : start + step, :].astype(f32))
        return (unit * gain + shift).astype(bf16)

    largest = None
    ready = normed(0)
    for start in range(0, rows, step):
        following = normed(start + step) if start + step < rows else None
        values = (dot(ready, w_all[...]) + bias).astype(bf16)
        out_ref[start : start + step, :] = values
        squares = jnp.max(dot(values * values, pick), axis=0, keepdims=True)
        largest = squares if largest is None else jnp.maximum(largest, squares)
        ready = following
    bound_ref[0] = jnp.broadcast_to(largest, (8, 128))


def project(tokens, vectors, weight, bias):
    rows, width = tokens.shape
    cols = weight.shape[2]
    block = 512
    fixed = lambda shape: pl.BlockSpec(shape, lambda i: (0,) * len(shape))
    return pl.pallas_call(
        project_kernel,
        grid=(rows // block,),
        in_specs=[
            pl.BlockSpec((block, width), lambda i: (i, 0)),
            fixed(vectors.shape),
            fixed(weight.shape),
            fixed(bias.shape),
        ],
        out_specs=[
            pl.BlockSpec((block, 3 * cols), lambda i: (i, 0)),
            pl.BlockSpec((1, 8, 128), lambda i: (i, 0, 0)),
        ],
        out_shape=[
            jax.ShapeDtypeStruct((rows, 3 * cols), bf16),
            jax.ShapeDtypeStruct((rows // block, 8, 128), f32),
        ],
        scratch_shapes=[pltpu.VMEM((width, 3 * cols), bf16)],
        compiler_params=pltpu.CompilerParams(vmem_limit_bytes=VMEM),
        cost_estimate=cost(6 * rows * width * cols, 2 * rows * (width + 3 * cols)),
        name="project",
    )(tokens, vectors, weight, bias)


def attend_kernel(bucket_ref, kvq_ref, bound_ref, o_ref, qx_ref, kx, vt, *, block):
    image_len, cols = o_ref.shape
    heads = cols // DH
    at_q = 2 * cols
    length = live_length(bucket_ref[pl.program_id(0)], image_len)
    squares = jnp.max(bound_ref[...], axis=0)
    lane = lanes(8, 128)
    largest_key = jnp.max(jnp.where(lane < heads, squares, 0.0))
    of_query = (lane >= 2 * heads) & (lane < 3 * heads)
    largest_query = jnp.max(jnp.where(of_query, squares, 0.0))
    small = largest_key * largest_query <= (8.0 * 60.0) ** 2

    def run(live, subtract):
        scaled = kvq_ref[0:live, 0:192] * jnp.asarray(0.125, bf16)
        flipped = jnp.transpose(kvq_ref[0:live, 128:384])
        lane = lanes(live, 128)
        for h in range(heads):
            if h < 2:
                keep = (lane < DH) if h == 0 else (lane >= DH)
                kx[h, 0:live, :] = jnp.where(keep, scaled[:, 0:128], jnp.zeros((), bf16))
            else:
                kx[h, 0:live, 0:DH] = scaled[:, 128:192]
            vt[h, 0:DH, 0:live] = flipped[DH * (h + 1) : DH * (h + 2)]
            vt[h, DH:128, 0:live] = jnp.ones((DH, live), bf16)

        def scores(h, start):
            here = slice(start, start + block)
            if h < 2:
                return dot(kx[h, 0:live, :], kvq_ref[here, at_q : at_q + 128], NT)
            return dot(kx[h, 0:live, 0:DH], kvq_ref[here, at_q + 128 : at_q + 192], NT)

        parts = {}

        def finish(h, start, score):
            offset = 0.0
            if subtract:
                key = lax.broadcasted_iota(jnp.int32, score.shape, 0)
                score = jnp.where(key < length, score, -1e30)
                offset = jnp.max(score, axis=0, keepdims=True)
                score = score - offset
            mixed = dot(vt[h, :, 0:live], jnp.exp(score).astype(bf16))
            total = mixed[DH : DH + 1]
            parts[h] = (mixed[:DH] * (1.0 / total), split3(-(offset + jnp.log(total))))
            if h == heads - 1:
                stack = [parts[i][0] for i in range(heads)]
                stack += [parts[i][1][j] for i in range(heads) for j in range(3)]
                stack += [jnp.zeros((DH - 3 * heads, block), f32)]
                turned = jnp.transpose(jnp.concatenate(stack, axis=0).astype(bf16))
                here = slice(start, start + block)
                o_ref[here, :] = turned[:, 0:cols]
                qx_ref[here, :] = jnp.concatenate(
                    [kvq_ref[here, at_q : at_q + cols], turned[:, cols:]], axis=1
                )

        items = [(h, s) for s in range(0, image_len, block) for h in range(heads)]
        score = scores(*items[0])
        for index, item in enumerate(items):
            following = scores(*items[index + 1]) if index + 1 < len(items) else None
            finish(*item, score)
            score = following

    for live in live_lengths(image_len):
        pl.when(small & (length == live))(functools.partial(run, live, False))
    pl.when(jnp.logical_not(small))(functools.partial(run, image_len, True))


def attend(buckets, kvq, bound):
    rows = kvq.shape[0]
    cols = kvq.shape[1] // 3
    images = buckets.shape[0]
    image_len = rows // images
    heads = cols // DH
    by_rows = lambda w: pl.BlockSpec((image_len, w), lambda i, b: (i, 0))
    return pl.pallas_call(
        functools.partial(attend_kernel, block=512),
        grid_spec=pltpu.PrefetchScalarGridSpec(
            num_scalar_prefetch=1,
            grid=(images,),
            in_specs=[by_rows(3 * cols), pl.BlockSpec(bound.shape, lambda i, b: (0, 0, 0))],
            out_specs=[by_rows(cols), by_rows(256)],
            scratch_shapes=[
                pltpu.VMEM((heads, image_len, 128), bf16),
                pltpu.VMEM((heads, 128, image_len), bf16),
            ],
        ),
        out_shape=[
            jax.ShapeDtypeStruct((rows, cols), bf16),
            jax.ShapeDtypeStruct((rows, 256), bf16),
        ],
        compiler_params=pltpu.CompilerParams(vmem_limit_bytes=VMEM),
        cost_estimate=cost(16 * rows * image_len * cols, 12 * rows * cols, rows * image_len * heads),
        name="attend",
    )(buckets, kvq, bound)


def image_back_kernel(bucket_ref, which_ref, kvq_ref, qx_ref, o_ref, do_ref, vec_ref, *refs, block, stage):
    refs = list(refs)
    take = lambda count: [refs.pop(0) for _ in range(count)]
    x_any, w_any, perm_any = take(3)
    old = take(3) if stage else None
    outs = take((2, 3, 1)[stage])
    dw_out, small_out, bias_out = take(3)
    dox, dot_t, q_t, kx, vx, k_t, grads, x, w, w_all, perm, da_s, dw, sems = take(14)
    image_len, cols = o_ref.shape
    heads = cols // DH
    image = which_ref[0]
    loads = [
        pltpu.make_async_copy(x_any.at[pl.ds(image * image_len, image_len)], x, sems.at[0]),
        pltpu.make_async_copy(w_any, w, sems.at[1]),
        pltpu.make_async_copy(perm_any, perm, sems.at[2]),
    ]
    if stage:
        loads.append(pltpu.make_async_copy(old[0], dw, sems.at[3]))
    for load in loads:
        load.start()
    length = live_length(bucket_ref[image], image_len)
    product = do_ref[...].astype(f32) * o_ref[...].astype(f32)
    high = product.astype(bf16)
    low = (product - high.astype(f32)).astype(bf16)
    row = lax.broadcasted_iota(jnp.int32, (cols, DH), 0)
    lane = lanes(cols, DH)
    pick = jnp.where(row // DH == lane // 3, 1.0, 0.0).astype(bf16)
    inner = split3(-(dot(high, pick) + dot(low, pick)))
    lane = lanes(image_len, DH)
    which = lane % 3
    inner = jnp.where(which == 0, inner[0], jnp.where(which == 1, inner[1], inner[2]))
    inner = jnp.where(lane < 3 * heads, inner, 0.0).astype(bf16)
    extended = jnp.concatenate([do_ref[...], inner], axis=1)
    dox[...] = extended
    dot_t[...] = jnp.transpose(extended)
    q_t[...] = jnp.transpose(qx_ref[...])
    for live in live_lengths(image_len):

        @pl.when(length == live)
        def _():
            if live < image_len:
                grads[live:image_len, 0 : 2 * cols] = jnp.zeros((image_len - live, 2 * cols), bf16)
            lane = lanes(live, cols)
            side = lanes(live, DH)
            scaled = kvq_ref[0:live, 0:cols] * jnp.asarray(0.125, bf16)
            values = kvq_ref[0:live, cols : 2 * cols]
            k_t[0:cols, 0:live] = jnp.transpose(scaled)
            zero = jnp.zeros((), bf16)
            for h in range(heads):
                keep = (lane >= DH * h) & (lane < DH * (h + 1))
                ones = jnp.where((side >= 3 * h) & (side < 3 * h + 3), 1.0, 0.0).astype(bf16)
                kx[h, 0:live, :] = jnp.concatenate([jnp.where(keep, scaled, zero), ones], axis=1)
                vx[h, 0:live, :] = jnp.concatenate([jnp.where(keep, values, zero), ones], axis=1)
            parts, grad_q = {}, {}
            for start in range(0, live, block):
                end = min(live, start + block)
                for h in range(heads):
                    probs = jnp.exp(dot(kx[h, start:end, :], qx_ref[...], NT))
                    grad_probs = dot(vx[h, start:end, :], dox[...], NT)
                    grad_scores = (probs * grad_probs).astype(bf16)
                    pair = slice(0, 128) if h < 2 else slice(128, 256)
                    own = slice(DH * (h % 2), DH * (h % 2) + DH)
                    grad_v = dot(dot_t[pair, :], probs.astype(bf16), NT)[own]
                    grad_k = dot(q_t[pair, :], grad_scores, NT)[own]
                    parts[h] = (grad_k * 0.125, grad_v)
                    step = dot(k_t[pair, start:end], grad_scores)[own]
                    grad_q[h] = step if start == 0 else grad_q[h] + step
                stack = [parts[h][j] for j in range(2) for h in range(heads)]
                turned = jnp.concatenate(stack, axis=0).astype(bf16)
                grads[start:end, 0 : 2 * cols] = jnp.transpose(turned)
            whole = jnp.concatenate([grad_q[h] for h in range(heads)], axis=0)
            grads[:, 2 * cols : 3 * cols] = jnp.transpose(whole.astype(bf16))

    for load in loads:
        load.wait()
    gain, shift = vec_ref[0:1, :].astype(f32), vec_ref[1:2, :].astype(f32)
    w_all[...] = jnp.concatenate([w[1], w[2], w[0]], axis=1)
    step = 256
    sum_one = sum_two = sum_three = jnp.zeros((1, 1), f32)
    normed = []
    for start in range(0, image_len, step):
        here = slice(start, start + step)
        unit, _ = unit_rows(x[here, :].astype(f32))
        normed.append((unit * gain + shift).astype(bf16))
        part = grads[here, :]
        da = dot(part, w_all[...], NT)
        da_s[here, :] = da.astype(bf16)
        sum_one = sum_one + jnp.sum(da * unit, axis=0, keepdims=True)
        sum_two = sum_two + jnp.sum(da, axis=0, keepdims=True)
        sum_three = sum_three + jnp.sum(part.astype(f32), axis=0, keepdims=True)
    me = lax.axis_index("tensor")
    core, side = me % 2, me // 2
    if stage == 0:
        half = image_len // 2
        spans = [(core * half, half), ((1 - core) * half, half)]
    elif stage == 1:
        half = image_len // 4
        far = (1 - side) * 2 * half
        spans = [(far + core * half, half), (far + (1 - core) * half, half), (side * 2 * half, 2 * half)]
    else:
        spans = [(0, image_len)]
    stores = []
    for index, (start, size) in enumerate(spans):
        source = da_s.at[pl.ds(pl.multiple_of(start, 256), size)] if size < image_len else da_s
        stores.append(pltpu.make_async_copy(source, outs[index], sems.at[4 + index]))
        stores[-1].start()
    flipped = dot(perm[...], jnp.concatenate(normed, axis=0), NT).astype(bf16)
    fresh = dot(flipped, grads[...])
    if stage:
        fresh = fresh + dw[...]
        sum_one = sum_one + old[1][0:1, :]
        sum_two = sum_two + old[1][1:2, :]
        sum_three = sum_three + old[2][0:1, :]
    dw_out[...] = fresh.astype(dw_out.dtype)
    small_out[...] = jnp.concatenate([sum_one, sum_two, jnp.zeros((6, sum_one.shape[1]), f32)], axis=0)
    bias_out[...] = jnp.broadcast_to(sum_three, bias_out.shape)
    for store in stores:
        store.wait()


def image_back(stage, buckets, which, kvq, qx, o, grad_o, vectors, tokens, weight, perm, old):
    rows, width = tokens.shape
    cols = o.shape[1]
    images = buckets.shape[0]
    image_len = rows // images
    heads = cols // DH
    half = image_len // 2
    da_rows = [[half, half], [half // 2, half // 2, half], [image_len]][stage]
    picked = lambda w: pl.BlockSpec((image_len, w), lambda i, b, s: (s[0], 0))
    fixed = lambda shape: pl.BlockSpec(shape, lambda i, b, s: (0,) * len(shape))
    dw_type = bf16 if stage == 2 else f32
    return pl.pallas_call(
        functools.partial(image_back_kernel, block=256, stage=stage),
        grid_spec=pltpu.PrefetchScalarGridSpec(
            num_scalar_prefetch=2,
            grid=(1,),
            in_specs=[picked(3 * cols), picked(256), picked(cols), picked(cols), fixed(vectors.shape)]
            + [ANY] * 3
            + ([ANY, fixed((8, width)), fixed((8, 3 * cols))] if stage else []),
            out_specs=[ANY] * len(da_rows)
            + [fixed((width, 3 * cols)), fixed((8, width)), fixed((8, 3 * cols))],
            scratch_shapes=[
                pltpu.VMEM((image_len, 256), bf16),
                pltpu.VMEM((256, image_len), bf16),
                pltpu.VMEM((256, image_len), bf16),
                pltpu.VMEM((heads, image_len, 256), bf16),
                pltpu.VMEM((heads, image_len, 256), bf16),
                pltpu.VMEM((256, image_len), bf16),
                pltpu.VMEM((image_len, 3 * cols), bf16),
                pltpu.VMEM((image_len, width), bf16),
                pltpu.VMEM(weight.shape, bf16),
                pltpu.VMEM((width, 3 * cols), bf16),
                pltpu.VMEM((width, width), bf16),
                pltpu.VMEM((image_len, width), bf16),
                pltpu.VMEM((width, 3 * cols), f32),
                pltpu.SemaphoreType.DMA((8,)),
            ],
        ),
        out_shape=[jax.ShapeDtypeStruct((n, width), bf16) for n in da_rows]
        + [
            jax.ShapeDtypeStruct((width, 3 * cols), dw_type),
            jax.ShapeDtypeStruct((8, width), f32),
            jax.ShapeDtypeStruct((8, 3 * cols), f32),
        ],
        compiler_params=pltpu.CompilerParams(vmem_limit_bytes=VMEM),
        cost_estimate=cost(
            40 * image_len * image_len * cols + 12 * image_len * width * cols,
            16 * image_len * width,
            image_len * image_len * heads,
        ),
        name=f"image_back_{stage}",
    )(buckets, which, kvq, qx, o, grad_o, vectors, tokens, weight, perm, *old)


def rows_kernel(*refs, parts):
    refs = list(refs)
    take = lambda count: [refs.pop(0) for _ in range(count)]
    x_ref, g_ref, vec_ref, bias_ref, o_in, perm_ref = take(6)
    wo_in, up_in, down_in = take(parts + 2), take(parts + 2), take(parts + 2)
    y_ref, dh_ref, keep_ref, send_ref, small_ref, do_ref = take(6)
    wo_w, up_w, down_w, hidden, normed, mixed, back, g_t, c_t, z_s, du_s, grads, wo_grads, sems = take(14)
    rows, width = x_ref.shape
    hid = up_w.shape[2]
    part = pl.program_id(0)
    bit = lax.axis_index("dp") % 2

    def loads(source, target, row):
        size = target.shape[1]
        half = size // 2
        near = pl.ds(pl.multiple_of(bit * half, 16), half)
        far = pl.ds(pl.multiple_of((1 - bit) * half, 16), half)
        places = [target.at[0], target.at[1]]
        for r in (2, 3):
            places += [target.at[r, near], target.at[r, far]]
        return [
            pltpu.make_async_copy(source[i], places[i], sems.at[row, i]) for i in range(parts + 2)
        ]

    wo_loads, up_loads, down_loads = loads(wo_in, wo_w, 0), loads(up_in, up_w, 1), loads(down_in, down_w, 2)
    gain, shift = vec_ref[2:3, :].astype(f32), vec_ref[3:4, :].astype(f32)

    def store(r):
        target = (send_ref if r % 2 else keep_ref).at[r // 2, :, pl.ds(0, 2 * hid)]
        return pltpu.make_async_copy(grads.at[r], target, sems.at[3, r])

    def store_out(r):
        target = (send_ref if r % 2 else keep_ref).at[r // 2, :, pl.ds(2 * hid, 256)]
        return pltpu.make_async_copy(wo_grads.at[r], target, sems.at[4, r])

    @pl.when(part == 0)
    def _():
        for load in wo_loads + up_loads + down_loads:
            load.start()
        for load in wo_loads:
            load.wait()
        g_t[...] = dot(perm_ref[...], g_ref[...], NT).astype(bf16)
        attended = dot(o_in[0], wo_w[0])
        for r in range(1, parts):
            attended += dot(o_in[r], wo_w[r])
        h1 = x_ref[...].astype(f32) + attended + vec_ref[4:5, :].astype(f32)
        hidden[...] = h1
        unit, _ = unit_rows(h1)
        normed[...] = (unit * gain + shift).astype(bf16)
        c_t[...] = dot(perm_ref[...], normed[...], NT).astype(bf16)
        mixed[...] = jnp.zeros_like(mixed)
        back[...] = jnp.zeros_like(back)
        small_ref[...] = jnp.zeros_like(small_ref)

    for r in range(parts):

        @pl.when(part == r)
        def _():
            for load in (up_loads[r : r + 1] + down_loads[r : r + 1]) if r < 2 else (
                up_loads[2 * r - 2 : 2 * r] + down_loads[2 * r - 2 : 2 * r]
            ):
                load.wait()

    step = 256
    chunks = [slice(s, s + step) for s in range(0, hid, step)]

    def first(cols):
        u = dot(normed[...], up_w[part, :, cols]) + bias_ref[part, 0:1, cols]
        return u, dot(g_ref[...], down_w[part, cols, :], NT)

    def bend(cols, u, dz):
        square = u * u
        scaled = u * GELU_SCALE
        gate = 0.5 + 0.5 * jnp.tanh(scaled * (1.0 + GELU_CUBE * square))
        z_s[:, cols] = (u * gate).astype(bf16)
        slope = gate + (2.0 * gate) * (1.0 - gate) * scaled * (1.0 + (3.0 * GELU_CUBE) * square)
        du = (dz * slope).astype(bf16)
        du_s[:, cols] = du
        small_ref[pl.ds(8 + part, 1), cols] = jnp.sum(du.astype(f32), axis=0, keepdims=True)

    def weigh(cols):
        grads[part, :, cols] = dot(g_t[...], z_s[:, cols]).astype(bf16)
        later = slice(hid + cols.start, hid + cols.stop)
        grads[part, :, later] = dot(c_t[...], du_s[:, cols]).astype(bf16)

    ready = first(chunks[0])
    for index, cols in enumerate(chunks):
        following = first(chunks[index + 1]) if index + 1 < len(chunks) else None
        bend(cols, *ready)
        if index:
            weigh(chunks[index - 1])
        ready = following
    mixed[...] += dot(z_s[...], down_w[part])
    weigh(chunks[-1])
    back[...] += dot(du_s[...], up_w[part], NT)
    for r in range(parts):

        @pl.when(part == r)
        def _():
            store(r).start()

    @pl.when(part == parts - 1)
    def _():
        h1 = hidden[...]
        y_ref[...] = (h1 + mixed[...] + vec_ref[5:6, :].astype(f32)).astype(bf16)
        unit, inverse = unit_rows(h1)
        dc = back[...]
        wide_g = g_ref[...].astype(f32)
        dh = wide_g + norm_back(dc, gain, unit, inverse)
        dh_ref[...] = dh
        e = dh.astype(bf16)
        for index, values in enumerate([dc * unit, dc, dh, wide_g]):
            small_ref[2 + index : 3 + index, :] = jnp.sum(values, axis=0, keepdims=True)
        for r in range(parts):
            do_ref[r] = dot(e, wo_w[r], NT).astype(bf16)
        e_t = dot(perm_ref[...], e, NT).astype(bf16)
        blank = jnp.zeros((width, 256 - o_in.shape[2]), bf16)
        for r in range(parts):
            wo_grads[r] = jnp.concatenate([dot(e_t, o_in[r]).astype(bf16), blank], axis=1)
            store_out(r).start()
        for r in range(parts):
            store(r).wait()
            store_out(r).wait()


def own_rows(x, g, vectors, up_bias, o_parts, perm, wo, up, down):
    parts, rows, cols = o_parts.shape
    width = x.shape[1]
    hid = up[0].shape[1]
    fixed = lambda shape: pl.BlockSpec(shape, lambda r: (0,) * len(shape))
    packed = jax.ShapeDtypeStruct((parts // 2, width, 2 * hid + 256), bf16)
    return pl.pallas_call(
        functools.partial(rows_kernel, parts=parts),
        grid=(parts,),
        in_specs=[
            fixed((rows, width)),
            fixed((rows, width)),
            fixed(vectors.shape),
            fixed(up_bias.shape),
            fixed(o_parts.shape),
            fixed(perm.shape),
        ]
        + [ANY] * (3 * (parts + 2)),
        out_specs=[
            fixed((rows, width)),
            fixed((rows, width)),
            ANY,
            ANY,
            fixed((16, width)),
            fixed((parts, rows, cols)),
        ],
        out_shape=[
            jax.ShapeDtypeStruct((rows, width), bf16),
            jax.ShapeDtypeStruct((rows, width), f32),
            packed,
            packed,
            jax.ShapeDtypeStruct((16, width), f32),
            jax.ShapeDtypeStruct((parts, rows, cols), bf16),
        ],
        scratch_shapes=[
            pltpu.VMEM((parts, cols, width), bf16),
            pltpu.VMEM((parts, width, hid), bf16),
            pltpu.VMEM((parts, hid, width), bf16),
            pltpu.VMEM((rows, width), f32),
            pltpu.VMEM((rows, width), bf16),
            pltpu.VMEM((rows, width), f32),
            pltpu.VMEM((rows, width), f32),
            pltpu.VMEM((width, rows), bf16),
            pltpu.VMEM((width, rows), bf16),
            pltpu.VMEM((rows, hid), bf16),
            pltpu.VMEM((rows, hid), bf16),
            pltpu.VMEM((parts, width, 2 * hid), bf16),
            pltpu.VMEM((parts, width, 256), bf16),
            pltpu.SemaphoreType.DMA((5, parts + 2)),
        ],
        compiler_params=pltpu.CompilerParams(vmem_limit_bytes=VMEM),
        cost_estimate=cost(12 * rows * width * hid * parts, 8 * parts * width * hid, rows * hid * parts),
        name="own_rows",
    )(x, g, vectors, up_bias, o_parts, perm, *wo, *up, *down)


def greet(partners):
    barrier = pltpu.get_barrier_semaphore()
    for partner in partners:
        pl.semaphore_signal(barrier, inc=1, device_id=partner, device_id_type=pl.DeviceIdType.MESH)
    pl.semaphore_wait(barrier, len(partners))


def send(source, target, sems, index, partner):
    return pltpu.make_async_remote_copy(
        src_ref=source,
        dst_ref=target,
        send_sem=sems.at[0, index],
        recv_sem=sems.at[1, index],
        device_id=partner,
        device_id_type=pl.DeviceIdType.MESH,
    )


def out_kernel(o_ref, bias_ref, o_all, bias_all, sems, local, *, parts):
    dp, me = lax.axis_index("dp"), lax.axis_index("tensor")
    rows = o_all.shape[1]
    partners = [(dp, me ^ r) for r in range(parts)]
    greet(partners[1:])
    copies = []
    for r in range(parts - 1, 0, -1):
        source = o_ref.at[pl.ds(pl.multiple_of((me ^ r) * rows, rows), rows)]
        copies.append(send(source, o_all.at[r], sems, r, partners[r]))
        copies.append(send(bias_ref, bias_all.at[r], sems, parts + r, partners[r]))
    source = o_ref.at[pl.ds(pl.multiple_of(me * rows, rows), rows)]
    copies.append(pltpu.make_async_copy(source, o_all.at[0], local.at[0]))
    copies.append(pltpu.make_async_copy(bias_ref, bias_all.at[0], local.at[1]))
    for copy in copies:
        copy.start()
    for copy in copies:
        copy.wait()


def back_kernel(do_all, do_ref, sems, local, *, parts):
    dp, me = lax.axis_index("dp"), lax.axis_index("tensor")
    rows = do_all.shape[1]
    partners = [(dp, me ^ r) for r in range(parts)]
    greet(partners[1:])
    mine = do_ref.at[pl.ds(pl.multiple_of(me * rows, rows), rows)]
    copies = [send(do_all.at[r], mine, sems, r, partners[r]) for r in range(parts - 1, 0, -1)]
    copies.append(pltpu.make_async_copy(do_all.at[0], mine, local.at[0]))
    for copy in copies:
        copy.start()
    for copy in copies:
        copy.wait()


def exchange(kernel, operands, shapes, parts, number, name):
    return pl.pallas_call(
        functools.partial(kernel, parts=parts),
        in_specs=[ANY] * len(operands),
        out_specs=[ANY] * len(shapes),
        out_shape=shapes,
        scratch_shapes=[pltpu.SemaphoreType.DMA((2, 2 * parts)), pltpu.SemaphoreType.DMA((2,))],
        compiler_params=pltpu.CompilerParams(collective_id=number, has_side_effects=True),
        name=name,
    )(*operands)


def finish_kernel(
    own_any, mid_any, far_own_any, far_mid_any, x_any, dh_any, vec_ref, dw_ref, late_ref, bias_ref, early_ref,
    out_ref, dw_out, sums_out, held, other, far_own, far_mid, x_v, dh_v, *refs, dp_size,
):
    bits = dp_size.bit_length() - 1
    refs = list(refs)
    sent_w = [refs.pop(0) for _ in range(bits)]
    got_w = [refs.pop(0) for _ in range(bits)]
    total, sums, got_s, sems, local = refs
    dp, me = lax.axis_index("dp"), lax.axis_index("tensor")
    core, side = me % 2, me // 2
    rows, width = out_ref.shape
    image_len = own_any.shape[0]
    half = image_len // 2
    at_own = side * half
    at_mid = (1 - side) * image_len
    across = [(dp, me ^ 1), (dp, me ^ 2)]
    along = [(dp ^ (1 << bit), me) for bit in range(bits)]
    greet(across + along)

    loads = [
        pltpu.make_async_copy(own_any, held.at[pl.ds(pl.multiple_of(at_own, half), image_len)], local.at[0]),
        pltpu.make_async_copy(mid_any, held.at[pl.ds(pl.multiple_of(at_mid, half), half)], local.at[1]),
        pltpu.make_async_copy(far_own_any, far_own, local.at[2]),
        pltpu.make_async_copy(far_mid_any, far_mid, local.at[3]),
        pltpu.make_async_copy(x_any, x_v, local.at[4]),
        pltpu.make_async_copy(dh_any, dh_v, local.at[5]),
    ]
    for load in loads:
        load.start()

    span = total.shape[0] // 2
    total[...] = dw_ref[...].astype(f32)
    sent_w[0][...] = dw_ref[span:, :].astype(sent_w[0].dtype)
    w_copies = [send(sent_w[0], got_w[0], sems, 0, along[0])]
    w_copies[0].start()

    sums[...] = early_ref[...]
    sums[0:2, :] = late_ref[0:2, :]
    sums[12:13, 0 : bias_ref.shape[1]] = bias_ref[0:1, :]
    routes = across + along
    s_copies = []

    def send_sums(step):
        s_copies.append(send(sums, got_s.at[step], sems, 8 + step, routes[step]))
        s_copies[step].start()

    def add_sums(step):
        s_copies[step].wait()
        if step < 2:
            sums[0:6, :] += got_s[step, 0:6, :]
            new = [sums[8 + r : 9 + r, :] + got_s[step, 8 + (r ^ (1 << step)) : 9 + (r ^ (1 << step)), :] for r in range(4)]
            for r in range(4):
                sums[8 + r : 9 + r, :] = new[r]
        else:
            sums[...] += got_s[step]

    send_sums(0)

    for load in loads[:4]:
        load.wait()
    here = pl.ds(pl.multiple_of(at_own + core * half, half), half)
    held[here, :] = (held[here, :].astype(f32) + far_own[...].astype(f32)).astype(bf16)
    here = pl.ds(pl.multiple_of(at_mid + core * (half // 2), half // 2), half // 2)
    held[here, :] = (held[here, :].astype(f32) + far_mid[...].astype(f32)).astype(bf16)
    theirs = held.at[pl.ds(pl.multiple_of((1 - core) * rows, rows), rows)]
    da_copy = send(theirs, other, sems, 20, across[0])
    da_copy.start()

    add_sums(0)
    send_sums(1)
    add_sums(1)
    send_sums(2)
    for load in loads[4:]:
        load.wait()
    da_copy.wait()
    gain = vec_ref[0:1, :].astype(f32)
    step = 256
    for start in range(0, rows, step):
        piece = slice(start, start + step)
        unit, inverse = unit_rows(x_v[piece, :].astype(f32))
        mine = held[pl.ds(pl.multiple_of(core * rows + start, step), step), :].astype(f32)
        da = mine + other[piece, :].astype(f32)
        out_ref[piece, :] = (dh_v[piece, :] + norm_back(da, gain, unit, inverse)).astype(bf16)

    for bit in range(bits):
        w_copies[bit].wait()
        total[0:span, :] += got_w[bit][...].astype(f32)
        if bit + 1 < bits:
            span //= 2
            sent_w[bit + 1][...] = total[span : 2 * span, :].astype(sent_w[bit + 1].dtype)
            w_copies.append(send(sent_w[bit + 1], got_w[bit + 1], sems, bit + 1, along[bit + 1]))
            w_copies[bit + 1].start()
        add_sums(2 + bit)
        if bit + 1 < bits:
            send_sums(3 + bit)
    dw_out[...] = total[0:span, :]
    sums_out[...] = sums[...]


def finish(own, mid, far_own, far_mid, x, dh, vectors, dw, late, bias, early, dp_size):
    rows, width = x.shape
    cols = dw.shape[1]
    bits = dp_size.bit_length() - 1
    spans = [width >> (bit + 1) for bit in range(bits)]
    kinds = [bf16 if span % 16 == 0 else f32 for span in spans]
    return pl.pallas_call(
        functools.partial(finish_kernel, dp_size=dp_size),
        in_specs=[ANY] * 6 + [pl.BlockSpec(memory_space=pltpu.VMEM)] * 5,
        out_specs=[pl.BlockSpec(memory_space=pltpu.VMEM)] * 3,
        out_shape=[
            jax.ShapeDtypeStruct((rows, width), bf16),
            jax.ShapeDtypeStruct((width // dp_size, cols), f32),
            jax.ShapeDtypeStruct((16, width), f32),
        ],
        scratch_shapes=[
            pltpu.VMEM((2 * rows, width), bf16),
            pltpu.VMEM((rows, width), bf16),
            pltpu.VMEM(far_own.shape, bf16),
            pltpu.VMEM(far_mid.shape, bf16),
            pltpu.VMEM((rows, width), bf16),
            pltpu.VMEM((rows, width), f32),
        ]
        + [pltpu.VMEM((span, cols), kind) for span, kind in zip(spans, kinds)] * 2
        + [
            pltpu.VMEM((width, cols), f32),
            pltpu.VMEM((16, width), f32),
            pltpu.VMEM((2 + bits, 16, width), f32),
            pltpu.SemaphoreType.DMA((2, 24)),
            pltpu.SemaphoreType.DMA((6,)),
        ],
        compiler_params=pltpu.CompilerParams(
            collective_id=3, has_side_effects=True, vmem_limit_bytes=VMEM
        ),
        name="finish",
    )(own, mid, far_own, far_mid, x, dh, vectors, dw, late, bias, early)


def on_device(
    dp_size, tokens, buckets, norm1_gain, norm1_bias, qkv_weight, qkv_bias, out_weight, out_bias,
    norm2_gain, norm2_bias, up_weight, up_bias, down_weight, down_bias, cotangent,
):
    parts = 4
    dp_bits = dp_size.bit_length() - 1
    me = lax.axis_index("tensor")
    group = lax.axis_index("dp")
    token_rows, width = tokens.shape
    share = token_rows // parts
    hid = up_weight.shape[1]
    cols = qkv_weight.shape[2]

    def over_tensor(values, mask):
        return lax.ppermute(values, "tensor", [(i, i ^ mask) for i in range(parts)])

    def over_dp(values, mask):
        return lax.ppermute(values, "dp", [(i, i ^ mask) for i in range(dp_size)])

    def block_of(values):
        return lax.dynamic_slice_in_dim(values, me * share, share, 0)

    def add(*terms):
        total = terms[0].astype(f32)
        for term in terms[1:]:
            total = total + term.astype(f32)
        return total.astype(bf16)

    def gather(shard):
        half = shard.shape[0] // 2
        near = over_tensor(lax.dynamic_slice_in_dim(shard, (group & 1) * half, half, 0), 2)
        far = over_dp(near, 1)
        return [shard, over_tensor(shard, 1), near, far, over_tensor(near, 1), over_tensor(far, 1)]

    wo = gather(out_weight)
    up = gather(up_weight)
    down = gather(down_weight)
    blank = jnp.zeros_like(norm1_gain)
    vectors = jnp.stack(
        [norm1_gain, norm1_bias, norm2_gain, norm2_bias, out_bias, down_bias, blank, blank]
    )
    up_bias_rows = jnp.broadcast_to(up_bias.astype(f32)[None], (8, hid))
    block_rows = width // dp_size
    place = jnp.arange(width, dtype=jnp.int32)
    block = place // block_rows
    turned = jnp.zeros_like(block)
    for bit in range(dp_bits):
        turned = turned | (((block >> bit) & 1) << (dp_bits - 1 - bit))
    source = (turned ^ group) * block_rows + place % block_rows
    perm = (source[:, None] == place[None, :]).astype(bf16)

    kvq, bound = project(tokens, vectors, qkv_weight, qkv_bias)
    o, qx = attend(buckets, kvq, bound)
    o_parts, bias_parts = exchange(
        out_kernel,
        (o, up_bias_rows),
        [
            jax.ShapeDtypeStruct((parts, share, cols), bf16),
            jax.ShapeDtypeStruct((parts, 8, hid), f32),
        ],
        parts,
        1,
        "exchange_out",
    )
    x_own = block_of(tokens)
    layer_out, dh, keep, away, early, do_parts = own_rows(
        x_own, block_of(cotangent), vectors, bias_parts, o_parts, perm, wo, up, down
    )
    (grad_o,) = exchange(
        back_kernel,
        (do_parts,),
        [jax.ShapeDtypeStruct((token_rows, cols), bf16)],
        parts,
        2,
        "exchange_back",
    )

    other = over_tensor(away, 1)
    half = width // 2
    kept, sent = add(keep[:, :half], other[:, :half]), add(keep[:, half:], other[:, half:])
    got = over_dp(sent, 1)
    cross = over_tensor(add(kept[1], got[1]), 2)
    if dp_bits > 1:
        half //= 2
        sent = add(kept[0, half:], got[0, half:], cross[half:])
        kept = add(kept[0, :half], got[0, :half], cross[:half])
    else:
        kept = add(kept[0], got[0], cross)
    for bit in range(1, dp_bits):
        got = over_dp(sent, 1 << bit)
        if bit + 1 < dp_bits:
            half //= 2
            sent = add(kept[half:], got[half:])
            kept = add(kept[:half], got[:half])
        else:
            kept = add(kept, got)
    packed = kept.astype(f32)
    grad_down = packed[:, :hid].T
    grad_up = packed[:, hid : 2 * hid]
    grad_out = packed[:, 2 * hid : 2 * hid + cols].T

    side = me // 2
    order = [2 - 2 * side, jnp.ones_like(side), 2 * side]
    run = lambda stage, old: image_back(
        stage, buckets, order[stage].reshape(1).astype(jnp.int32), kvq, qx, o, grad_o, vectors, tokens, qkv_weight, perm, old
    )
    da_keep, da_send, *old = run(0, [])
    far_own = over_tensor(add(da_keep, over_tensor(da_send, 1)), 2)
    da_keep, da_send, mid, *old = run(1, old)
    far_mid = over_tensor(add(da_keep, over_tensor(da_send, 1)), 2)
    own, dw, late, bias_sums = run(2, old)
    input_grad, dw, sums = finish(
        own, mid, far_own, far_mid, x_own, dh, vectors, dw, late, bias_sums, early, dp_size
    )
    grad_qkv_weight = jnp.stack([dw[:, 2 * cols :], dw[:, :cols], dw[:, cols : 2 * cols]])
    grad_qkv_bias = jnp.stack([sums[12, 2 * cols : 3 * cols], sums[12, cols : 2 * cols]])
    return (
        layer_out,
        input_grad,
        sums[0],
        sums[1],
        grad_qkv_weight,
        grad_qkv_bias,
        grad_out,
        sums[4],
        sums[2],
        sums[3],
        grad_up,
        sums[8],
        grad_down,
        sums[5],
    )


def solution(mesh):
    return jax.shard_map(
        functools.partial(on_device, mesh.shape["dp"]),
        mesh=mesh,
        in_specs=(
            P("dp", None),
            P("dp"),
            P(),
            P(),
            P(None, None, "tensor"),
            P(None, "tensor"),
            P("tensor", None),
            P(),
            P(),
            P(),
            P(None, "tensor"),
            P("tensor"),
            P("tensor", None),
            P(),
            P("dp", None),
        ),
        out_specs=(
            P(("dp", "tensor"), None),
            P(("dp", "tensor"), None),
            P(),
            P(),
            P(None, "dp", "tensor"),
            P(None, "tensor"),
            P("tensor", "dp"),
            P(),
            P(),
            P(),
            P("dp", "tensor"),
            P("tensor"),
            P("tensor", "dp"),
            P(),
        ),
        check_vma=False,
    )
```

```python
import functools

import jax
import jax.numpy as jnp
from jax import lax
from jax.experimental import pallas as pl
from jax.experimental.pallas import tpu as pltpu
from jax.sharding import PartitionSpec as P

DH = 64
NORM_EPSILON = 1e-06
GRID_SIXTEENTHS = (16, 15, 15, 12, 12, 8, 8, 6, 6)
GELU_SCALE = 0.7978845608028654
GELU_CUBE = 0.044715
VMEM = 60 << 20
NN = (((1,), (0,)), ((), ()))
NT = (((1,), (1,)), ((), ()))
TN = (((0,), (0,)), ((), ()))
bf16 = jnp.bfloat16
f32 = jnp.float32
ANY = pl.BlockSpec(memory_space=pl.ANY)


def dot(left, right, dims=NN):
    return lax.dot_general(left, right, dims, preferred_element_type=f32)


def lanes(rows, width):
    return lax.broadcasted_iota(jnp.int32, (rows, width), 1)


def live_lengths(image_len):
    return sorted({image_len * s // 16 for s in GRID_SIXTEENTHS})


def live_length(bucket, image_len):
    length = jnp.int32(0)
    for index, sixteenths in enumerate(GRID_SIXTEENTHS):
        length = jnp.where(bucket == index, image_len * sixteenths // 16, length)
    return length


def cost(flops, nbytes, transcendentals=0):
    return pl.CostEstimate(flops=flops, bytes_accessed=nbytes, transcendentals=transcendentals)


def split3(values):
    high = values.astype(bf16).astype(f32)
    middle = (values - high).astype(bf16).astype(f32)
    return high, middle, values - high - middle


def halving_order(order, width, dp_size):
    bits = dp_size.bit_length() - 1
    size = width // dp_size
    place = lax.broadcasted_iota(jnp.int32, (width, 128), 0)
    block = jnp.zeros_like(place)
    for index in range(1, dp_size):
        block = block + (place >= index * size).astype(jnp.int32)
    turned = jnp.zeros_like(block)
    for step, bit in enumerate(order):
        turned = turned | (((block >> (bits - 1 - step)) & 1) << bit)
    source = (turned ^ lax.axis_index("dp")) * size + (place - block * size)
    lane = lanes(width, 128)
    return jnp.concatenate(
        [jnp.where(source == lane + start, 1.0, 0.0).astype(bf16) for start in range(0, width, 128)], axis=1
    )


def unit_rows(values):
    centred = values - jnp.mean(values, axis=-1, keepdims=True)
    spread = jnp.mean(centred * centred, axis=-1, keepdims=True)
    inverse = lax.rsqrt(spread + NORM_EPSILON)
    return centred * inverse, inverse


def norm_back(grad, gain, unit, inverse):
    scaled = grad * gain
    mean_one = jnp.mean(scaled, axis=-1, keepdims=True)
    mean_two = jnp.mean(scaled * unit, axis=-1, keepdims=True)
    return inverse * (scaled - mean_one - unit * mean_two)


def project_kernel(x_ref, vec_ref, w_ref, bias_ref, out_ref, bound_ref, w_all):
    cols = w_ref.shape[1]

    @pl.when(pl.program_id(0) == 0)
    def _():
        for index, source in enumerate((1, 2, 0)):
            w_all[index * cols : (index + 1) * cols, :] = w_ref[source]

    gain, shift = vec_ref[0:1, :].astype(f32), vec_ref[1:2, :].astype(f32)
    bias = bias_ref[...].astype(f32)
    bias = jnp.concatenate([jnp.zeros((1, cols), f32), bias[1:2], bias[0:1]], axis=1)
    rows, step = x_ref.shape[0], 128
    row = lax.broadcasted_iota(jnp.int32, (3 * cols, 128), 0)
    pick = jnp.where(row // DH == lanes(3 * cols, 128), 1.0, 0.0).astype(bf16)

    def normed(start):
        unit, _ = unit_rows(x_ref[start : start + step, :].astype(f32))
        return (unit * gain + shift).astype(bf16)

    largest = None
    ready = normed(0)
    for start in range(0, rows, step):
        following = normed(start + step) if start + step < rows else None
        values = (dot(ready, w_all[...], NT) + bias).astype(bf16)
        out_ref[start : start + step, :] = values
        squares = jnp.max(dot(values * values, pick), axis=0, keepdims=True)
        largest = squares if largest is None else jnp.maximum(largest, squares)
        ready = following
    bound_ref[0] = jnp.broadcast_to(largest, (8, 128))


def project(tokens, vectors, weight, bias):
    rows, width = tokens.shape
    cols = weight.shape[1]
    block = 512
    fixed = lambda shape: pl.BlockSpec(shape, lambda i: (0,) * len(shape))
    return pl.pallas_call(
        project_kernel,
        grid=(rows // block,),
        in_specs=[
            pl.BlockSpec((block, width), lambda i: (i, 0)),
            fixed(vectors.shape),
            fixed(weight.shape),
            fixed(bias.shape),
        ],
        out_specs=[
            pl.BlockSpec((block, 3 * cols), lambda i: (i, 0)),
            pl.BlockSpec((1, 8, 128), lambda i: (i, 0, 0)),
        ],
        out_shape=[
            jax.ShapeDtypeStruct((rows, 3 * cols), bf16),
            jax.ShapeDtypeStruct((rows // block, 8, 128), f32),
        ],
        scratch_shapes=[pltpu.VMEM((3 * cols, width), bf16)],
        compiler_params=pltpu.CompilerParams(vmem_limit_bytes=VMEM),
        cost_estimate=cost(6 * rows * width * cols, 2 * rows * (width + 3 * cols)),
        name="project",
    )(tokens, vectors, weight, bias)


def attend_kernel(bucket_ref, kvq_ref, bound_ref, o_ref, lse_ref, kx, vt, *, block):
    cols, image_len = o_ref.shape
    heads = cols // DH
    at_q = 2 * cols
    length = live_length(bucket_ref[pl.program_id(0)], image_len)
    squares = jnp.max(bound_ref[...], axis=0)
    lane = lanes(8, 128)
    largest_key = jnp.max(jnp.where(lane < heads, squares, 0.0))
    of_query = (lane >= 2 * heads) & (lane < 3 * heads)
    largest_query = jnp.max(jnp.where(of_query, squares, 0.0))
    small = largest_key * largest_query <= (8.0 * 60.0) ** 2

    def run(live, subtract):
        scaled = kvq_ref[0:live, 0:192] * jnp.asarray(0.125, bf16)
        flipped = jnp.transpose(kvq_ref[0:live, 128:384])
        lane = lanes(live, 128)
        for h in range(heads):
            if h < 2:
                keep = (lane < DH) if h == 0 else (lane >= DH)
                kx[h, 0:live, :] = jnp.where(keep, scaled[:, 0:128], jnp.zeros((), bf16))
            else:
                kx[h, 0:live, 0:DH] = scaled[:, 128:192]
            vt[h, 0:DH, 0:live] = flipped[DH * (h + 1) : DH * (h + 2)]
            vt[h, DH:128, 0:live] = jnp.ones((DH, live), bf16)

        def scores(h, start):
            here = slice(start, start + block)
            if h < 2:
                return dot(kx[h, 0:live, :], kvq_ref[here, at_q : at_q + 128], NT)
            return dot(kx[h, 0:live, 0:DH], kvq_ref[here, at_q + 128 : at_q + 192], NT)

        parts = {}

        def finish(h, start, score):
            offset = 0.0
            if subtract:
                key = lax.broadcasted_iota(jnp.int32, score.shape, 0)
                score = jnp.where(key < length, score, -1e30)
                offset = jnp.max(score, axis=0, keepdims=True)
                score = score - offset
            mixed = dot(vt[h, :, 0:live], jnp.exp(score).astype(bf16))
            total = mixed[DH : DH + 1]
            here = slice(start, start + block)
            parts[h] = -(offset + jnp.log(total))
            o_ref[DH * h : DH * (h + 1), here] = (mixed[:DH] * (1.0 / total)).astype(bf16)
            if h == heads - 1:
                rows = [parts[i] for i in range(heads)]
                lse_ref[:, here] = jnp.concatenate(rows + [jnp.zeros((8 - heads, block), f32)], axis=0)

        items = [(h, s) for s in range(0, image_len, block) for h in range(heads)]
        score = scores(*items[0])
        for index, item in enumerate(items):
            following = scores(*items[index + 1]) if index + 1 < len(items) else None
            finish(*item, score)
            score = following

    for live in live_lengths(image_len):
        pl.when(small & (length == live))(functools.partial(run, live, False))
    pl.when(jnp.logical_not(small))(functools.partial(run, image_len, True))


def attend(buckets, kvq, bound):
    rows = kvq.shape[0]
    cols = kvq.shape[1] // 3
    images = buckets.shape[0]
    image_len = rows // images
    heads = cols // DH
    by_rows = lambda w: pl.BlockSpec((image_len, w), lambda i, b: (i, 0))
    by_cols = lambda w: pl.BlockSpec((w, image_len), lambda i, b: (0, i))
    return pl.pallas_call(
        functools.partial(attend_kernel, block=512),
        grid_spec=pltpu.PrefetchScalarGridSpec(
            num_scalar_prefetch=1,
            grid=(images,),
            in_specs=[by_rows(3 * cols), pl.BlockSpec(bound.shape, lambda i, b: (0, 0, 0))],
            out_specs=[by_cols(cols), by_cols(8)],
            scratch_shapes=[
                pltpu.VMEM((heads, image_len, 128), bf16),
                pltpu.VMEM((heads, 128, image_len), bf16),
            ],
        ),
        out_shape=[
            jax.ShapeDtypeStruct((cols, rows), bf16),
            jax.ShapeDtypeStruct((8, rows), f32),
        ],
        compiler_params=pltpu.CompilerParams(vmem_limit_bytes=VMEM),
        cost_estimate=cost(16 * rows * image_len * cols, 12 * rows * cols, rows * image_len * heads),
        name="attend",
    )(buckets, kvq, bound)


def image_back_kernel(bucket_ref, which_ref, kvq_ref, lse_ref, o_ref, do_ref, vec_ref, *refs, block, stage, dp_size, orders):
    refs = list(refs)
    take = lambda count: [refs.pop(0) for _ in range(count)]
    x_any, w_any = take(2)
    old = take(3) if stage else None
    outs = take((2, 3, 1)[stage])
    dw_outs = take(2 if stage == 2 else 1)
    small_out, bias_out = take(2)
    dox, dot_t, qx, q_t, kx, vx, k_t, grad_q, grads, x, w_all, da_s, normed, dw, sems = take(15)
    cols, image_len = o_ref.shape
    heads = cols // DH
    image = which_ref[0]
    loads = [
        pltpu.make_async_copy(x_any.at[pl.ds(image * image_len, image_len)], x, sems.at[0]),
    ]
    for index, source in enumerate((1, 2, 0)):
        target = w_all.at[pl.ds(index * cols, cols)]
        loads.append(pltpu.make_async_copy(w_any.at[source], target, sems.at[7 + index]))
    if stage:
        loads.append(pltpu.make_async_copy(old[0], dw, sems.at[3]))
    for load in loads:
        load.start()
    length = live_length(bucket_ref[image], image_len)
    inner = []
    for h in range(heads):
        own = slice(DH * h, DH * (h + 1))
        product = do_ref[own, :].astype(f32) * o_ref[own, :].astype(f32)
        inner += list(split3(-jnp.sum(product, axis=0, keepdims=True)))
    blank = [jnp.zeros((DH - 3 * heads, image_len), f32)]
    dot_t[0:cols, :] = do_ref[...]
    dot_t[cols:, :] = jnp.concatenate(inner + blank, axis=0).astype(bf16)
    dox[...] = jnp.transpose(dot_t[...])
    outer = [part for h in range(heads) for part in split3(lse_ref[h : h + 1, :])]
    row = lax.broadcasted_iota(jnp.int32, (DH - 3 * heads, image_len), 0)
    outer = jnp.concatenate(outer + [jnp.where(row == 0, 1.0, 0.0)], axis=0).astype(bf16)
    q = kvq_ref[:, 2 * cols : 3 * cols]
    q_t[0:cols, :] = jnp.transpose(q)
    q_t[cols:, :] = outer
    qx[...] = jnp.concatenate([q, jnp.transpose(outer)], axis=1)
    scaled = kvq_ref[:, 0:cols] * jnp.asarray(0.125, bf16)
    values = kvq_ref[:, cols : 2 * cols]
    k_t[0:cols, :] = jnp.transpose(scaled)
    lane, side = lanes(image_len, cols), lanes(image_len, DH)
    key = lax.broadcasted_iota(jnp.int32, (image_len, DH), 0)
    zero = jnp.zeros((), bf16)
    for h in range(heads):
        keep = (lane >= DH * h) & (lane < DH * (h + 1))
        ones = jnp.where((side >= 3 * h) & (side < 3 * h + 3), 1.0, 0.0)
        dead = jnp.where((side == 3 * heads) & (key >= length), -1e30, ones).astype(bf16)
        kx[h] = jnp.concatenate([jnp.where(keep, scaled, zero), dead], axis=1)
        vx[h] = jnp.concatenate([jnp.where(keep, values, zero), ones.astype(bf16)], axis=1)
    grads[:, 0 : 2 * cols] = jnp.zeros((image_len, 2 * cols), bf16)
    grad_q[...] = jnp.zeros_like(grad_q)

    def key_block(index, carry):
        here = pl.ds(pl.multiple_of(index * block, block), block)
        parts = {}
        for h in range(heads):
            probs = jnp.exp(dot(kx[h, here, :], qx[...], NT))
            grad_probs = dot(vx[h, here, :], dox[...], NT)
            grad_scores = (probs * grad_probs).astype(bf16)
            pair = slice(0, 128) if h < 2 else slice(128, 256)
            own = slice(DH * (h % 2), DH * (h % 2) + DH)
            grad_v = dot(dot_t[pair, :], probs.astype(bf16), NT)[own]
            grad_k = dot(q_t[pair, :], grad_scores, NT)[own]
            parts[h] = (grad_k * 0.125, grad_v)
            grad_q[DH * h : DH * (h + 1), :] += dot(k_t[pair, here], grad_scores)[own]
        stack = [parts[h][j] for j in range(2) for h in range(heads)]
        grads[here, 0 : 2 * cols] = jnp.transpose(jnp.concatenate(stack, axis=0).astype(bf16))
        return carry

    lax.fori_loop(0, (length + block - 1) // block, key_block, 0)
    grads[:, 2 * cols : 3 * cols] = jnp.transpose(grad_q[...].astype(bf16))

    for load in loads:
        load.wait()
    gain, shift = vec_ref[0:1, :].astype(f32), vec_ref[1:2, :].astype(f32)
    step = 256
    sums = [jnp.zeros((1, 1), f32)] * 3
    if stage:
        sums = [old[1][0:1, :], old[1][1:2, :], old[2][0:1, :]]
    for start in range(0, image_len, step):
        here = slice(start, start + step)
        unit, _ = unit_rows(x[here, :].astype(f32))
        normed[here, :] = (unit * gain + shift).astype(bf16)
        part = grads[here, :]
        da = dot(part, w_all[...])
        da_s[here, :] = da.astype(bf16)
        more = [da * unit, da, part.astype(f32)]
        sums = [old_sum + jnp.sum(new, axis=0, keepdims=True) for old_sum, new in zip(sums, more)]
    me = lax.axis_index("tensor")
    core, side = me % 2, me // 2
    if stage == 0:
        half = image_len // 2
        spans = [(core * half, half), ((1 - core) * half, half)]
    elif stage == 1:
        half = image_len // 4
        far = (1 - side) * 2 * half
        spans = [(far + core * half, half), (far + (1 - core) * half, half), (side * 2 * half, 2 * half)]
    else:
        spans = [(0, image_len)]
    stores = []
    for index, (start, size) in enumerate(spans):
        source = da_s.at[pl.ds(pl.multiple_of(start, 256), size)] if size < image_len else da_s
        stores.append(pltpu.make_async_copy(source, outs[index], sems.at[4 + index]))
        stores[-1].start()
    fresh = dot(normed[...], grads[...], TN)
    if stage:
        fresh = fresh + dw[...]
    if stage == 2:
        fresh = fresh.astype(bf16)
        at = 0
        for order, target in zip(orders, dw_outs):
            piece = fresh[:, at : at + target.shape[1]]
            at += target.shape[1]
            target[...] = dot(halving_order(order, fresh.shape[0], dp_size), piece).astype(bf16)
    else:
        dw_outs[0][...] = fresh
    small_out[...] = jnp.concatenate([sums[0], sums[1], jnp.zeros((6, sums[0].shape[1]), f32)], axis=0)
    bias_out[...] = jnp.broadcast_to(sums[2], bias_out.shape)
    for store in stores:
        store.wait()


def image_back(stage, buckets, which, kvq, lse, o, grad_o, vectors, tokens, weight, dp_size, orders, old):
    rows, width = tokens.shape
    cols = o.shape[0]
    images = buckets.shape[0]
    image_len = rows // images
    heads = cols // DH
    half = image_len // 2
    da_rows = [[half, half], [half // 2, half // 2, half], [image_len]][stage]
    picked = lambda w: pl.BlockSpec((image_len, w), lambda i, b, s: (s[0], 0))
    across = lambda w: pl.BlockSpec((w, image_len), lambda i, b, s: (0, s[0]))
    fixed = lambda shape: pl.BlockSpec(shape, lambda i, b, s: (0,) * len(shape))
    if stage == 2:
        dw_shapes = [((width, n), bf16) for n in (256, 3 * cols - 256)]
    else:
        dw_shapes = [((width, 3 * cols), f32)]
    return pl.pallas_call(
        functools.partial(image_back_kernel, block=256, stage=stage, dp_size=dp_size, orders=orders),
        grid_spec=pltpu.PrefetchScalarGridSpec(
            num_scalar_prefetch=2,
            grid=(1,),
            in_specs=[picked(3 * cols), across(8), across(cols), across(cols), fixed(vectors.shape)]
            + [ANY] * 2
            + ([ANY, fixed((8, width)), fixed((8, 3 * cols))] if stage else []),
            out_specs=[ANY] * len(da_rows)
            + [fixed(shape) for shape, _ in dw_shapes]
            + [fixed((8, width)), fixed((8, 3 * cols))],
            scratch_shapes=[
                pltpu.VMEM((image_len, 256), bf16),
                pltpu.VMEM((256, image_len), bf16),
                pltpu.VMEM((image_len, 256), bf16),
                pltpu.VMEM((256, image_len), bf16),
                pltpu.VMEM((heads, image_len, 256), bf16),
                pltpu.VMEM((heads, image_len, 256), bf16),
                pltpu.VMEM((256, image_len), bf16),
                pltpu.VMEM((cols, image_len), f32),
                pltpu.VMEM((image_len, 3 * cols), bf16),
                pltpu.VMEM((image_len, width), bf16),
                pltpu.VMEM((3 * cols, width), bf16),
                pltpu.VMEM((image_len, width), bf16),
                pltpu.VMEM((image_len, width), bf16),
                pltpu.VMEM((width, 3 * cols), f32),
                pltpu.SemaphoreType.DMA((10,)),
            ],
        ),
        out_shape=[jax.ShapeDtypeStruct((n, width), bf16) for n in da_rows]
        + [
            *[jax.ShapeDtypeStruct(*shape) for shape in dw_shapes],
            jax.ShapeDtypeStruct((8, width), f32),
            jax.ShapeDtypeStruct((8, 3 * cols), f32),
        ],
        compiler_params=pltpu.CompilerParams(vmem_limit_bytes=VMEM),
        cost_estimate=cost(10**6, 10**4),
        name=f"image_back_{stage}",
    )(buckets, which, kvq, lse, o, grad_o, vectors, tokens, weight, *old)


def rows_kernel(me_ref, *refs, parts, dp_size, orders):
    refs = list(refs)
    take = lambda count: [refs.pop(0) for _ in range(count)]
    x_ref, g_ref, vec_ref, bias_ref, o_in = take(5)
    wo_in, up_in, down_in = take(2), take(2), take(2)
    quarters = [take(5), take(5)]
    y_ref, dh_ref, down_keep, down_send, up_keep, up_send, small_ref, do_ref = take(8)
    wo_w, up_w, down_w, hidden, normed, mixed, back, g_t, c_t, z_s, du_s, perm_ref, grads, wo_grads, sems = take(15)
    rows, width = x_ref.shape
    hid = up_w.shape[2]
    part = pl.program_id(0)
    quarter = lax.axis_index("dp") % 4

    def loads(source, target, row, at):
        found = [[pltpu.make_async_copy(source[r], target.at[r], sems.at[row, r])] for r in range(2)]
        size = target.shape[1] // 4
        for r in (2, 3):
            found.append([])
            for i in range(4):
                piece, here = quarters[r - 2][i], at
                if i == 3 and at >= split:
                    piece, here = quarters[r - 2][4], at - split
                place = target.at[r, pl.ds(pl.multiple_of((quarter ^ i) * size, size), size)]
                index = 2 + 4 * (r - 2) + i
                found[r].append(pltpu.make_async_copy(piece.at[pl.ds(here, size)], place, sems.at[row, index]))
        return found

    mixed_cols = o_in.shape[1]
    split = (mixed_cols + hid) // 4
    wo_loads = loads(wo_in, wo_w, 0, 0)
    up_loads = loads(up_in, up_w, 1, mixed_cols // 4)
    down_loads = loads(down_in, down_w, 2, (mixed_cols + hid) // 4)
    gain, shift = vec_ref[2:3, :].astype(f32), vec_ref[3:4, :].astype(f32)

    def store(r):
        down = (down_send if r % 2 else down_keep).at[r // 2, :, pl.ds(0, hid)]
        up = (up_send if r % 2 else up_keep).at[r // 2]
        return [
            pltpu.make_async_copy(grads.at[r, :, pl.ds(0, hid)], down, sems.at[3, r]),
            pltpu.make_async_copy(grads.at[r, :, pl.ds(hid, hid)], up, sems.at[3, 4 + r]),
        ]

    def store_out(r):
        target = (down_send if r % 2 else down_keep).at[r // 2, :, pl.ds(hid, 256)]
        return pltpu.make_async_copy(wo_grads.at[r], target, sems.at[3, 8 + r])

    @pl.when(part == 0)
    def _():
        for group in wo_loads + up_loads + down_loads:
            for load in group:
                load.start()
        for group in wo_loads:
            for load in group:
                load.wait()
        perm_ref[...] = halving_order(orders[0], width, dp_size)
        g_t[...] = dot(perm_ref[...], g_ref[...], NT).astype(bf16)
        attended = dot(o_in[0], wo_w[0], TN)
        for r in range(1, parts):
            attended += dot(o_in[r], wo_w[r], TN)
        h1 = x_ref[...].astype(f32) + attended + vec_ref[4:5, :].astype(f32)
        hidden[...] = h1
        unit, _ = unit_rows(h1)
        normed[...] = (unit * gain + shift).astype(bf16)
        c_t[...] = dot(halving_order(orders[1], width, dp_size), normed[...], NT).astype(bf16)
        mixed[...] = jnp.zeros_like(mixed)
        back[...] = jnp.zeros_like(back)
        small_ref[...] = jnp.zeros_like(small_ref)

    for r in range(parts):

        @pl.when(part == r)
        def _():
            for load in up_loads[r] + down_loads[r]:
                load.wait()

    step = 256
    chunks = [slice(s, s + step) for s in range(0, hid, step)]

    def first(cols):
        u = dot(normed[...], up_w[part, :, cols]) + bias_ref[part, 0:1, cols]
        return u, dot(g_ref[...], down_w[part, cols, :], NT)

    def bend(cols, u, dz):
        square = u * u
        scaled = u * GELU_SCALE
        gate = 0.5 + 0.5 * jnp.tanh(scaled * (1.0 + GELU_CUBE * square))
        z_s[:, cols] = (u * gate).astype(bf16)
        slope = gate + (2.0 * gate) * (1.0 - gate) * scaled * (1.0 + (3.0 * GELU_CUBE) * square)
        du = (dz * slope).astype(bf16)
        du_s[:, cols] = du
        small_ref[pl.ds(8 + part, 1), cols] = jnp.sum(du.astype(f32), axis=0, keepdims=True)

    def weigh(cols):
        grads[part, :, cols] = dot(g_t[...], z_s[:, cols]).astype(bf16)
        later = slice(hid + cols.start, hid + cols.stop)
        grads[part, :, later] = dot(c_t[...], du_s[:, cols]).astype(bf16)

    ready = first(chunks[0])
    for index, cols in enumerate(chunks):
        following = first(chunks[index + 1]) if index + 1 < len(chunks) else None
        bend(cols, *ready)
        if index:
            weigh(chunks[index - 1])
        ready = following
    mixed[...] += dot(z_s[...], down_w[part])
    weigh(chunks[-1])
    back[...] += dot(du_s[...], up_w[part], NT)
    for r in range(parts):

        @pl.when(part == r)
        def _():
            for copy in store(r):
                copy.start()

    @pl.when(part == parts - 1)
    def _():
        h1 = hidden[...]
        y_ref[...] = (h1 + mixed[...] + vec_ref[5:6, :].astype(f32)).astype(bf16)
        unit, inverse = unit_rows(h1)
        dc = back[...]
        wide_g = g_ref[...].astype(f32)
        dh = wide_g + norm_back(dc, gain, unit, inverse)
        dh_ref[...] = dh
        e = dh.astype(bf16)
        for index, values in enumerate([dc * unit, dc, dh, wide_g]):
            small_ref[2 + index : 3 + index, :] = jnp.sum(values, axis=0, keepdims=True)
        for r in range(parts):
            do_ref[r] = dot(wo_w[r], e, NT).astype(bf16)
        e_t = dot(perm_ref[...], e, NT).astype(bf16)
        blank = jnp.zeros((width, 256 - mixed_cols), bf16)
        for r in range(parts):
            wo_grads[r] = jnp.concatenate([dot(e_t, o_in[r], NT).astype(bf16), blank], axis=1)
            store_out(r).start()
        for r in range(parts):
            for copy in store(r) + [store_out(r)]:
                copy.wait()


def own_rows(me, x, g, vectors, up_bias, o_parts, wo, up, down, quarters, dp_size, orders):
    parts, cols, rows = o_parts.shape
    width = x.shape[1]
    hid = up[0].shape[1]
    fixed = lambda shape: pl.BlockSpec(shape, lambda r, m: (0,) * len(shape))
    own = pl.BlockSpec((rows, width), lambda r, m: (m[0], 0))
    packed = [jax.ShapeDtypeStruct((parts // 2, width, hid + 256), bf16)] * 2
    packed += [jax.ShapeDtypeStruct((parts // 2, width, hid), bf16)] * 2
    return pl.pallas_call(
        functools.partial(rows_kernel, parts=parts, dp_size=dp_size, orders=orders),
        grid_spec=pltpu.PrefetchScalarGridSpec(num_scalar_prefetch=1, grid=(parts,),
        in_specs=[
            own,
            own,
            fixed(vectors.shape),
            fixed(up_bias.shape),
            fixed(o_parts.shape),
        ]
        + [ANY] * 16,
        out_specs=[
            fixed((rows, width)),
            fixed((rows, width)),
            ANY,
            ANY,
            ANY,
            ANY,
            fixed((16, width)),
            fixed((parts, cols, rows)),
        ],
        scratch_shapes=[
            pltpu.VMEM((parts, cols, width), bf16),
            pltpu.VMEM((parts, width, hid), bf16),
            pltpu.VMEM((parts, hid, width), bf16),
            pltpu.VMEM((rows, width), f32),
            pltpu.VMEM((rows, width), bf16),
            pltpu.VMEM((rows, width), f32),
            pltpu.VMEM((rows, width), f32),
            pltpu.VMEM((width, rows), bf16),
            pltpu.VMEM((width, rows), bf16),
            pltpu.VMEM((rows, hid), bf16),
            pltpu.VMEM((rows, hid), bf16),
            pltpu.VMEM((width, width), bf16),
            pltpu.VMEM((parts, width, 2 * hid), bf16),
            pltpu.VMEM((parts, width, 256), bf16),
            pltpu.SemaphoreType.DMA((4, 12)),
        ],
        ),
        out_shape=[
            jax.ShapeDtypeStruct((rows, width), bf16),
            jax.ShapeDtypeStruct((rows, width), f32),
            *packed,
            jax.ShapeDtypeStruct((16, width), f32),
            jax.ShapeDtypeStruct((parts, cols, rows), bf16),
        ],
        compiler_params=pltpu.CompilerParams(vmem_limit_bytes=VMEM),
        cost_estimate=cost(12 * rows * width * hid * parts, 8 * parts * width * hid, rows * hid * parts),
        name="own_rows",
    )(me, x, g, vectors, up_bias, o_parts, *wo, *up, *down, *quarters[0], *quarters[1])


def greet(partners):
    barrier = pltpu.get_barrier_semaphore()
    for partner in partners:
        pl.semaphore_signal(barrier, inc=1, device_id=partner, device_id_type=pl.DeviceIdType.MESH)
    pl.semaphore_wait(barrier, len(partners))


def send(source, target, sems, index, partner):
    return pltpu.make_async_remote_copy(
        src_ref=source,
        dst_ref=target,
        send_sem=sems.at[0, index],
        recv_sem=sems.at[1, index],
        device_id=partner,
        device_id_type=pl.DeviceIdType.MESH,
    )


def out_kernel(*refs, parts):
    refs = list(refs)
    take = lambda count: [refs.pop(0) for _ in range(count)]
    o_ref, bias_ref = take(2)
    shards, pieces = take(3), take(3)
    o_all, bias_all = take(2)
    shards_to, pieces_to, across, across_to = take(3), take(3), take(2), take(2)
    own_o, own_bias, sems, local = refs
    dp, me = lax.axis_index("dp"), lax.axis_index("tensor")
    rows = o_all.shape[2]
    partners = [(dp, me ^ r) for r in range(parts)]
    beside, along = (dp ^ 1, me), (dp ^ 2, me)
    greet(partners[1:] + [beside, along])
    copies = []

    def start(source, target, partner):
        copies.append(send(source, target, sems, len(copies), partner))
        copies[-1].start()

    split = across[0].shape[0]
    start(pieces[1].at[pl.ds(0, split)], across[0], along)
    start(pieces[2].at[pl.ds(split, across[1].shape[0])], across[1], beside)
    for r in range(parts - 1, 0, -1):
        source = o_ref.at[:, pl.ds(pl.multiple_of((me ^ r) * rows, rows), rows)]
        start(source, o_all.at[r], partners[r])
        start(bias_ref, bias_all.at[r], partners[r])
    for source, target in zip(shards + pieces, shards_to + pieces_to):
        start(source, target, partners[1])
    mine = o_ref.at[:, pl.ds(pl.multiple_of(me * rows, rows), rows)]
    loads = [pltpu.make_async_copy(mine, own_o, local.at[0]), pltpu.make_async_copy(bias_ref, own_bias, local.at[1])]
    for load in loads:
        load.start()
    for load in loads:
        load.wait()
    stores = [
        pltpu.make_async_copy(own_o, o_all.at[0], local.at[0]),
        pltpu.make_async_copy(own_bias, bias_all.at[0], local.at[1]),
    ]
    for store in stores:
        store.start()
    for index in range(2):
        copies[index].wait_recv()
        start(across[index], across_to[index], partners[1])
    for index, copy in enumerate(copies):
        if index < 2:
            copy.wait_send()
        else:
            copy.wait()
    for store in stores:
        store.wait()


def exchange_out(o, bias, shards, pieces, parts):
    cols, rows = o.shape
    split = pieces[0].shape[0] - shards[2].shape[0] // 4
    like = lambda x, count=None: jax.ShapeDtypeStruct((count or x.shape[0],) + x.shape[1:], x.dtype)
    halves = [like(pieces[0], split), like(pieces[0], pieces[0].shape[0] - split)]
    shapes = [
        jax.ShapeDtypeStruct((parts, cols, rows // parts), bf16),
        jax.ShapeDtypeStruct((parts,) + bias.shape, f32),
        *map(like, shards),
        *map(like, pieces),
        *halves,
        *halves,
    ]
    out = pl.pallas_call(
        functools.partial(out_kernel, parts=parts),
        in_specs=[ANY] * 8,
        out_specs=[ANY] * len(shapes),
        out_shape=shapes,
        scratch_shapes=[
            pltpu.VMEM((cols, rows // parts), bf16),
            pltpu.VMEM(bias.shape, f32),
            pltpu.SemaphoreType.DMA((2, 18)),
            pltpu.SemaphoreType.DMA((2,)),
        ],
        compiler_params=pltpu.CompilerParams(collective_id=1, has_side_effects=True),
        cost_estimate=cost(15 * 10**9, 10**7),
        name="exchange_out",
    )(o, bias, *shards, *pieces)
    return out[0], out[1], out[2:5], out[5:8], out[8:10], out[10:12]


def back_kernel(do_all, *refs, parts):
    refs = list(refs)
    take = lambda count: [refs.pop(0) for _ in range(count)]
    keeps, aways = take(2), take(2)
    (do_ref,) = take(1)
    kept, sent = take(2), take(2)
    held, came, own_do, sems, local = take(2), take(2), *take(3)
    dp, me = lax.axis_index("dp"), lax.axis_index("tensor")
    rows = do_all.shape[2]
    partners = [(dp, me ^ r) for r in range(parts)]
    greet(partners[1:])
    mine = do_ref.at[:, pl.ds(pl.multiple_of(me * rows, rows), rows)]
    copies = [send(do_all.at[r], mine, sems, r - 1, partners[r]) for r in range(parts - 1, 0, -1)]
    items = [(track, index) for track in range(2) for index in range(2)]
    core, loads = [], []
    for number, (track, index) in enumerate(items):
        core.append(send(aways[track].at[index], came[track].at[index], sems, parts + number, partners[1]))
        loads.append(pltpu.make_async_copy(keeps[track].at[index], held[track].at[index], local.at[number]))
    load = pltpu.make_async_copy(do_all.at[0], own_do, local.at[4])
    for copy in copies + core + loads + [load]:
        copy.start()
    load.wait()
    store = pltpu.make_async_copy(own_do, mine, local.at[4])
    store.start()
    stores = []
    half = keeps[0].shape[1] // 2
    for number, (track, index) in enumerate(items):
        core[number].wait()
        loads[number].wait()
        total = held[track][index].astype(f32) + came[track][index].astype(f32)
        held[track][index] = total.astype(bf16)
        for at, target in enumerate((kept[track], sent[track])):
            source = held[track].at[index, pl.ds(at * half, half)]
            stores.append(pltpu.make_async_copy(source, target.at[index], local.at[5 + 2 * number + at]))
            stores[-1].start()
    for copy in copies + stores + [store]:
        copy.wait()


def exchange_back(do_parts, keeps, aways):
    parts, cols, rows = do_parts.shape
    half = lambda x: jax.ShapeDtypeStruct((x.shape[0], x.shape[1] // 2, x.shape[2]), bf16)
    shapes = [jax.ShapeDtypeStruct((cols, parts * rows), bf16), *map(half, keeps), *map(half, keeps)]
    buffers = [pltpu.VMEM(x.shape, bf16) for x in keeps]
    out = pl.pallas_call(
        functools.partial(back_kernel, parts=parts),
        in_specs=[ANY] * 5,
        out_specs=[ANY] * 5,
        out_shape=shapes,
        scratch_shapes=buffers * 2
        + [
            pltpu.VMEM((cols, rows), bf16),
            pltpu.SemaphoreType.DMA((2, parts + 4)),
            pltpu.SemaphoreType.DMA((13,)),
        ],
        compiler_params=pltpu.CompilerParams(collective_id=2, has_side_effects=True, vmem_limit_bytes=VMEM),
        cost_estimate=cost(15 * 10**9, 10**7),
        name="exchange_back",
    )(do_parts, *keeps, *aways)
    return out[0], out[1:3], out[3:5]


def pick_kernel(*refs):
    *sources, target, sems = refs
    quarter = lax.axis_index("dp") % 4
    copies, at = [], 0
    for index, source in enumerate(sources):
        size = source.shape[0] // 4
        piece = source.at[pl.ds(pl.multiple_of(quarter * size, size), size)]
        copies.append(pltpu.make_async_copy(piece, target.at[pl.ds(at, size)], sems.at[index]))
        copies[index].start()
        at += size
    for copy in copies:
        copy.wait()


def pick_quarter(shards):
    rows = sum(shard.shape[0] for shard in shards) // 4
    return pl.pallas_call(
        pick_kernel,
        in_specs=[ANY] * len(shards),
        out_specs=pl.BlockSpec(memory_space=pltpu.VMEM),
        out_shape=jax.ShapeDtypeStruct((rows, shards[0].shape[1]), bf16),
        scratch_shapes=[pltpu.SemaphoreType.DMA((len(shards),))],
        name="pick_quarter",
    )(*shards)


def finish_kernel(
    own_any, mid_any, far_own_any, mid_keep_any, mid_came_any, x_any, dh_any, vec_ref, late_ref, bias_ref, early_ref, *refs,
    dp_size, tracks,
):
    bits = dp_size.bit_length() - 1
    refs = list(refs)
    take = lambda count: [refs.pop(0) for _ in range(count)]
    weights = [take(1), take(1)] + [take(2) for _ in tracks[2:]]
    (out_ref,) = take(1)
    weights_out = take(len(tracks))
    (sums_out,) = take(1)
    held, other, far_own, mid_keep, mid_came, far_mid, x_v, dh_v = take(8)
    sent = [take(len(order)) for order in tracks]
    got = [take(len(order)) for order in tracks]
    totals = take(len(tracks))
    sums, got_s, sems, w_sems, local = refs
    dp, me = lax.axis_index("dp"), lax.axis_index("tensor")
    core, side = me % 2, me // 2
    rows, width = out_ref.shape
    image_len = own_any.shape[0]
    half = image_len // 2
    x_own = x_any.at[pl.ds(pl.multiple_of(me * rows, rows), rows)]
    at_own = side * half
    at_mid = (1 - side) * image_len
    across = [(dp, me ^ 1), (dp, me ^ 2)]
    along = [(dp ^ (1 << bit), me) for bit in range(bits)]
    greet(across + along)

    loads = [
        pltpu.make_async_copy(own_any, held.at[pl.ds(pl.multiple_of(at_own, half), image_len)], local.at[0]),
        pltpu.make_async_copy(mid_any, held.at[pl.ds(pl.multiple_of(at_mid, half), half)], local.at[1]),
        pltpu.make_async_copy(far_own_any, far_own, local.at[2]),
        pltpu.make_async_copy(mid_keep_any, mid_keep, local.at[3]),
        pltpu.make_async_copy(mid_came_any, mid_came, local.at[6]),
        pltpu.make_async_copy(x_own, x_v, local.at[4]),
        pltpu.make_async_copy(dh_any, dh_v, local.at[5]),
    ]
    for load in loads:
        load.start()
    mid_load = loads.pop(4)
    mid_load.wait()
    loads[3].wait()
    mid_keep[...] = (mid_keep[...].astype(f32) + mid_came[...].astype(f32)).astype(bf16)

    copies = [[] for _ in tracks]
    tall = [totals[track].shape[0] for track in range(len(tracks))]

    def first(track, here):
        terms = [term[here, :].astype(f32) for term in weights[track]]
        return terms[0] + terms[1] if len(terms) > 1 else terms[0]

    def send_weight(track, step):
        target = sent[track][step]
        bit = tracks[track][step]
        if bit < 0:
            kept, came = weights[track]
            target[...] = (kept[1].astype(f32) + came[1].astype(f32)).astype(target.dtype)
            route = across[1]
        else:
            span = tall[track] // 2
            if step == 0:
                target[...] = first(track, slice(span, 2 * span)).astype(target.dtype)
            else:
                target[...] = totals[track][span : 2 * span, :].astype(target.dtype)
            route = along[bit]
        index = sum(len(order) for order in tracks[:track]) + step
        copies[track].append(send(target, got[track][step], w_sems, index, route))
        copies[track][step].start()

    def add_weight(track, step):
        bit = tracks[track][step]
        copies[track][step].wait()
        if bit < 0:
            kept, came = weights[track]
            kept = kept[0].astype(f32) + came[0].astype(f32)
        else:
            tall[track] //= 2
            span = tall[track]
            kept = totals[track][0:span, :] if step else first(track, slice(0, span))
        totals[track][0 : tall[track], :] = kept + got[track][step][...].astype(f32)

    send_weight(0, 0)
    send_weight(1, 0)
    send_weight(2, 0)
    mid_copy = send(mid_keep, far_mid, sems, 14, across[1])

    sums[...] = early_ref[...]
    sums[0:2, :] = late_ref[0:2, :]
    sums[12:13, 0 : bias_ref.shape[1]] = bias_ref[0:1, :]
    routes = across + along
    s_copies = []

    def send_sums(step):
        s_copies.append(send(sums, got_s.at[step], sems, step, routes[step]))
        s_copies[step].start()

    def add_sums(step):
        s_copies[step].wait()
        if step < 2:
            sums[0:6, :] += got_s[step, 0:6, :]
            new = [sums[8 + r : 9 + r, :] + got_s[step, 8 + (r ^ (1 << step)) : 9 + (r ^ (1 << step)), :] for r in range(4)]
            for r in range(4):
                sums[8 + r : 9 + r, :] = new[r]
        else:
            sums[...] += got_s[step]

    def turn(track, step):
        add_weight(track, step)
        if step + 1 < len(tracks[track]):
            send_weight(track, step + 1)

    send_sums(0)
    turn(0, 0)
    turn(1, 0)
    add_sums(0)
    send_sums(1)
    turn(2, 0)
    send_weight(3, 0)
    turn(0, 1)
    turn(1, 1)
    add_sums(1)
    send_sums(2)
    mid_copy.start()

    for load in loads[:3]:
        load.wait()
    here = pl.ds(pl.multiple_of(at_own + core * half, half), half)
    held[here, :] = (held[here, :].astype(f32) + far_own[...].astype(f32)).astype(bf16)
    turn(3, 0)
    add_sums(2)
    if bits > 1:
        send_sums(3)
    mid_copy.wait()
    here = pl.ds(pl.multiple_of(at_mid + core * (half // 2), half // 2), half // 2)
    held[here, :] = (held[here, :].astype(f32) + far_mid[...].astype(f32)).astype(bf16)
    theirs = held.at[pl.ds(pl.multiple_of((1 - core) * rows, rows), rows)]
    da_copy = send(theirs, other, sems, 15, across[0])
    da_copy.start()
    for step in range(1, bits):
        add_sums(2 + step)
        if step + 1 < bits:
            send_sums(3 + step)
    for load in loads[4:]:
        load.wait()
    da_copy.wait()
    gain = vec_ref[0:1, :].astype(f32)
    step = 256
    for start in range(0, rows, step):
        piece = slice(start, start + step)
        unit, inverse = unit_rows(x_v[piece, :].astype(f32))
        mine = held[pl.ds(pl.multiple_of(core * rows + start, step), step), :].astype(f32)
        da = mine + other[piece, :].astype(f32)
        out_ref[piece, :] = (dh_v[piece, :] + norm_back(da, gain, unit, inverse)).astype(bf16)

    for step in range(1, bits):
        for track in range(len(tracks)):
            if (step > 1 or track > 1) and step < len(tracks[track]):
                turn(track, step)
    for track in range(len(tracks)):
        weights_out[track][...] = totals[track][0 : weights_out[track].shape[0], :]
    sums_out[...] = sums[...]


def unpack_kernel(out_ref, dw_one, dw_two, down_ref, out_to, qkv_ref, down_to, wo_ref):
    out_to[...] = out_ref[...]
    hid, cols = down_to.shape[0], wo_ref.shape[0]
    dw_ref = jnp.concatenate([dw_one[...], dw_two[...]], axis=1)
    for index, at in enumerate((2, 0, 1)):
        qkv_ref[index] = dw_ref[:, at * cols : (at + 1) * cols]
    turned = jnp.transpose(down_ref[...])
    down_to[...] = turned[0:hid]
    wo_ref[...] = turned[hid : hid + cols]


def unpack(out, dw_one, dw_two, down, hid, cols):
    rows = dw_one.shape[0]
    vmem = pl.BlockSpec(memory_space=pltpu.VMEM)
    return pl.pallas_call(
        unpack_kernel,
        in_specs=[vmem] * 4,
        out_specs=[vmem] * 4,
        out_shape=[
            jax.ShapeDtypeStruct(out.shape, bf16),
            jax.ShapeDtypeStruct((3, rows, cols), f32),
            jax.ShapeDtypeStruct((hid, rows), f32),
            jax.ShapeDtypeStruct((cols, rows), f32),
        ],
        compiler_params=pltpu.CompilerParams(vmem_limit_bytes=VMEM),
        name="unpack",
    )(out, dw_one, dw_two, down)


def finish(own, mid, far_own, mid_keep, mid_came, x, dh, vectors, late, bias, early, weights, tracks, dp_size):
    rows, width = dh.shape
    bits = dp_size.bit_length() - 1
    buffers, totals = [], []
    for group, order in zip(weights, tracks):
        tall, wide = group[0].shape[-2:]
        totals.append(pltpu.VMEM((tall, wide), f32))
        for bit in order:
            tall = tall if bit < 0 else tall // 2
            buffers.append(pltpu.VMEM((tall, wide), bf16 if tall % 16 == 0 else f32))
    count = sum(len(order) for order in tracks)
    flat = [weight for group in weights for weight in group]
    vmem = pl.BlockSpec(memory_space=pltpu.VMEM)
    return pl.pallas_call(
        functools.partial(finish_kernel, dp_size=dp_size, tracks=tracks),
        in_specs=[ANY] * 7 + [vmem] * (4 + len(flat)),
        out_specs=[vmem] * (2 + len(tracks)),
        out_shape=[jax.ShapeDtypeStruct((rows, width), bf16)]
        + [jax.ShapeDtypeStruct((width // dp_size, group[0].shape[-1]), f32) for group in weights]
        + [jax.ShapeDtypeStruct((16, width), f32)],
        scratch_shapes=[
            pltpu.VMEM((2 * rows, width), bf16),
            pltpu.VMEM((rows, width), bf16),
            pltpu.VMEM(far_own.shape, bf16),
            pltpu.VMEM(mid_keep.shape, bf16),
            pltpu.VMEM(mid_keep.shape, bf16),
            pltpu.VMEM(mid_keep.shape, bf16),
            pltpu.VMEM((rows, width), bf16),
            pltpu.VMEM((rows, width), f32),
        ]
        + buffers * 2
        + totals
        + [
            pltpu.VMEM((16, width), f32),
            pltpu.VMEM((2 + bits, 16, width), f32),
            pltpu.SemaphoreType.DMA((2, 16)),
            pltpu.SemaphoreType.DMA((2, count)),
            pltpu.SemaphoreType.DMA((7,)),
        ],
        compiler_params=pltpu.CompilerParams(
            collective_id=3, has_side_effects=True, vmem_limit_bytes=VMEM
        ),
        name="finish",
    )(own, mid, far_own, mid_keep, mid_came, x, dh, vectors, late, bias, early, *flat)


def on_device(
    dp_size, tokens, buckets, norm1_gain, norm1_bias, qkv_weight, qkv_bias, out_weight, out_bias,
    norm2_gain, norm2_bias, up_weight, up_bias, down_weight, down_bias, cotangent,
):
    parts = 4
    dp_bits = dp_size.bit_length() - 1
    me = lax.axis_index("tensor")
    token_rows, width = tokens.shape
    share = token_rows // parts
    hid = up_weight.shape[1]
    cols = qkv_weight.shape[2]

    def over_tensor(values, mask):
        return lax.ppermute(values, "tensor", [(i, i ^ mask) for i in range(parts)])

    def over_dp(values, mask):
        return lax.ppermute(values, "dp", [(i, i ^ mask) for i in range(dp_size)])

    def add(*terms):
        total = terms[0].astype(f32)
        for term in terms[1:]:
            total = total + term.astype(f32)
        return total.astype(bf16)

    shards = (out_weight, up_weight, down_weight)
    near = over_tensor(pick_quarter(shards), 2)
    blank = jnp.zeros_like(norm1_gain)
    vectors = jnp.stack(
        [norm1_gain, norm1_bias, norm2_gain, norm2_bias, out_bias, down_bias, blank, blank]
    )
    up_bias_rows = jnp.broadcast_to(up_bias.astype(f32)[None], (8, hid))
    orders = [list(range(dp_bits)), [1, 0] + list(range(2, dp_bits))]
    turned_weight = jnp.swapaxes(qkv_weight, 1, 2)
    kvq, bound = project(tokens, vectors, turned_weight, qkv_bias)
    near, kvq = lax.optimization_barrier((near, kvq))
    beside, along = over_dp(near, 1), over_dp(near, 2)
    o, lse = attend(buckets, kvq, bound)
    near, beside, along, o = lax.optimization_barrier((near, beside, along, o))
    mine = [near, beside, along]
    o_parts, bias_parts, shards_to, other, across, across_to = exchange_out(o, up_bias_rows, shards, mine, parts)
    wo, up, down = zip(shards, shards_to)
    quarters = [[*mine, *across], [*other, *across_to]]
    layer_out, dh, down_keep, down_away, up_keep, up_away, early, do_parts = own_rows(
        me.reshape(1).astype(jnp.int32), tokens, cotangent, vectors, bias_parts, o_parts, wo, up, down, quarters,
        dp_size, orders,
    )
    grad_o, kept, sent = exchange_back(do_parts, [down_keep, up_keep], [down_away, up_away])
    tie = lax.optimization_barrier
    got = [over_dp(half, 1 << order[0]) for half, order in zip(sent, orders)]

    side = me // 2
    order = [2 - 2 * side, jnp.ones_like(side), 2 * side]
    run = lambda stage, old, o: image_back(
        stage, buckets, order[stage].reshape(1).astype(jnp.int32), kvq, lse, o, grad_o, vectors, tokens, turned_weight,
        dp_size, orders, old,
    )
    da_keep, da_send, *old = run(0, [], o)
    came, first_keep = over_tensor(da_send, 1), da_keep
    mid_keep, da_send, mid, *old = run(1, old, o)
    came, o, *got = tie((came, o, *got, *old))[:4]
    far_own = over_tensor(add(first_keep, came), 2)
    mid_came = over_tensor(da_send, 1)
    split = width // 4
    sent = [add(k[:, split:], g[:, split:]) for k, g in zip(kept, got)]
    kept = [add(k[:, :split], g[:, :split]) for k, g in zip(kept, got)]
    got = [over_dp(half, 1 << order[1]) for half, order in zip(sent, orders)]
    own, *dw, late, bias_sums = run(2, old, o)
    *got, far_own, mid_came, own = tie((*got, far_own, mid_came, own))
    weights = [dw[:1], dw[1:]] + [[k, g] for k, g in zip(kept, got)]
    tracks = [orders[0], orders[1], [-1] + orders[0][2:], [-1] + orders[1][2:]]
    out, dw_one, dw_two, down_out, grad_up, sums = finish(
        own, mid, far_own, mid_keep, mid_came, tokens, dh, vectors, late, bias_sums, early, weights, tracks, dp_size
    )
    input_grad, grad_qkv_weight, grad_down, grad_out = unpack(out, dw_one, dw_two, down_out, hid, cols)
    grad_qkv_bias = jnp.stack([sums[12, 2 * cols : 3 * cols], sums[12, cols : 2 * cols]])
    return (
        layer_out,
        input_grad,
        sums[0],
        sums[1],
        grad_qkv_weight,
        grad_qkv_bias,
        grad_out,
        sums[4],
        sums[2],
        sums[3],
        grad_up,
        sums[8],
        grad_down,
        sums[5],
    )


def solution(mesh):
    return jax.shard_map(
        functools.partial(on_device, mesh.shape["dp"]),
        mesh=mesh,
        in_specs=(
            P("dp", None),
            P("dp"),
            P(),
            P(),
            P(None, None, "tensor"),
            P(None, "tensor"),
            P("tensor", None),
            P(),
            P(),
            P(),
            P(None, "tensor"),
            P("tensor"),
            P("tensor", None),
            P(),
            P("dp", None),
        ),
        out_specs=(
            P(("dp", "tensor"), None),
            P(("dp", "tensor"), None),
            P(),
            P(),
            P(None, "dp", "tensor"),
            P(None, "tensor"),
            P("tensor", "dp"),
            P(),
            P(),
            P(),
            P("dp", "tensor"),
            P("tensor"),
            P("tensor", "dp"),
            P(),
        ),
        check_vma=False,
    )
```

```python
import functools

import jax
import jax.numpy as jnp
from jax import lax
from jax.experimental import pallas as pl
from jax.experimental.pallas import tpu as pltpu
from jax.sharding import PartitionSpec as P

DH = 64
NORM_EPSILON = 1e-06
GRID_SIXTEENTHS = (16, 15, 15, 12, 12, 8, 8, 6, 6)
GELU_SCALE = 0.7978845608028654
GELU_CUBE = 0.044715
VMEM = 60 << 20
NN = (((1,), (0,)), ((), ()))
NT = (((1,), (1,)), ((), ()))
TN = (((0,), (0,)), ((), ()))
bf16 = jnp.bfloat16
f32 = jnp.float32
ANY = pl.BlockSpec(memory_space=pl.ANY)


def dot(left, right, dims=NN):
    return lax.dot_general(left, right, dims, preferred_element_type=f32)


def lanes(rows, width):
    return lax.broadcasted_iota(jnp.int32, (rows, width), 1)


def live_lengths(image_len):
    return sorted({image_len * s // 16 for s in GRID_SIXTEENTHS})


def live_length(bucket, image_len):
    length = jnp.int32(0)
    for index, sixteenths in enumerate(GRID_SIXTEENTHS):
        length = jnp.where(bucket == index, image_len * sixteenths // 16, length)
    return length


def cost(flops, nbytes, transcendentals=0):
    return pl.CostEstimate(flops=flops, bytes_accessed=nbytes, transcendentals=transcendentals)


def split3(values):
    high = values.astype(bf16).astype(f32)
    middle = (values - high).astype(bf16).astype(f32)
    return high, middle, values - high - middle


def halving_order(order, width, dp_size):
    bits = dp_size.bit_length() - 1
    size = width // dp_size
    place = lax.broadcasted_iota(jnp.int32, (width, 128), 0)
    block = jnp.zeros_like(place)
    for index in range(1, dp_size):
        block = block + (place >= index * size).astype(jnp.int32)
    turned = jnp.zeros_like(block)
    for step, bit in enumerate(order):
        turned = turned | (((block >> (bits - 1 - step)) & 1) << bit)
    source = (turned ^ lax.axis_index("dp")) * size + (place - block * size)
    lane = lanes(width, 128)
    return jnp.concatenate(
        [jnp.where(source == lane + start, 1.0, 0.0).astype(bf16) for start in range(0, width, 128)], axis=1
    )


def unit_rows(values):
    centred = values - jnp.mean(values, axis=-1, keepdims=True)
    spread = jnp.mean(centred * centred, axis=-1, keepdims=True)
    inverse = lax.rsqrt(spread + NORM_EPSILON)
    return centred * inverse, inverse


def norm_back(grad, gain, unit, inverse):
    scaled = grad * gain
    mean_one = jnp.mean(scaled, axis=-1, keepdims=True)
    mean_two = jnp.mean(scaled * unit, axis=-1, keepdims=True)
    return inverse * (scaled - mean_one - unit * mean_two)


def project_kernel(x_ref, vec_ref, w_ref, bias_ref, out_ref, bound_ref, w_all):
    cols = w_ref.shape[1]

    @pl.when(pl.program_id(0) == 0)
    def _():
        for index, source in enumerate((1, 2, 0)):
            w_all[index * cols : (index + 1) * cols, :] = w_ref[source]

    gain, shift = vec_ref[0:1, :].astype(f32), vec_ref[1:2, :].astype(f32)
    bias = bias_ref[...].astype(f32)
    bias = jnp.concatenate([jnp.zeros((1, cols), f32), bias[1:2], bias[0:1]], axis=1)
    rows, step = x_ref.shape[0], 128
    row = lax.broadcasted_iota(jnp.int32, (3 * cols, 128), 0)
    pick = jnp.where(row // DH == lanes(3 * cols, 128), 1.0, 0.0).astype(bf16)

    def normed(start):
        unit, _ = unit_rows(x_ref[start : start + step, :].astype(f32))
        return (unit * gain + shift).astype(bf16)

    largest = None
    ready = normed(0)
    for start in range(0, rows, step):
        following = normed(start + step) if start + step < rows else None
        values = (dot(ready, w_all[...], NT) + bias).astype(bf16)
        out_ref[start : start + step, :] = values
        squares = jnp.max(dot(values * values, pick), axis=0, keepdims=True)
        largest = squares if largest is None else jnp.maximum(largest, squares)
        ready = following
    bound_ref[0] = jnp.broadcast_to(largest, (8, 128))


def project(tokens, vectors, weight, bias):
    rows, width = tokens.shape
    cols = weight.shape[1]
    block = 512
    fixed = lambda shape: pl.BlockSpec(shape, lambda i: (0,) * len(shape))
    return pl.pallas_call(
        project_kernel,
        grid=(rows // block,),
        in_specs=[
            pl.BlockSpec((block, width), lambda i: (i, 0)),
            fixed(vectors.shape),
            fixed(weight.shape),
            fixed(bias.shape),
        ],
        out_specs=[
            pl.BlockSpec((block, 3 * cols), lambda i: (i, 0)),
            pl.BlockSpec((1, 8, 128), lambda i: (i, 0, 0)),
        ],
        out_shape=[
            jax.ShapeDtypeStruct((rows, 3 * cols), bf16),
            jax.ShapeDtypeStruct((rows // block, 8, 128), f32),
        ],
        scratch_shapes=[pltpu.VMEM((3 * cols, width), bf16)],
        compiler_params=pltpu.CompilerParams(vmem_limit_bytes=VMEM),
        cost_estimate=cost(6 * rows * width * cols, 2 * rows * (width + 3 * cols)),
        name="project",
    )(tokens, vectors, weight, bias)


def attend_kernel(bucket_ref, kvq_ref, bound_ref, o_ref, lse_ref, kx, vt, *, block):
    cols, image_len = o_ref.shape
    heads = cols // DH
    at_q = 2 * cols
    length = live_length(bucket_ref[pl.program_id(0)], image_len)
    squares = jnp.max(bound_ref[...], axis=0)
    lane = lanes(8, 128)
    largest_key = jnp.max(jnp.where(lane < heads, squares, 0.0))
    of_query = (lane >= 2 * heads) & (lane < 3 * heads)
    largest_query = jnp.max(jnp.where(of_query, squares, 0.0))
    small = largest_key * largest_query <= (8.0 * 60.0) ** 2

    def run(live, subtract):
        scaled = kvq_ref[0:live, 0:192] * jnp.asarray(0.125, bf16)
        flipped = jnp.transpose(kvq_ref[0:live, 128:384])
        lane = lanes(live, 128)
        for h in range(heads):
            if h < 2:
                keep = (lane < DH) if h == 0 else (lane >= DH)
                kx[h, 0:live, :] = jnp.where(keep, scaled[:, 0:128], jnp.zeros((), bf16))
            else:
                kx[h, 0:live, 0:DH] = scaled[:, 128:192]
            vt[h, 0:DH, 0:live] = flipped[DH * (h + 1) : DH * (h + 2)]
            vt[h, DH:128, 0:live] = jnp.ones((DH, live), bf16)

        def scores(h, start):
            here = slice(start, start + block)
            if h < 2:
                return dot(kx[h, 0:live, :], kvq_ref[here, at_q : at_q + 128], NT)
            return dot(kx[h, 0:live, 0:DH], kvq_ref[here, at_q + 128 : at_q + 192], NT)

        parts = {}

        def finish(h, start, score):
            offset = 0.0
            if subtract:
                key = lax.broadcasted_iota(jnp.int32, score.shape, 0)
                score = jnp.where(key < length, score, -1e30)
                offset = jnp.max(score, axis=0, keepdims=True)
                score = score - offset
            mixed = dot(vt[h, :, 0:live], jnp.exp(score).astype(bf16))
            total = mixed[DH : DH + 1]
            here = slice(start, start + block)
            parts[h] = -(offset + jnp.log(total))
            o_ref[DH * h : DH * (h + 1), here] = (mixed[:DH] * (1.0 / total)).astype(bf16)
            if h == heads - 1:
                rows = [parts[i] for i in range(heads)]
                lse_ref[:, here] = jnp.concatenate(rows + [jnp.zeros((8 - heads, block), f32)], axis=0)

        items = [(h, s) for s in range(0, image_len, block) for h in range(heads)]
        score = scores(*items[0])
        for index, item in enumerate(items):
            following = scores(*items[index + 1]) if index + 1 < len(items) else None
            finish(*item, score)
            score = following

    for live in live_lengths(image_len):
        pl.when(small & (length == live))(functools.partial(run, live, False))
    pl.when(jnp.logical_not(small))(functools.partial(run, image_len, True))


def attend(buckets, kvq, bound):
    rows = kvq.shape[0]
    cols = kvq.shape[1] // 3
    images = buckets.shape[0]
    image_len = rows // images
    heads = cols // DH
    by_rows = lambda w: pl.BlockSpec((image_len, w), lambda i, b: (i, 0))
    by_cols = lambda w: pl.BlockSpec((w, image_len), lambda i, b: (0, i))
    return pl.pallas_call(
        functools.partial(attend_kernel, block=512),
        grid_spec=pltpu.PrefetchScalarGridSpec(
            num_scalar_prefetch=1,
            grid=(images,),
            in_specs=[by_rows(3 * cols), pl.BlockSpec(bound.shape, lambda i, b: (0, 0, 0))],
            out_specs=[by_cols(cols), by_cols(8)],
            scratch_shapes=[
                pltpu.VMEM((heads, image_len, 128), bf16),
                pltpu.VMEM((heads, 128, image_len), bf16),
            ],
        ),
        out_shape=[
            jax.ShapeDtypeStruct((cols, rows), bf16),
            jax.ShapeDtypeStruct((8, rows), f32),
        ],
        compiler_params=pltpu.CompilerParams(vmem_limit_bytes=VMEM),
        cost_estimate=cost(16 * rows * image_len * cols, 12 * rows * cols, rows * image_len * heads),
        name="attend",
    )(buckets, kvq, bound)


def image_back_kernel(bucket_ref, which_ref, kvq_ref, lse_ref, o_ref, do_ref, vec_ref, *refs, block, stage, dp_size, orders):
    refs = list(refs)
    take = lambda count: [refs.pop(0) for _ in range(count)]
    x_any, w_any = take(2)
    old = take(3) if stage else None
    outs = take((2, 3, 1)[stage])
    dw_outs = take(2 if stage == 2 else 1)
    small_out, bias_out = take(2)
    dox, dot_t, qx, q_t, kx, vx, k_t, grad_q, grads, x, w_all, da_s, normed, dw, sems = take(15)
    cols, image_len = o_ref.shape
    heads = cols // DH
    image = which_ref[0]
    loads = [
        pltpu.make_async_copy(x_any.at[pl.ds(image * image_len, image_len)], x, sems.at[0]),
    ]
    for index, source in enumerate((1, 2, 0)):
        target = w_all.at[pl.ds(index * cols, cols)]
        loads.append(pltpu.make_async_copy(w_any.at[source], target, sems.at[7 + index]))
    if stage:
        loads.append(pltpu.make_async_copy(old[0], dw, sems.at[3]))
    for load in loads:
        load.start()
    length = live_length(bucket_ref[image], image_len)
    inner = []
    for h in range(heads):
        own = slice(DH * h, DH * (h + 1))
        product = do_ref[own, :].astype(f32) * o_ref[own, :].astype(f32)
        inner += list(split3(-jnp.sum(product, axis=0, keepdims=True)))
    blank = [jnp.zeros((DH - 3 * heads, image_len), f32)]
    dot_t[0:cols, :] = do_ref[...]
    dot_t[cols:, :] = jnp.concatenate(inner + blank, axis=0).astype(bf16)
    dox[...] = jnp.transpose(dot_t[...])
    outer = [part for h in range(heads) for part in split3(lse_ref[h : h + 1, :])]
    row = lax.broadcasted_iota(jnp.int32, (DH - 3 * heads, image_len), 0)
    outer = jnp.concatenate(outer + [jnp.where(row == 0, 1.0, 0.0)], axis=0).astype(bf16)
    q = kvq_ref[:, 2 * cols : 3 * cols]
    q_t[0:cols, :] = jnp.transpose(q)
    q_t[cols:, :] = outer
    qx[...] = jnp.concatenate([q, jnp.transpose(outer)], axis=1)
    scaled = kvq_ref[:, 0:cols] * jnp.asarray(0.125, bf16)
    values = kvq_ref[:, cols : 2 * cols]
    k_t[0:cols, :] = jnp.transpose(scaled)
    lane, side = lanes(image_len, cols), lanes(image_len, DH)
    key = lax.broadcasted_iota(jnp.int32, (image_len, DH), 0)
    zero = jnp.zeros((), bf16)
    for h in range(heads):
        keep = (lane >= DH * h) & (lane < DH * (h + 1))
        ones = jnp.where((side >= 3 * h) & (side < 3 * h + 3), 1.0, 0.0)
        dead = jnp.where((side == 3 * heads) & (key >= length), -1e30, ones).astype(bf16)
        kx[h] = jnp.concatenate([jnp.where(keep, scaled, zero), dead], axis=1)
        vx[h] = jnp.concatenate([jnp.where(keep, values, zero), ones.astype(bf16)], axis=1)
    grads[:, 0 : 2 * cols] = jnp.zeros((image_len, 2 * cols), bf16)
    grad_q[...] = jnp.zeros_like(grad_q)

    def key_block(index, carry):
        here = pl.ds(pl.multiple_of(index * block, block), block)
        parts = {}
        for h in range(heads):
            probs = jnp.exp(dot(kx[h, here, :], qx[...], NT))
            grad_probs = dot(vx[h, here, :], dox[...], NT)
            grad_scores = (probs * grad_probs).astype(bf16)
            pair = slice(0, 128) if h < 2 else slice(128, 256)
            own = slice(DH * (h % 2), DH * (h % 2) + DH)
            grad_v = dot(dot_t[pair, :], probs.astype(bf16), NT)[own]
            grad_k = dot(q_t[pair, :], grad_scores, NT)[own]
            parts[h] = (grad_k * 0.125, grad_v)
            grad_q[DH * h : DH * (h + 1), :] += dot(k_t[pair, here], grad_scores)[own]
        stack = [parts[h][j] for j in range(2) for h in range(heads)]
        grads[here, 0 : 2 * cols] = jnp.transpose(jnp.concatenate(stack, axis=0).astype(bf16))
        return carry

    lax.fori_loop(0, (length + block - 1) // block, key_block, 0)
    grads[:, 2 * cols : 3 * cols] = jnp.transpose(grad_q[...].astype(bf16))

    for load in loads:
        load.wait()
    gain, shift = vec_ref[0:1, :].astype(f32), vec_ref[1:2, :].astype(f32)
    step = 256
    sums = [jnp.zeros((1, 1), f32)] * 3
    if stage:
        sums = [old[1][0:1, :], old[1][1:2, :], old[2][0:1, :]]
    for start in range(0, image_len, step):
        here = slice(start, start + step)
        unit, _ = unit_rows(x[here, :].astype(f32))
        normed[here, :] = (unit * gain + shift).astype(bf16)
        part = grads[here, :]
        da = dot(part, w_all[...])
        da_s[here, :] = da.astype(bf16)
        more = [da * unit, da, part.astype(f32)]
        sums = [old_sum + jnp.sum(new, axis=0, keepdims=True) for old_sum, new in zip(sums, more)]
    me = lax.axis_index("tensor")
    core, side = me % 2, me // 2
    if stage == 0:
        half = image_len // 2
        spans = [(core * half, half), ((1 - core) * half, half)]
    elif stage == 1:
        half = image_len // 4
        far = (1 - side) * 2 * half
        spans = [(far + core * half, half), (far + (1 - core) * half, half), (side * 2 * half, 2 * half)]
    else:
        spans = [(0, image_len)]
    stores = []
    for index, (start, size) in enumerate(spans):
        source = da_s.at[pl.ds(pl.multiple_of(start, 256), size)] if size < image_len else da_s
        stores.append(pltpu.make_async_copy(source, outs[index], sems.at[4 + index]))
        stores[-1].start()
    fresh = dot(normed[...], grads[...], TN)
    if stage:
        fresh = fresh + dw[...]
    if stage == 2:
        fresh = fresh.astype(bf16)
        at = 0
        for order, target in zip(orders, dw_outs):
            piece = fresh[:, at : at + target.shape[1]]
            at += target.shape[1]
            target[...] = dot(halving_order(order, fresh.shape[0], dp_size), piece).astype(bf16)
    else:
        dw_outs[0][...] = fresh
    small_out[...] = jnp.concatenate([sums[0], sums[1], jnp.zeros((6, sums[0].shape[1]), f32)], axis=0)
    bias_out[...] = jnp.broadcast_to(sums[2], bias_out.shape)
    for store in stores:
        store.wait()


def image_back(stage, buckets, which, kvq, lse, o, grad_o, vectors, tokens, weight, dp_size, orders, old):
    rows, width = tokens.shape
    cols = o.shape[0]
    images = buckets.shape[0]
    image_len = rows // images
    heads = cols // DH
    half = image_len // 2
    da_rows = [[half, half], [half // 2, half // 2, half], [image_len]][stage]
    picked = lambda w: pl.BlockSpec((image_len, w), lambda i, b, s: (s[0], 0))
    across = lambda w: pl.BlockSpec((w, image_len), lambda i, b, s: (0, s[0]))
    fixed = lambda shape: pl.BlockSpec(shape, lambda i, b, s: (0,) * len(shape))
    if stage == 2:
        dw_shapes = [((width, n), bf16) for n in (256, 3 * cols - 256)]
    else:
        dw_shapes = [((width, 3 * cols), f32)]
    return pl.pallas_call(
        functools.partial(image_back_kernel, block=256, stage=stage, dp_size=dp_size, orders=orders),
        grid_spec=pltpu.PrefetchScalarGridSpec(
            num_scalar_prefetch=2,
            grid=(1,),
            in_specs=[picked(3 * cols), across(8), across(cols), across(cols), fixed(vectors.shape)]
            + [ANY] * 2
            + ([ANY, fixed((8, width)), fixed((8, 3 * cols))] if stage else []),
            out_specs=[ANY] * len(da_rows)
            + [fixed(shape) for shape, _ in dw_shapes]
            + [fixed((8, width)), fixed((8, 3 * cols))],
            scratch_shapes=[
                pltpu.VMEM((image_len, 256), bf16),
                pltpu.VMEM((256, image_len), bf16),
                pltpu.VMEM((image_len, 256), bf16),
                pltpu.VMEM((256, image_len), bf16),
                pltpu.VMEM((heads, image_len, 256), bf16),
                pltpu.VMEM((heads, image_len, 256), bf16),
                pltpu.VMEM((256, image_len), bf16),
                pltpu.VMEM((cols, image_len), f32),
                pltpu.VMEM((image_len, 3 * cols), bf16),
                pltpu.VMEM((image_len, width), bf16),
                pltpu.VMEM((3 * cols, width), bf16),
                pltpu.VMEM((image_len, width), bf16),
                pltpu.VMEM((image_len, width), bf16),
                pltpu.VMEM((width, 3 * cols), f32),
                pltpu.SemaphoreType.DMA((10,)),
            ],
        ),
        out_shape=[jax.ShapeDtypeStruct((n, width), bf16) for n in da_rows]
        + [
            *[jax.ShapeDtypeStruct(*shape) for shape in dw_shapes],
            jax.ShapeDtypeStruct((8, width), f32),
            jax.ShapeDtypeStruct((8, 3 * cols), f32),
        ],
        compiler_params=pltpu.CompilerParams(vmem_limit_bytes=VMEM),
        cost_estimate=cost(10**6, 10**4),
        name=f"image_back_{stage}",
    )(buckets, which, kvq, lse, o, grad_o, vectors, tokens, weight, *old)


def rows_kernel(*refs, parts, dp_size, orders):
    refs = list(refs)
    take = lambda count: [refs.pop(0) for _ in range(count)]
    x_any, g_any, vec_ref, bias_ref, o_in, g_t = take(6)
    wo_in, up_in, down_in = take(2), take(2), take(2)
    quarters = [take(5), take(5)]
    y_ref, e_ref, kept, sent, keep, away, small_ref, do_ref = *take(2), take(2), take(2), take(2), take(2), *take(2)
    x_ref, g_ref, wo_w, up_w, down_w, hidden, normed, mixed, back, c_t, z_s, du_s, grads, came, sems, core_sems = take(16)
    rows, width = x_ref.shape
    hid = up_w.shape[2]
    step_index = pl.program_id(0)
    part = step_index ^ 2
    dp, me = lax.axis_index("dp"), lax.axis_index("tensor")
    quarter = dp % 4
    here = pl.ds(pl.multiple_of(me * rows, rows), rows)
    inputs = [
        pltpu.make_async_copy(x_any.at[here], x_ref, sems.at[4, 0]),
        pltpu.make_async_copy(g_any.at[here], g_ref, sems.at[4, 1]),
    ]
    to_core = send(grads.at[3], came, core_sems, 0, (dp, me ^ 1))

    def loads(source, target, row, at):
        found = [[pltpu.make_async_copy(source[r], target.at[r], sems.at[row, r])] for r in range(2)]
        size = target.shape[1] // 4
        for r in (2, 3):
            found.append([])
            for i in range(4):
                piece, here = quarters[r - 2][i], at
                if i == 3 and at >= split:
                    piece, here = quarters[r - 2][4], at - split
                place = target.at[r, pl.ds(pl.multiple_of((quarter ^ i) * size, size), size)]
                index = 2 + 4 * (r - 2) + i
                found[r].append(pltpu.make_async_copy(piece.at[pl.ds(here, size)], place, sems.at[row, index]))
        return found

    mixed_cols = o_in.shape[1]
    split = (mixed_cols + hid) // 4
    wo_loads = loads(wo_in, wo_w, 0, 0)
    up_loads = loads(up_in, up_w, 1, mixed_cols // 4)
    down_loads = loads(down_in, down_w, 2, (mixed_cols + hid) // 4)
    gain, shift = vec_ref[2:3, :].astype(f32), vec_ref[3:4, :].astype(f32)

    def store(r):
        targets = away if r % 2 else keep
        return [
            pltpu.make_async_copy(grads.at[r, :, pl.ds(at * hid, hid)], target, sems.at[3, 2 * r + at])
            for at, target in enumerate(targets)
        ]

    def store_halves():
        half = width // 2
        return [
            pltpu.make_async_copy(
                grads.at[2, pl.ds(side * half, half), pl.ds(at * hid, hid)], group[at], sems.at[3, 4 + 2 * side + at]
            )
            for side, group in enumerate((kept, sent))
            for at in range(2)
        ]

    @pl.when(step_index == 0)
    def _():
        for load in inputs:
            load.start()
        for group in wo_loads + up_loads[2:] + down_loads[2:] + up_loads[:2] + down_loads[:2]:
            for load in group:
                load.start()
        greet([(dp, me ^ 1)])
        for group in wo_loads:
            for load in group:
                load.wait()
        attended = dot(o_in[0], wo_w[0], TN)
        for r in range(1, parts):
            attended += dot(o_in[r], wo_w[r], TN)
        for load in inputs:
            load.wait()
        h1 = x_ref[...].astype(f32) + attended + vec_ref[4:5, :].astype(f32)
        hidden[...] = h1
        unit, _ = unit_rows(h1)
        normed[...] = (unit * gain + shift).astype(bf16)
        c_t[...] = dot(halving_order(orders[1], width, dp_size), normed[...], NT).astype(bf16)
        mixed[...] = jnp.zeros_like(mixed)
        back[...] = jnp.zeros_like(back)
        small_ref[...] = jnp.zeros_like(small_ref)

    for r in range(parts):

        @pl.when(part == r)
        def _():
            for load in up_loads[r] + down_loads[r]:
                load.wait()

    step = 256
    chunks = [slice(s, s + step) for s in range(0, hid, step)]

    def first(cols):
        u = dot(normed[...], up_w[part, :, cols]) + bias_ref[part, 0:1, cols]
        return u, dot(g_ref[...], down_w[part, cols, :], NT)

    def bend(cols, u, dz):
        square = u * u
        scaled = u * GELU_SCALE
        gate = 0.5 + 0.5 * jnp.tanh(scaled * (1.0 + GELU_CUBE * square))
        z_s[:, cols] = (u * gate).astype(bf16)
        slope = gate + (2.0 * gate) * (1.0 - gate) * scaled * (1.0 + (3.0 * GELU_CUBE) * square)
        du = (dz * slope).astype(bf16)
        du_s[:, cols] = du
        small_ref[pl.ds(8 + part, 1), cols] = jnp.sum(du.astype(f32), axis=0, keepdims=True)

    def weigh(cols):
        grads[part, :, cols] = dot(g_t[...], z_s[:, cols]).astype(bf16)
        later = slice(hid + cols.start, hid + cols.stop)
        grads[part, :, later] = dot(c_t[...], du_s[:, cols]).astype(bf16)

    ready = first(chunks[0])
    for index, cols in enumerate(chunks):
        following = first(chunks[index + 1]) if index + 1 < len(chunks) else None
        bend(cols, *ready)
        if index:
            weigh(chunks[index - 1])
        ready = following
    mixed[...] += dot(z_s[...], down_w[part])
    weigh(chunks[-1])
    back[...] += dot(du_s[...], up_w[part], NT)
    for r in range(2):

        @pl.when(part == r)
        def _():
            for copy in store(r):
                copy.start()

    @pl.when(part == 3)
    def _():
        to_core.start()

    @pl.when(step_index == parts - 1)
    def _():
        to_core.wait()
        grads[2] = (grads[2].astype(f32) + came[...].astype(f32)).astype(bf16)
        for copy in store_halves():
            copy.start()
        h1 = hidden[...]
        y_ref[...] = (h1 + mixed[...] + vec_ref[5:6, :].astype(f32)).astype(bf16)
        unit, inverse = unit_rows(h1)
        dc = back[...]
        wide_g = g_ref[...].astype(f32)
        dh = wide_g + norm_back(dc, gain, unit, inverse)
        e = dh.astype(bf16)
        e_ref[...] = e
        for index, values in enumerate([dc * unit, dc, dh, wide_g]):
            small_ref[2 + index : 3 + index, :] = jnp.sum(values, axis=0, keepdims=True)
        for r in range(parts):
            do_ref[r] = dot(wo_w[r], e, NT).astype(bf16)
        for copy in store(0) + store(1) + store_halves():
            copy.wait()


def own_rows(x, g, vectors, up_bias, o_parts, g_turned, wo, up, down, quarters, dp_size, orders):
    parts, cols, rows = o_parts.shape
    width = x.shape[1]
    hid = up[0].shape[1]
    fixed = lambda shape: pl.BlockSpec(shape, lambda r: (0,) * len(shape))
    array = lambda *shape: jax.ShapeDtypeStruct(shape, bf16)
    out = pl.pallas_call(
        functools.partial(rows_kernel, parts=parts, dp_size=dp_size, orders=orders),
        grid=(parts,),
        in_specs=[
            ANY,
            ANY,
            fixed(vectors.shape),
            fixed(up_bias.shape),
            fixed(o_parts.shape),
            fixed(g_turned.shape),
        ]
        + [ANY] * 16,
        out_specs=[fixed((rows, width))] * 2 + [ANY] * 8 + [fixed((16, width)), fixed((parts, cols, rows))],
        out_shape=[array(rows, width)] * 2
        + [array(width // 2, hid)] * 4
        + [array(width, hid)] * 4
        + [jax.ShapeDtypeStruct((16, width), f32), array(parts, cols, rows)],
        scratch_shapes=[
            pltpu.VMEM((rows, width), bf16),
            pltpu.VMEM((rows, width), bf16),
            pltpu.VMEM((parts, cols, width), bf16),
            pltpu.VMEM((parts, width, hid), bf16),
            pltpu.VMEM((parts, hid, width), bf16),
            pltpu.VMEM((rows, width), f32),
            pltpu.VMEM((rows, width), bf16),
            pltpu.VMEM((rows, width), f32),
            pltpu.VMEM((rows, width), f32),
            pltpu.VMEM((width, rows), bf16),
            pltpu.VMEM((rows, hid), bf16),
            pltpu.VMEM((rows, hid), bf16),
            pltpu.VMEM((parts, width, 2 * hid), bf16),
            pltpu.VMEM((width, 2 * hid), bf16),
            pltpu.SemaphoreType.DMA((5, 12)),
            pltpu.SemaphoreType.DMA((2, 1)),
        ],
        compiler_params=pltpu.CompilerParams(collective_id=4, has_side_effects=True, vmem_limit_bytes=VMEM),
        cost_estimate=cost(12 * rows * width * hid * parts, 8 * parts * width * hid, rows * hid * parts),
        name="own_rows",
    )(x, g, vectors, up_bias, o_parts, g_turned, *wo, *up, *down, *quarters[0], *quarters[1])
    return out[0], out[1], out[2:4], out[4:6], out[6:8], out[8:10], out[10], out[11]


def greet(partners):
    barrier = pltpu.get_barrier_semaphore()
    for partner in partners:
        pl.semaphore_signal(barrier, inc=1, device_id=partner, device_id_type=pl.DeviceIdType.MESH)
    pl.semaphore_wait(barrier, len(partners))


def send(source, target, sems, index, partner):
    return pltpu.make_async_remote_copy(
        src_ref=source,
        dst_ref=target,
        send_sem=sems.at[0, index],
        recv_sem=sems.at[1, index],
        device_id=partner,
        device_id_type=pl.DeviceIdType.MESH,
    )


def out_kernel(*refs, parts, dp_size, order):
    refs = list(refs)
    take = lambda count: [refs.pop(0) for _ in range(count)]
    o_ref, bias_ref, g_any = take(3)
    shards, pieces = take(3), take(3)
    o_all, bias_all, g_t = take(3)
    shards_to, pieces_to, across, across_to = take(3), take(3), take(2), take(2)
    own_o, own_bias, g_own, sems, local = refs
    dp, me = lax.axis_index("dp"), lax.axis_index("tensor")
    rows = o_all.shape[2]
    partners = [(dp, me ^ r) for r in range(parts)]
    beside, along = (dp ^ 1, me), (dp ^ 2, me)
    greet(partners[1:] + [beside, along])
    copies = []

    def start(source, target, partner):
        copies.append(send(source, target, sems, len(copies), partner))
        copies[-1].start()

    split = across[0].shape[0]
    start(pieces[1].at[pl.ds(0, split)], across[0], along)
    start(pieces[2].at[pl.ds(split, across[1].shape[0])], across[1], beside)
    for r in range(parts - 1, 0, -1):
        source = o_ref.at[:, pl.ds(pl.multiple_of((me ^ r) * rows, rows), rows)]
        start(source, o_all.at[r], partners[r])
        start(bias_ref, bias_all.at[r], partners[r])
    for source, target in zip(shards + pieces, shards_to + pieces_to):
        start(source, target, partners[1])
    mine = o_ref.at[:, pl.ds(pl.multiple_of(me * rows, rows), rows)]
    g_here = g_any.at[pl.ds(pl.multiple_of(me * rows, rows), rows)]
    loads = [
        pltpu.make_async_copy(mine, own_o, local.at[0]),
        pltpu.make_async_copy(bias_ref, own_bias, local.at[1]),
        pltpu.make_async_copy(g_here, g_own, local.at[2]),
    ]
    for load in loads:
        load.start()
    for load in loads:
        load.wait()
    stores = [
        pltpu.make_async_copy(own_o, o_all.at[0], local.at[0]),
        pltpu.make_async_copy(own_bias, bias_all.at[0], local.at[1]),
    ]
    for store in stores:
        store.start()
    g_t[...] = dot(halving_order(order, g_own.shape[1], dp_size), g_own[...], NT).astype(bf16)
    for index in range(2):
        copies[index].wait_recv()
        start(across[index], across_to[index], partners[1])
    for index, copy in enumerate(copies):
        if index < 2:
            copy.wait_send()
        else:
            copy.wait()
    for store in stores:
        store.wait()


def exchange_out(o, bias, g, shards, pieces, parts, dp_size, order):
    cols, rows = o.shape
    split = pieces[0].shape[0] - shards[2].shape[0] // 4
    like = lambda x, count=None: jax.ShapeDtypeStruct((count or x.shape[0],) + x.shape[1:], x.dtype)
    halves = [like(pieces[0], split), like(pieces[0], pieces[0].shape[0] - split)]
    shapes = [
        jax.ShapeDtypeStruct((parts, cols, rows // parts), bf16),
        jax.ShapeDtypeStruct((parts,) + bias.shape, f32),
        jax.ShapeDtypeStruct((g.shape[1], rows // parts), bf16),
        *map(like, shards),
        *map(like, pieces),
        *halves,
        *halves,
    ]
    out = pl.pallas_call(
        functools.partial(out_kernel, parts=parts, dp_size=dp_size, order=order),
        in_specs=[ANY] * 9,
        out_specs=[ANY] * 2 + [pl.BlockSpec(memory_space=pltpu.VMEM)] + [ANY] * (len(shapes) - 3),
        out_shape=shapes,
        scratch_shapes=[
            pltpu.VMEM((cols, rows // parts), bf16),
            pltpu.VMEM(bias.shape, f32),
            pltpu.VMEM((rows // parts, g.shape[1]), bf16),
            pltpu.SemaphoreType.DMA((2, 18)),
            pltpu.SemaphoreType.DMA((3,)),
        ],
        compiler_params=pltpu.CompilerParams(collective_id=1, has_side_effects=True, vmem_limit_bytes=VMEM),
        cost_estimate=cost(15 * 10**9, 10**7),
        name="exchange_out",
    )(o, bias, g, *shards, *pieces)
    return out[0], out[1], out[2], out[3:6], out[6:9], out[9:11], out[11:13]


def back_kernel(do_all, *refs, parts, dp_size, orders):
    refs = list(refs)
    take = lambda count: [refs.pop(0) for _ in range(count)]
    e_ref, o_in = take(2)
    keeps, aways, far_kept, far_sent = take(2), take(2), take(2), take(2)
    (do_ref,) = take(1)
    kept, far_kept_to, sends, wo_refs = take(2), take(2), take(2), take(2)
    held, came, far_held, far_came = take(2), take(2), take(2), take(2)
    own_do, wo_made, wo_came, sems, local = refs
    dp, me = lax.axis_index("dp"), lax.axis_index("tensor")
    rows = do_all.shape[2]
    width = e_ref.shape[1]
    partners = [(dp, me ^ r) for r in range(parts)]
    along = [(dp ^ (1 << order[0]), me) for order in orders]
    greet(partners[1:] + along)
    mine = do_ref.at[:, pl.ds(pl.multiple_of(me * rows, rows), rows)]
    copies = [send(do_all.at[r], mine, sems, r - 1, partners[r]) for r in range(parts - 1, 0, -1)]
    cores = [send(aways[track], came[track], sems, 3 + track, partners[1]) for track in range(2)]
    fars = [send(far_sent[track], far_came[track], sems, 5 + track, along[track]) for track in range(2)]
    loads = [pltpu.make_async_copy(keeps[track], held[track], local.at[track]) for track in range(2)]
    far_loads = [pltpu.make_async_copy(far_kept[track], far_held[track], local.at[2 + track]) for track in range(2)]
    load = pltpu.make_async_copy(do_all.at[0], own_do, local.at[4])
    for copy in fars + copies + cores + loads + far_loads + [load]:
        copy.start()
    load.wait()
    store = pltpu.make_async_copy(own_do, mine, local.at[4])
    store.start()
    e_t = dot(halving_order(orders[0], width, dp_size), e_ref[...], NT).astype(bf16)
    blank = jnp.zeros((width, 256 - o_in.shape[1]), bf16)
    for r in range(parts):
        wo_made[r % 2, r // 2] = jnp.concatenate([dot(e_t, o_in[r], NT).astype(bf16), blank], axis=1)
    wo_copy = send(wo_made.at[1], wo_came, sems, 7, partners[1])
    wo_copy.start()
    stores = [store]

    def put(total, buffer, targets, number):
        half = buffer.shape[0] // 2
        buffer[...] = total.astype(bf16)
        for side, target in enumerate(targets):
            stores.append(pltpu.make_async_copy(buffer.at[pl.ds(side * half, half)], target, local.at[number + side]))
            stores[-1].start()

    for track in range(2):
        cores[track].wait()
        loads[track].wait()
        total = held[track][...].astype(f32) + came[track][...].astype(f32)
        put(total, held[track], (kept[track], sends[track].at[pl.ds(0, width // 2)]), 5 + 2 * track)
    wo_copy.wait()
    for index, target in enumerate(wo_refs):
        target[...] = (wo_made[0, index].astype(f32) + wo_came[index].astype(f32)).astype(bf16)
    for track in range(2):
        fars[track].wait()
        far_loads[track].wait()
        total = far_held[track][...].astype(f32) + far_came[track][...].astype(f32)
        target = sends[1 - track].at[pl.ds(width // 2, width // 4)]
        put(total, far_held[track], (far_kept_to[track], target), 9 + 2 * track)
    for copy in copies + stores:
        copy.wait()


def exchange_back(do_parts, e, o_parts, keeps, aways, far_kept, far_sent, dp_size, orders):
    parts, cols, rows = do_parts.shape
    width = e.shape[1]
    array = lambda *shape: jax.ShapeDtypeStruct(shape, bf16)
    hid = keeps[0].shape[1]
    shapes = [array(cols, parts * rows)] + [array(width // 2, hid)] * 2 + [array(width // 4, hid)] * 2
    shapes += [array(width // 2 + width // 4, hid)] * 2 + [array(width, 256)] * 2
    buffer = lambda x: pltpu.VMEM(x.shape, bf16)
    vmem = pl.BlockSpec(memory_space=pltpu.VMEM)
    out = pl.pallas_call(
        functools.partial(back_kernel, parts=parts, dp_size=dp_size, orders=orders),
        in_specs=[ANY, vmem, vmem] + [ANY] * 8,
        out_specs=[ANY] * 7 + [vmem] * 2,
        out_shape=shapes,
        scratch_shapes=[*map(buffer, keeps), *map(buffer, keeps), *map(buffer, far_kept), *map(buffer, far_kept)]
        + [
            pltpu.VMEM((cols, rows), bf16),
            pltpu.VMEM((2, 2, width, 256), bf16),
            pltpu.VMEM((2, width, 256), bf16),
            pltpu.SemaphoreType.DMA((2, 8)),
            pltpu.SemaphoreType.DMA((13,)),
        ],
        compiler_params=pltpu.CompilerParams(collective_id=2, has_side_effects=True, vmem_limit_bytes=VMEM),
        cost_estimate=cost(15 * 10**9, 10**7),
        name="exchange_back",
    )(do_parts, e, o_parts, *keeps, *aways, *far_kept, *far_sent)
    return out[0], out[1:3], out[3:5], out[5:7], out[7:9]


def pick_kernel(*refs):
    *sources, target, sems = refs
    quarter = lax.axis_index("dp") % 4
    copies, at = [], 0
    for index, source in enumerate(sources):
        size = source.shape[0] // 4
        piece = source.at[pl.ds(pl.multiple_of(quarter * size, size), size)]
        copies.append(pltpu.make_async_copy(piece, target.at[pl.ds(at, size)], sems.at[index]))
        copies[index].start()
        at += size
    for copy in copies:
        copy.wait()


def pick_quarter(shards):
    rows = sum(shard.shape[0] for shard in shards) // 4
    return pl.pallas_call(
        pick_kernel,
        in_specs=[ANY] * len(shards),
        out_specs=pl.BlockSpec(memory_space=pltpu.VMEM),
        out_shape=jax.ShapeDtypeStruct((rows, shards[0].shape[1]), bf16),
        scratch_shapes=[pltpu.SemaphoreType.DMA((len(shards),))],
        name="pick_quarter",
    )(*shards)


def finish_kernel(
    own_any, mid_any, far_own_any, mid_keep_any, mid_came_any, x_any, dh_any, vec_ref, late_ref, bias_ref, early_ref, *refs,
    dp_size, tracks,
):
    bits = dp_size.bit_length() - 1
    refs = list(refs)
    take = lambda count: [refs.pop(0) for _ in range(count)]
    weights = [take(1), take(1), take(2), take(2), take(2)]
    (out_ref,) = take(1)
    weights_out = take(len(tracks))
    (sums_out,) = take(1)
    held, other, far_own, mid_keep, mid_came, far_mid, x_v, dh_v = take(8)
    sent = [take(len(order)) for order in tracks]
    got = [take(len(order)) for order in tracks]
    totals = take(len(tracks))
    sums, got_s, sems, w_sems, local = refs
    dp, me = lax.axis_index("dp"), lax.axis_index("tensor")
    core, side = me % 2, me // 2
    rows, width = out_ref.shape
    image_len = own_any.shape[0]
    half = image_len // 2
    x_own = x_any.at[pl.ds(pl.multiple_of(me * rows, rows), rows)]
    at_own = side * half
    at_mid = (1 - side) * image_len
    across = [(dp, me ^ 1), (dp, me ^ 2)]
    along = [(dp ^ (1 << bit), me) for bit in range(bits)]
    greet(across + along)

    loads = [
        pltpu.make_async_copy(own_any, held.at[pl.ds(pl.multiple_of(at_own, half), image_len)], local.at[0]),
        pltpu.make_async_copy(mid_any, held.at[pl.ds(pl.multiple_of(at_mid, half), half)], local.at[1]),
        pltpu.make_async_copy(far_own_any, far_own, local.at[2]),
        pltpu.make_async_copy(mid_keep_any, mid_keep, local.at[3]),
        pltpu.make_async_copy(mid_came_any, mid_came, local.at[6]),
        pltpu.make_async_copy(x_own, x_v, local.at[4]),
        pltpu.make_async_copy(dh_any, dh_v, local.at[5]),
    ]
    for load in loads:
        load.start()
    mid_load = loads.pop(4)
    mid_load.wait()
    loads[3].wait()
    mid_keep[...] = (mid_keep[...].astype(f32) + mid_came[...].astype(f32)).astype(bf16)

    copies = [[] for _ in tracks]
    tall = [totals[track].shape[0] for track in range(len(tracks))]

    def first(track, here):
        terms = [term[here, :].astype(f32) for term in weights[track]]
        return terms[0] + terms[1] if len(terms) > 1 else terms[0]

    def send_weight(track, step):
        target = sent[track][step]
        span = tall[track] // 2
        if step == 0:
            target[...] = first(track, slice(span, 2 * span)).astype(target.dtype)
        else:
            target[...] = totals[track][span : 2 * span, :].astype(target.dtype)
        route = along[tracks[track][step]]
        index = sum(len(order) for order in tracks[:track]) + step
        copies[track].append(send(target, got[track][step], w_sems, index, route))
        copies[track][step].start()

    def add_weight(track, step):
        copies[track][step].wait()
        tall[track] //= 2
        span = tall[track]
        kept = totals[track][0:span, :] if step else first(track, slice(0, span))
        totals[track][0:span, :] = kept + got[track][step][...].astype(f32)

    for track in range(len(tracks)):
        if tracks[track]:
            send_weight(track, 0)
    mid_copy = send(mid_keep, far_mid, sems, 14, across[1])

    sums[...] = early_ref[...]
    sums[0:2, :] = late_ref[0:2, :]
    sums[12:13, 0 : bias_ref.shape[1]] = bias_ref[0:1, :]
    routes = across + along
    s_copies = []

    def send_sums(step):
        s_copies.append(send(sums, got_s.at[step], sems, step, routes[step]))
        s_copies[step].start()

    def add_sums(step):
        s_copies[step].wait()
        if step < 2:
            sums[0:6, :] += got_s[step, 0:6, :]
            new = [sums[8 + r : 9 + r, :] + got_s[step, 8 + (r ^ (1 << step)) : 9 + (r ^ (1 << step)), :] for r in range(4)]
            for r in range(4):
                sums[8 + r : 9 + r, :] = new[r]
        else:
            sums[...] += got_s[step]

    def turn(track, step):
        add_weight(track, step)
        if step + 1 < len(tracks[track]):
            send_weight(track, step + 1)

    mid_copy.start()
    send_sums(0)
    for load in loads[:3]:
        load.wait()
    here = pl.ds(pl.multiple_of(at_own + core * half, half), half)
    held[here, :] = (held[here, :].astype(f32) + far_own[...].astype(f32)).astype(bf16)
    turn(0, 0)
    add_sums(0)
    send_sums(1)
    turn(1, 0)
    turn(2, 0)
    add_sums(1)
    send_sums(2)
    turn(0, 1)
    mid_copy.wait()

    here = pl.ds(pl.multiple_of(at_mid + core * (half // 2), half // 2), half // 2)
    held[here, :] = (held[here, :].astype(f32) + far_mid[...].astype(f32)).astype(bf16)
    theirs = held.at[pl.ds(pl.multiple_of((1 - core) * rows, rows), rows)]
    da_copy = send(theirs, other, sems, 15, across[0])
    da_copy.start()
    turn(1, 1)
    turn(2, 1)
    add_sums(2)
    if bits > 1:
        send_sums(3)
    for load in loads[4:]:
        load.wait()
    da_copy.wait()
    gain = vec_ref[0:1, :].astype(f32)
    step = 256
    for start in range(0, rows, step):
        piece = slice(start, start + step)
        unit, inverse = unit_rows(x_v[piece, :].astype(f32))
        mine = held[pl.ds(pl.multiple_of(core * rows + start, step), step), :].astype(f32)
        da = mine + other[piece, :].astype(f32)
        out_ref[piece, :] = (dh_v[piece, :].astype(f32) + norm_back(da, gain, unit, inverse)).astype(bf16)

    for step in range(2, bits):
        for track in range(3):
            turn(track, step)
        add_sums(1 + step)
        if step < bits:
            send_sums(2 + step)
    add_sums(1 + bits)
    for step in range(bits):
        for track in (3, 4):
            if step < len(tracks[track]):
                turn(track, step)
    for track in range(len(tracks)):
        if tracks[track]:
            weights_out[track][...] = totals[track][0 : weights_out[track].shape[0], :]
        else:
            weights_out[track][...] = first(track, slice(None))
    sums_out[...] = sums[...]


def unpack_kernel(out_ref, dw_one, dw_two, wo_in, down_ref, up_ref, sums_ref, out_to, qkv_to, wo_to, down_to, up_to, bias_to):
    out_to[...] = out_ref[...]
    down_to[...] = down_ref[...]
    up_to[...] = up_ref[...]
    cols = wo_to.shape[0]
    dw_ref = jnp.concatenate([dw_one[...], dw_two[...]], axis=1)
    for index, at in enumerate((2, 0, 1)):
        qkv_to[index] = dw_ref[:, at * cols : (at + 1) * cols]
    wo_to[...] = jnp.transpose(wo_in[...])[0:cols]
    for index, at in enumerate((2, 1)):
        bias_to[index : index + 1, :] = sums_ref[12:13, at * cols : (at + 1) * cols]


def unpack(out, dw_one, dw_two, wo, down, up, sums, cols):
    rows = dw_one.shape[0]
    vmem = pl.BlockSpec(memory_space=pltpu.VMEM)
    array = lambda *shape: jax.ShapeDtypeStruct(shape, f32)
    return pl.pallas_call(
        unpack_kernel,
        in_specs=[vmem] * 7,
        out_specs=[vmem] * 6,
        out_shape=[
            jax.ShapeDtypeStruct(out.shape, bf16),
            array(3, rows, cols),
            array(cols, rows),
            array(*down.shape),
            array(*up.shape),
            array(2, cols),
        ],
        compiler_params=pltpu.CompilerParams(vmem_limit_bytes=VMEM),
        name="unpack",
    )(out, dw_one, dw_two, wo, down, up, sums)


def finish(own, mid, far_own, mid_keep, mid_came, x, dh, vectors, late, bias, early, weights, tracks, dp_size):
    rows, width = dh.shape
    bits = dp_size.bit_length() - 1
    buffers, totals = [], []
    for group, order in zip(weights, tracks):
        tall, wide = group[0].shape[-2:]
        totals.append(pltpu.VMEM((tall, wide), f32))
        for bit in order:
            tall //= 2
            buffers.append(pltpu.VMEM((tall, wide), bf16 if tall % 16 == 0 else f32))
    count = sum(len(order) for order in tracks)
    flat = [weight for group in weights for weight in group]
    vmem = pl.BlockSpec(memory_space=pltpu.VMEM)
    return pl.pallas_call(
        functools.partial(finish_kernel, dp_size=dp_size, tracks=tracks),
        in_specs=[ANY] * 7 + [vmem] * (4 + len(flat)),
        out_specs=[vmem] * (2 + len(tracks)),
        out_shape=[jax.ShapeDtypeStruct((rows, width), bf16)]
        + [jax.ShapeDtypeStruct((width // dp_size, group[0].shape[-1]), f32) for group in weights]
        + [jax.ShapeDtypeStruct((16, width), f32)],
        scratch_shapes=[
            pltpu.VMEM((2 * rows, width), bf16),
            pltpu.VMEM((rows, width), bf16),
            pltpu.VMEM(far_own.shape, bf16),
            pltpu.VMEM(mid_keep.shape, bf16),
            pltpu.VMEM(mid_keep.shape, bf16),
            pltpu.VMEM(mid_keep.shape, bf16),
            pltpu.VMEM((rows, width), bf16),
            pltpu.VMEM((rows, width), bf16),
        ]
        + buffers * 2
        + totals
        + [
            pltpu.VMEM((16, width), f32),
            pltpu.VMEM((2 + bits, 16, width), f32),
            pltpu.SemaphoreType.DMA((2, 16)),
            pltpu.SemaphoreType.DMA((2, count)),
            pltpu.SemaphoreType.DMA((7,)),
        ],
        compiler_params=pltpu.CompilerParams(
            collective_id=3, has_side_effects=True, vmem_limit_bytes=VMEM
        ),
        name="finish",
    )(own, mid, far_own, mid_keep, mid_came, x, dh, vectors, late, bias, early, *flat)


def on_device(
    dp_size, tokens, buckets, norm1_gain, norm1_bias, qkv_weight, qkv_bias, out_weight, out_bias,
    norm2_gain, norm2_bias, up_weight, up_bias, down_weight, down_bias, cotangent,
):
    parts = 4
    dp_bits = dp_size.bit_length() - 1
    me = lax.axis_index("tensor")
    token_rows, width = tokens.shape
    share = token_rows // parts
    hid = up_weight.shape[1]
    cols = qkv_weight.shape[2]

    def over_tensor(values, mask):
        return lax.ppermute(values, "tensor", [(i, i ^ mask) for i in range(parts)])

    def over_dp(values, mask):
        return lax.ppermute(values, "dp", [(i, i ^ mask) for i in range(dp_size)])

    def add(*terms):
        total = terms[0].astype(f32)
        for term in terms[1:]:
            total = total + term.astype(f32)
        return total.astype(bf16)

    shards = (out_weight, up_weight, down_weight)
    near = over_tensor(pick_quarter(shards), 2)
    blank = jnp.zeros_like(norm1_gain)
    vectors = jnp.stack(
        [norm1_gain, norm1_bias, norm2_gain, norm2_bias, out_bias, down_bias, blank, blank]
    )
    up_bias_rows = jnp.broadcast_to(up_bias.astype(f32)[None], (8, hid))
    orders = [list(range(dp_bits)), [1, 0] + list(range(2, dp_bits))]
    turned_weight = jnp.swapaxes(qkv_weight, 1, 2)
    kvq, bound = project(tokens, vectors, turned_weight, qkv_bias)
    near, kvq = lax.optimization_barrier((near, kvq))
    beside, along = over_dp(near, 1), over_dp(near, 2)
    o, lse = attend(buckets, kvq, bound)
    near, beside, along, o = lax.optimization_barrier((near, beside, along, o))
    mine = [near, beside, along]
    o_parts, bias_parts, g_turned, shards_to, other, across, across_to = exchange_out(
        o, up_bias_rows, cotangent, shards, mine, parts, dp_size, orders[0]
    )
    wo, up, down = zip(shards, shards_to)
    quarters = [[*mine, *across], [*other, *across_to]]
    layer_out, e, far_kept, far_sent, keeps, aways, early, do_parts = own_rows(
        tokens, cotangent, vectors, bias_parts, o_parts, g_turned, wo, up, down, quarters, dp_size, orders
    )
    grad_o, kept, far_kept, sends, grad_wo = exchange_back(
        do_parts, e, o_parts, keeps, aways, far_kept, far_sent, dp_size, orders
    )

    tie = lax.optimization_barrier
    got = [over_dp(both, 1 << order[0]) for both, order in zip(sends, orders)]
    wo_far = over_tensor(grad_wo[1], 2)

    side = me // 2
    order = [2 - 2 * side, jnp.ones_like(side), 2 * side]
    run = lambda stage, old, o: image_back(
        stage, buckets, order[stage].reshape(1).astype(jnp.int32), kvq, lse, o, grad_o, vectors, tokens, turned_weight,
        dp_size, orders, old,
    )
    da_keep, da_send, *old = run(0, [], o)
    came, first_keep = over_tensor(da_send, 1), da_keep
    *got, o = tie((*got, o, *old))[:3]
    split = width // 2
    crossed = over_tensor(jnp.stack([add(k, g[split:]) for k, g in zip(far_kept, got[::-1])]), 2)
    got = [g[:split] for g in got]
    split //= 2
    sent = [add(k[split:], g[split:]) for k, g in zip(kept, got)]
    kept = [add(k[:split], g[:split]) for k, g in zip(kept, got)]
    got = [over_dp(half, 1 << order[1]) for half, order in zip(sent, orders)]
    mid_keep, da_send, mid, *old = run(1, old, o)
    came, o, crossed, *got = tie((came, o, crossed, *got, *old))[:5]
    far_own = over_tensor(add(first_keep, came), 2)
    mid_came = over_tensor(da_send, 1)
    split //= 2
    terms = list(zip(kept, got, crossed))
    sent = jnp.stack([add(*[t[split:] for t in group]) for group in terms])
    kept = [add(*[t[:split] for t in group]) for group in terms]
    got = over_dp(sent, 1 << orders[0][2])
    own, *dw, late, bias_sums = run(2, old, o)
    got, far_own, mid_came, own, wo_far = tie((got, far_own, mid_came, own, wo_far))
    weights = [dw[:1], dw[1:], [grad_wo[0], wo_far]] + [[k, g] for k, g in zip(kept, got)]
    tracks = [orders[0], orders[1], orders[0], orders[0][3:], orders[1][3:]]
    out, dw_one, dw_two, wo_out, down_out, grad_up, sums = finish(
        own, mid, far_own, mid_keep, mid_came, tokens, e, vectors, late, bias_sums, early, weights, tracks, dp_size
    )
    input_grad, grad_qkv_weight, grad_out, down_out, grad_up, grad_qkv_bias = unpack(
        out, dw_one, dw_two, wo_out, down_out, grad_up, sums, cols
    )
    grad_down = down_out.T
    return (
        layer_out,
        input_grad,
        sums[0],
        sums[1],
        grad_qkv_weight,
        grad_qkv_bias,
        grad_out,
        sums[4],
        sums[2],
        sums[3],
        grad_up,
        sums[8],
        grad_down,
        sums[5],
    )


def solution(mesh):
    return jax.shard_map(
        functools.partial(on_device, mesh.shape["dp"]),
        mesh=mesh,
        in_specs=(
            P("dp", None),
            P("dp"),
            P(),
            P(),
            P(None, None, "tensor"),
            P(None, "tensor"),
            P("tensor", None),
            P(),
            P(),
            P(),
            P(None, "tensor"),
            P("tensor"),
            P("tensor", None),
            P(),
            P("dp", None),
        ),
        out_specs=(
            P(("dp", "tensor"), None),
            P(("dp", "tensor"), None),
            P(),
            P(),
            P(None, "dp", "tensor"),
            P(None, "tensor"),
            P("tensor", "dp"),
            P(),
            P(),
            P(),
            P("dp", "tensor"),
            P("tensor"),
            P("tensor", "dp"),
            P(),
        ),
        check_vma=False,
    )
```

```python
import functools

import jax
import jax.numpy as jnp
from jax import lax
from jax.experimental import pallas as pl
from jax.experimental.pallas import tpu as pltpu
from jax.sharding import PartitionSpec as P

DH = 64
NORM_EPSILON = 1e-06
GRID_SIXTEENTHS = (16, 15, 15, 12, 12, 8, 8, 6, 6)
GELU_SCALE = 0.7978845608028654
GELU_CUBE = 0.044715
VMEM = 60 << 20
NN = (((1,), (0,)), ((), ()))
NT = (((1,), (1,)), ((), ()))
TN = (((0,), (0,)), ((), ()))
bf16 = jnp.bfloat16
f32 = jnp.float32
ANY = pl.BlockSpec(memory_space=pl.ANY)


def dot(left, right, dims=NN):
    return lax.dot_general(left, right, dims, preferred_element_type=f32)


def lanes(rows, width):
    return lax.broadcasted_iota(jnp.int32, (rows, width), 1)


def live_lengths(image_len):
    return sorted({image_len * s // 16 for s in GRID_SIXTEENTHS})


def live_length(bucket, image_len):
    length = jnp.int32(0)
    for index, sixteenths in enumerate(GRID_SIXTEENTHS):
        length = jnp.where(bucket == index, image_len * sixteenths // 16, length)
    return length


def cost(flops, nbytes, transcendentals=0):
    return pl.CostEstimate(flops=flops, bytes_accessed=nbytes, transcendentals=transcendentals)


def split3(values):
    high = values.astype(bf16).astype(f32)
    middle = (values - high).astype(bf16).astype(f32)
    return high, middle, values - high - middle


def halving_order(order, width, dp_size):
    bits = dp_size.bit_length() - 1
    size = width // dp_size
    place = lax.broadcasted_iota(jnp.int32, (width, 128), 0)
    block = jnp.zeros_like(place)
    for index in range(1, dp_size):
        block = block + (place >= index * size).astype(jnp.int32)
    turned = jnp.zeros_like(block)
    for step, bit in enumerate(order):
        turned = turned | (((block >> (bits - 1 - step)) & 1) << bit)
    source = (turned ^ lax.axis_index("dp")) * size + (place - block * size)
    lane = lanes(width, 128)
    return jnp.concatenate(
        [jnp.where(source == lane + start, 1.0, 0.0).astype(bf16) for start in range(0, width, 128)], axis=1
    )


def unit_rows(values):
    centred = values - jnp.mean(values, axis=-1, keepdims=True)
    spread = jnp.mean(centred * centred, axis=-1, keepdims=True)
    inverse = lax.rsqrt(spread + NORM_EPSILON)
    return centred * inverse, inverse


def norm_back(grad, gain, unit, inverse):
    scaled = grad * gain
    mean_one = jnp.mean(scaled, axis=-1, keepdims=True)
    mean_two = jnp.mean(scaled * unit, axis=-1, keepdims=True)
    return inverse * (scaled - mean_one - unit * mean_two)


def project_kernel(x_ref, vec_ref, w_ref, bias_ref, out_ref, bound_ref, w_all):
    cols = w_ref.shape[1]

    @pl.when(pl.program_id(0) == 0)
    def _():
        for index, source in enumerate((1, 2, 0)):
            w_all[index * cols : (index + 1) * cols, :] = w_ref[source]

    gain, shift = vec_ref[0:1, :].astype(f32), vec_ref[1:2, :].astype(f32)
    bias = bias_ref[...].astype(f32)
    bias = jnp.concatenate([jnp.zeros((1, cols), f32), bias[1:2], bias[0:1]], axis=1)
    rows, step = x_ref.shape[0], 128
    row = lax.broadcasted_iota(jnp.int32, (3 * cols, 128), 0)
    pick = jnp.where(row // DH == lanes(3 * cols, 128), 1.0, 0.0).astype(bf16)

    def normed(start):
        unit, _ = unit_rows(x_ref[start : start + step, :].astype(f32))
        return (unit * gain + shift).astype(bf16)

    largest = None
    ready = normed(0)
    for start in range(0, rows, step):
        following = normed(start + step) if start + step < rows else None
        values = (dot(ready, w_all[...], NT) + bias).astype(bf16)
        out_ref[start : start + step, :] = values
        squares = jnp.max(dot(values * values, pick), axis=0, keepdims=True)
        largest = squares if largest is None else jnp.maximum(largest, squares)
        ready = following
    bound_ref[0] = jnp.broadcast_to(largest, (8, 128))


def project(tokens, vectors, weight, bias):
    rows, width = tokens.shape
    cols = weight.shape[1]
    block = 512
    fixed = lambda shape: pl.BlockSpec(shape, lambda i: (0,) * len(shape))
    return pl.pallas_call(
        project_kernel,
        grid=(rows // block,),
        in_specs=[
            pl.BlockSpec((block, width), lambda i: (i, 0)),
            fixed(vectors.shape),
            fixed(weight.shape),
            fixed(bias.shape),
        ],
        out_specs=[
            pl.BlockSpec((block, 3 * cols), lambda i: (i, 0)),
            pl.BlockSpec((1, 8, 128), lambda i: (i, 0, 0)),
        ],
        out_shape=[
            jax.ShapeDtypeStruct((rows, 3 * cols), bf16),
            jax.ShapeDtypeStruct((rows // block, 8, 128), f32),
        ],
        scratch_shapes=[pltpu.VMEM((3 * cols, width), bf16)],
        compiler_params=pltpu.CompilerParams(vmem_limit_bytes=VMEM),
        cost_estimate=cost(6 * rows * width * cols, 2 * rows * (width + 3 * cols)),
        name="project",
    )(tokens, vectors, weight, bias)


def attend_kernel(bucket_ref, kvq_ref, bound_ref, o_ref, lse_ref, kx, vt, *, block):
    cols, image_len = o_ref.shape
    heads = cols // DH
    at_q = 2 * cols
    length = live_length(bucket_ref[pl.program_id(0)], image_len)
    squares = jnp.max(bound_ref[...], axis=0)
    lane = lanes(8, 128)
    largest_key = jnp.max(jnp.where(lane < heads, squares, 0.0))
    of_query = (lane >= 2 * heads) & (lane < 3 * heads)
    largest_query = jnp.max(jnp.where(of_query, squares, 0.0))
    small = largest_key * largest_query <= (8.0 * 60.0) ** 2

    def run(live, subtract):
        scaled = kvq_ref[0:live, 0:192] * jnp.asarray(0.125, bf16)
        flipped = jnp.transpose(kvq_ref[0:live, 128:384])
        lane = lanes(live, 128)
        for h in range(heads):
            if h < 2:
                keep = (lane < DH) if h == 0 else (lane >= DH)
                kx[h, 0:live, :] = jnp.where(keep, scaled[:, 0:128], jnp.zeros((), bf16))
            else:
                kx[h, 0:live, 0:DH] = scaled[:, 128:192]
            vt[h, 0:DH, 0:live] = flipped[DH * (h + 1) : DH * (h + 2)]
            vt[h, DH:128, 0:live] = jnp.ones((DH, live), bf16)

        def scores(h, start):
            here = slice(start, start + block)
            if h < 2:
                return dot(kx[h, 0:live, :], kvq_ref[here, at_q : at_q + 128], NT)
            return dot(kx[h, 0:live, 0:DH], kvq_ref[here, at_q + 128 : at_q + 192], NT)

        parts = {}

        def finish(h, start, score):
            offset = 0.0
            if subtract:
                key = lax.broadcasted_iota(jnp.int32, score.shape, 0)
                score = jnp.where(key < length, score, -1e30)
                offset = jnp.max(score, axis=0, keepdims=True)
                score = score - offset
            mixed = dot(vt[h, :, 0:live], jnp.exp(score).astype(bf16))
            total = mixed[DH : DH + 1]
            here = slice(start, start + block)
            parts[h] = -(offset + jnp.log(total))
            o_ref[DH * h : DH * (h + 1), here] = (mixed[:DH] * (1.0 / total)).astype(bf16)
            if h == heads - 1:
                rows = [parts[i] for i in range(heads)]
                lse_ref[:, here] = jnp.concatenate(rows + [jnp.zeros((8 - heads, block), f32)], axis=0)

        items = [(h, s) for s in range(0, image_len, block) for h in range(heads)]
        score = scores(*items[0])
        for index, item in enumerate(items):
            following = scores(*items[index + 1]) if index + 1 < len(items) else None
            finish(*item, score)
            score = following

    for live in live_lengths(image_len):
        pl.when(small & (length == live))(functools.partial(run, live, False))
    pl.when(jnp.logical_not(small))(functools.partial(run, image_len, True))


def attend(buckets, kvq, bound):
    rows = kvq.shape[0]
    cols = kvq.shape[1] // 3
    images = buckets.shape[0]
    image_len = rows // images
    heads = cols // DH
    by_rows = lambda w: pl.BlockSpec((image_len, w), lambda i, b: (i, 0))
    by_cols = lambda w: pl.BlockSpec((w, image_len), lambda i, b: (0, i))
    return pl.pallas_call(
        functools.partial(attend_kernel, block=512),
        grid_spec=pltpu.PrefetchScalarGridSpec(
            num_scalar_prefetch=1,
            grid=(images,),
            in_specs=[by_rows(3 * cols), pl.BlockSpec(bound.shape, lambda i, b: (0, 0, 0))],
            out_specs=[by_cols(cols), by_cols(8)],
            scratch_shapes=[
                pltpu.VMEM((heads, image_len, 128), bf16),
                pltpu.VMEM((heads, 128, image_len), bf16),
            ],
        ),
        out_shape=[
            jax.ShapeDtypeStruct((cols, rows), bf16),
            jax.ShapeDtypeStruct((8, rows), f32),
        ],
        compiler_params=pltpu.CompilerParams(vmem_limit_bytes=VMEM),
        cost_estimate=cost(16 * rows * image_len * cols, 12 * rows * cols, rows * image_len * heads),
        name="attend",
    )(buckets, kvq, bound)


def image_back_kernel(bucket_ref, which_ref, kvq_ref, lse_ref, o_ref, do_ref, vec_ref, *refs, block, stage, dp_size, orders):
    refs = list(refs)
    take = lambda count: [refs.pop(0) for _ in range(count)]
    x_any, w_any = take(2)
    old = take(3) if stage else None
    outs = take((2, 3, 1)[stage])
    dw_outs = take(2 if stage == 2 else 1)
    small_out, bias_out = take(2)
    dox, dot_t, qx, q_t, kx, vx, k_t, grad_q, grads, x, w_all, da_s, normed, dw, sems = take(15)
    cols, image_len = o_ref.shape
    heads = cols // DH
    image = which_ref[0]
    loads = [
        pltpu.make_async_copy(x_any.at[pl.ds(image * image_len, image_len)], x, sems.at[0]),
    ]
    for index, source in enumerate((1, 2, 0)):
        target = w_all.at[pl.ds(index * cols, cols)]
        loads.append(pltpu.make_async_copy(w_any.at[source], target, sems.at[7 + index]))
    if stage:
        loads.append(pltpu.make_async_copy(old[0], dw, sems.at[3]))
    for load in loads:
        load.start()
    length = live_length(bucket_ref[image], image_len)
    inner = []
    for h in range(heads):
        own = slice(DH * h, DH * (h + 1))
        product = do_ref[own, :].astype(f32) * o_ref[own, :].astype(f32)
        inner += list(split3(-jnp.sum(product, axis=0, keepdims=True)))
    blank = [jnp.zeros((DH - 3 * heads, image_len), f32)]
    dot_t[0:cols, :] = do_ref[...]
    dot_t[cols:, :] = jnp.concatenate(inner + blank, axis=0).astype(bf16)
    dox[...] = jnp.transpose(dot_t[...])
    outer = [part for h in range(heads) for part in split3(lse_ref[h : h + 1, :])]
    row = lax.broadcasted_iota(jnp.int32, (DH - 3 * heads, image_len), 0)
    outer = jnp.concatenate(outer + [jnp.where(row == 0, 1.0, 0.0)], axis=0).astype(bf16)
    q = kvq_ref[:, 2 * cols : 3 * cols]
    q_t[0:cols, :] = jnp.transpose(q)
    q_t[cols:, :] = outer
    qx[...] = jnp.concatenate([q, jnp.transpose(outer)], axis=1)
    scaled = kvq_ref[:, 0:cols] * jnp.asarray(0.125, bf16)
    values = kvq_ref[:, cols : 2 * cols]
    k_t[0:cols, :] = jnp.transpose(scaled)
    lane, side = lanes(image_len, cols), lanes(image_len, DH)
    key = lax.broadcasted_iota(jnp.int32, (image_len, DH), 0)
    zero = jnp.zeros((), bf16)
    for h in range(heads):
        keep = (lane >= DH * h) & (lane < DH * (h + 1))
        ones = jnp.where((side >= 3 * h) & (side < 3 * h + 3), 1.0, 0.0)
        dead = jnp.where((side == 3 * heads) & (key >= length), -1e30, ones).astype(bf16)
        kx[h] = jnp.concatenate([jnp.where(keep, scaled, zero), dead], axis=1)
        vx[h] = jnp.concatenate([jnp.where(keep, values, zero), ones.astype(bf16)], axis=1)
    grads[:, 0 : 2 * cols] = jnp.zeros((image_len, 2 * cols), bf16)
    grad_q[...] = jnp.zeros_like(grad_q)

    def key_block(index, carry):
        here = pl.ds(pl.multiple_of(index * block, block), block)
        parts = {}
        for h in range(heads):
            probs = jnp.exp(dot(kx[h, here, :], qx[...], NT))
            grad_probs = dot(vx[h, here, :], dox[...], NT)
            grad_scores = (probs * grad_probs).astype(bf16)
            pair = slice(0, 128) if h < 2 else slice(128, 256)
            own = slice(DH * (h % 2), DH * (h % 2) + DH)
            grad_v = dot(dot_t[pair, :], probs.astype(bf16), NT)[own]
            grad_k = dot(q_t[pair, :], grad_scores, NT)[own]
            parts[h] = (grad_k * 0.125, grad_v)
            grad_q[DH * h : DH * (h + 1), :] += dot(k_t[pair, here], grad_scores)[own]
        stack = [parts[h][j] for j in range(2) for h in range(heads)]
        grads[here, 0 : 2 * cols] = jnp.transpose(jnp.concatenate(stack, axis=0).astype(bf16))
        return carry

    lax.fori_loop(0, (length + block - 1) // block, key_block, 0)
    grads[:, 2 * cols : 3 * cols] = jnp.transpose(grad_q[...].astype(bf16))

    for load in loads:
        load.wait()
    gain, shift = vec_ref[0:1, :].astype(f32), vec_ref[1:2, :].astype(f32)
    step = 256
    sums = [jnp.zeros((1, 1), f32)] * 3
    if stage:
        sums = [old[1][0:1, :], old[1][1:2, :], old[2][0:1, :]]
    for start in range(0, image_len, step):
        here = slice(start, start + step)
        unit, _ = unit_rows(x[here, :].astype(f32))
        normed[here, :] = (unit * gain + shift).astype(bf16)
        part = grads[here, :]
        da = dot(part, w_all[...])
        da_s[here, :] = da.astype(bf16)
        more = [da * unit, da, part.astype(f32)]
        sums = [old_sum + jnp.sum(new, axis=0, keepdims=True) for old_sum, new in zip(sums, more)]
    me = lax.axis_index("tensor")
    core, side = me % 2, me // 2
    if stage == 0:
        half = image_len // 2
        spans = [(core * half, half), ((1 - core) * half, half)]
    elif stage == 1:
        half = image_len // 4
        far = (1 - side) * 2 * half
        spans = [(far + core * half, half), (far + (1 - core) * half, half), (side * 2 * half, 2 * half)]
    else:
        spans = [(0, image_len)]
    stores = []
    for index, (start, size) in enumerate(spans):
        source = da_s.at[pl.ds(pl.multiple_of(start, 256), size)] if size < image_len else da_s
        stores.append(pltpu.make_async_copy(source, outs[index], sems.at[4 + index]))
        stores[-1].start()
    fresh = dot(normed[...], grads[...], TN)
    if stage:
        fresh = fresh + dw[...]
    if stage == 2:
        fresh = fresh.astype(bf16)
        at = 0
        for order, target in zip(orders, dw_outs):
            piece = fresh[:, at : at + target.shape[1]]
            at += target.shape[1]
            target[...] = dot(halving_order(order, fresh.shape[0], dp_size), piece).astype(bf16)
    else:
        dw_outs[0][...] = fresh
    small_out[...] = jnp.concatenate([sums[0], sums[1], jnp.zeros((6, sums[0].shape[1]), f32)], axis=0)
    bias_out[...] = jnp.broadcast_to(sums[2], bias_out.shape)
    for store in stores:
        store.wait()


def image_back(stage, buckets, which, kvq, lse, o, grad_o, vectors, tokens, weight, dp_size, orders, old):
    rows, width = tokens.shape
    cols = o.shape[0]
    images = buckets.shape[0]
    image_len = rows // images
    heads = cols // DH
    half = image_len // 2
    da_rows = [[half, half], [half // 2, half // 2, half], [image_len]][stage]
    picked = lambda w: pl.BlockSpec((image_len, w), lambda i, b, s: (s[0], 0))
    across = lambda w: pl.BlockSpec((w, image_len), lambda i, b, s: (0, s[0]))
    fixed = lambda shape: pl.BlockSpec(shape, lambda i, b, s: (0,) * len(shape))
    if stage == 2:
        dw_shapes = [((width, n), bf16) for n in (256, 3 * cols - 256)]
    else:
        dw_shapes = [((width, 3 * cols), f32)]
    return pl.pallas_call(
        functools.partial(image_back_kernel, block=256, stage=stage, dp_size=dp_size, orders=orders),
        grid_spec=pltpu.PrefetchScalarGridSpec(
            num_scalar_prefetch=2,
            grid=(1,),
            in_specs=[picked(3 * cols), across(8), across(cols), across(cols), fixed(vectors.shape)]
            + [ANY] * 2
            + ([ANY, fixed((8, width)), fixed((8, 3 * cols))] if stage else []),
            out_specs=[ANY] * len(da_rows)
            + [fixed(shape) for shape, _ in dw_shapes]
            + [fixed((8, width)), fixed((8, 3 * cols))],
            scratch_shapes=[
                pltpu.VMEM((image_len, 256), bf16),
                pltpu.VMEM((256, image_len), bf16),
                pltpu.VMEM((image_len, 256), bf16),
                pltpu.VMEM((256, image_len), bf16),
                pltpu.VMEM((heads, image_len, 256), bf16),
                pltpu.VMEM((heads, image_len, 256), bf16),
                pltpu.VMEM((256, image_len), bf16),
                pltpu.VMEM((cols, image_len), f32),
                pltpu.VMEM((image_len, 3 * cols), bf16),
                pltpu.VMEM((image_len, width), bf16),
                pltpu.VMEM((3 * cols, width), bf16),
                pltpu.VMEM((image_len, width), bf16),
                pltpu.VMEM((image_len, width), bf16),
                pltpu.VMEM((width, 3 * cols), f32),
                pltpu.SemaphoreType.DMA((10,)),
            ],
        ),
        out_shape=[jax.ShapeDtypeStruct((n, width), bf16) for n in da_rows]
        + [
            *[jax.ShapeDtypeStruct(*shape) for shape in dw_shapes],
            jax.ShapeDtypeStruct((8, width), f32),
            jax.ShapeDtypeStruct((8, 3 * cols), f32),
        ],
        compiler_params=pltpu.CompilerParams(vmem_limit_bytes=VMEM),
        cost_estimate=cost(10**6, 10**4),
        name=f"image_back_{stage}",
    )(buckets, which, kvq, lse, o, grad_o, vectors, tokens, weight, *old)


def rows_kernel(*refs, parts, dp_size, orders):
    refs = list(refs)
    take = lambda count: [refs.pop(0) for _ in range(count)]
    x_any, g_any, vec_ref, bias_ref, o_in, g_t = take(6)
    wo_in, up_in, down_in = take(2), take(2), take(2)
    quarters = [take(5), take(5)]
    y_ref, e_ref, kept, sent, far_out, small_ref, do_out, wo_refs = *take(2), take(2), take(2), *take(3), take(2)
    x_ref, g_ref, wo_w, up_w, down_w, hidden, normed, mixed, back, c_t, z_s, du_s, grads, came, do_s = take(15)
    far_came, far_next, wo_made, wo_came, sems, far_sems = take(6)
    rows, width = x_ref.shape
    hid = up_w.shape[2]
    step_index = pl.program_id(0)
    part = step_index ^ 2
    dp, me = lax.axis_index("dp"), lax.axis_index("tensor")
    quarter = dp % 4
    here = pl.ds(pl.multiple_of(me * rows, rows), rows)
    inputs = [
        pltpu.make_async_copy(x_any.at[here], x_ref, sems.at[4, 0]),
        pltpu.make_async_copy(g_any.at[here], g_ref, sems.at[4, 1]),
    ]
    half, fourth = width // 2, width // 4
    partners = [(dp, me ^ r) for r in range(parts)]
    along = [(dp ^ (1 << order[0]), me) for order in orders]
    core = [send(grads.at[3 - 2 * i], came.at[i], far_sems, i, partners[1]) for i in range(2)]
    columns = [pl.ds(0, hid), pl.ds(hid, hid)]
    fars = [
        send(grads.at[2, pl.ds(half, half), columns[at]], far_came.at[at], far_sems, 2 + at, along[at]) for at in range(2)
    ]
    nexts = [
        send(grads.at[2, pl.ds(fourth, fourth), columns[at]], far_next.at[at], far_sems, 4 + at, along[1 - at])
        for at in range(2)
    ]
    mine = do_out.at[:, here]
    do_copies = [send(do_s.at[r], mine, far_sems, 5 + r, partners[r]) for r in range(parts - 1, 0, -1)]
    do_copies.append(pltpu.make_async_copy(do_s.at[0], mine, sems.at[4, 2]))
    results = [pltpu.make_async_copy(z_s, e_ref, sems.at[4, 3]), pltpu.make_async_copy(du_s, y_ref, sems.at[4, 4])]
    wo_copy = send(wo_made.at[1], wo_came, far_sems, 9, partners[1])

    def wide(block):
        return block.astype(f32)

    def add_into(target, source, count, columns=slice(None)):
        for start in range(0, count, 64):
            piece = slice(start, start + 64)
            target[piece, columns] = (wide(target[piece, columns]) + wide(source[piece, :])).astype(bf16)

    def loads(source, target, row, at):
        found = [[pltpu.make_async_copy(source[r], target.at[r], sems.at[row, r])] for r in range(2)]
        size = target.shape[1] // 4
        for r in (2, 3):
            found.append([])
            for i in range(4):
                piece, here = quarters[r - 2][i], at
                if i == 3 and at >= split:
                    piece, here = quarters[r - 2][4], at - split
                place = target.at[r, pl.ds(pl.multiple_of((quarter ^ i) * size, size), size)]
                index = 2 + 4 * (r - 2) + i
                found[r].append(pltpu.make_async_copy(piece.at[pl.ds(here, size)], place, sems.at[row, index]))
        return found

    mixed_cols = o_in.shape[1]
    split = (mixed_cols + hid) // 4
    wo_loads = loads(wo_in, wo_w, 0, 0)
    up_loads = loads(up_in, up_w, 1, mixed_cols // 4)
    down_loads = loads(down_in, down_w, 2, (mixed_cols + hid) // 4)
    gain, shift = vec_ref[2:3, :].astype(f32), vec_ref[3:4, :].astype(f32)

    def store_own():
        return [
            pltpu.make_async_copy(
                grads.at[0, pl.ds(side * half, half), columns[at]], group[at], sems.at[3, 2 * side + at]
            )
            for side, group in enumerate((kept, sent))
            for at in range(2)
        ]

    def store_far():
        return [
            pltpu.make_async_copy(grads.at[2, pl.ds(0, fourth), columns[at]], far_out.at[at], sems.at[3, 4 + at])
            for at in range(2)
        ]

    @pl.when(step_index == 0)
    def _():
        for load in inputs:
            load.start()
        for group in wo_loads + up_loads[2:] + down_loads[2:] + up_loads[:2] + down_loads[:2]:
            for load in group:
                load.start()
        greet(partners[1:] + along)
        for group in wo_loads:
            for load in group:
                load.wait()
        for load in inputs:
            load.wait()
        for start in range(0, rows, 256):
            piece = slice(start, start + 256)
            attended = dot(o_in[0, :, piece], wo_w[0], TN)
            for r in range(1, parts):
                attended += dot(o_in[r, :, piece], wo_w[r], TN)
            h1 = x_ref[piece, :].astype(f32) + attended + vec_ref[4:5, :].astype(f32)
            hidden[piece, :] = h1
            unit, _ = unit_rows(h1)
            normed[piece, :] = (unit * gain + shift).astype(bf16)
        c_t[...] = dot(halving_order(orders[1], width, dp_size), normed[...], NT).astype(bf16)
        mixed[...] = jnp.zeros_like(mixed)
        back[...] = jnp.zeros_like(back)
        small_ref[...] = jnp.zeros_like(small_ref)

    for r in range(parts):

        @pl.when(part == r)
        def _():
            for load in up_loads[r] + down_loads[r]:
                load.wait()

    step = 256
    chunks = [slice(s, s + step) for s in range(0, hid, step)]

    def first(cols):
        u = dot(normed[...], up_w[part, :, cols]) + bias_ref[part, 0:1, cols]
        return u, dot(g_ref[...], down_w[part, cols, :], NT)

    def bend(cols, u, dz):
        square = u * u
        scaled = u * GELU_SCALE
        gate = 0.5 + 0.5 * jnp.tanh(scaled * (1.0 + GELU_CUBE * square))
        z_s[:, cols] = (u * gate).astype(bf16)
        slope = gate + (2.0 * gate) * (1.0 - gate) * scaled * (1.0 + (3.0 * GELU_CUBE) * square)
        du = (dz * slope).astype(bf16)
        du_s[:, cols] = du
        small_ref[pl.ds(8 + part, 1), cols] = jnp.sum(du.astype(f32), axis=0, keepdims=True)

    def weigh(cols):
        grads[part, :, cols] = dot(g_t[...], z_s[:, cols]).astype(bf16)
        later = slice(hid + cols.start, hid + cols.stop)
        grads[part, :, later] = dot(c_t[...], du_s[:, cols]).astype(bf16)

    ready = first(chunks[0])
    for index, cols in enumerate(chunks):
        following = first(chunks[index + 1]) if index + 1 < len(chunks) else None
        bend(cols, *ready)
        if index:
            weigh(chunks[index - 1])
        ready = following
    mixed[...] += dot(z_s[...], down_w[part])
    weigh(chunks[-1])
    back[...] += dot(du_s[...], up_w[part], NT)
    @pl.when(part == 3)
    def _():
        core[0].start()

    @pl.when(part == 0)
    def _():
        core[0].wait()
        add_into(grads.at[2], came.at[0], width)
        for copy in fars:
            copy.start()

    @pl.when(part == 1)
    def _():
        core[1].start()
        totals = [jnp.zeros((1, width), f32)] * 4
        for start in range(0, rows, 256):
            piece = slice(start, start + 256)
            h1 = hidden[piece, :]
            unit, inverse = unit_rows(h1)
            dc = back[piece, :]
            wide_g = wide(g_ref[piece, :])
            dh = wide_g + norm_back(dc, gain, unit, inverse)
            z_s[piece, :] = dh.astype(bf16)
            du_s[piece, :] = (h1 + mixed[piece, :] + vec_ref[5:6, :].astype(f32)).astype(bf16)
            news = [jnp.sum(values, axis=0, keepdims=True) for values in (dc * unit, dc, dh, wide_g)]
            totals = [old + new for old, new in zip(totals, news)]
        for index, values in enumerate(totals):
            small_ref[2 + index : 3 + index, :] = values
        results[1].start()
        e = z_s[...]
        results[0].start()
        for r in range(parts):
            do_s[r] = dot(wo_w[r], e, NT).astype(bf16)
        for copy in do_copies:
            copy.start()
        for at in range(2):
            fars[at].wait()
            add_into(grads.at[2], far_came.at[at], half, columns[at])
            nexts[at].start()
        e_t = dot(halving_order(orders[0], width, dp_size), e, NT).astype(bf16)
        blank = jnp.zeros((width, 256 - mixed_cols), bf16)
        for r in range(parts):
            wo_made[r % 2, r // 2] = jnp.concatenate([dot(e_t, o_in[r], NT).astype(bf16), blank], axis=1)
        wo_copy.start()
        core[1].wait()
        add_into(grads.at[0], came.at[1], width)
        for copy in store_own():
            copy.start()
        for at in range(2):
            nexts[at].wait()
            add_into(grads.at[2], far_next.at[at], fourth, columns[at])
        for copy in store_far():
            copy.start()
        wo_copy.wait()
        for index in range(2):
            add_into(wo_made.at[0, index], wo_came.at[index], width)
        wo_stores = [
            pltpu.make_async_copy(wo_made.at[0, index], wo_refs[index], sems.at[4, 5 + index]) for index in range(2)
        ]
        for copy in wo_stores:
            copy.start()
        for copy in store_own() + store_far() + do_copies + results + wo_stores:
            copy.wait()


def own_rows(x, g, vectors, up_bias, o_parts, g_turned, wo, up, down, quarters, dp_size, orders):
    parts, cols, rows = o_parts.shape
    width = x.shape[1]
    hid = up[0].shape[1]
    fixed = lambda shape: pl.BlockSpec(shape, lambda r: (0,) * len(shape))
    once = lambda shape: pl.BlockSpec(shape, lambda r: (0,) * len(shape), pipeline_mode=pl.Buffered(1))
    array = lambda *shape: jax.ShapeDtypeStruct(shape, bf16)
    out = pl.pallas_call(
        functools.partial(rows_kernel, parts=parts, dp_size=dp_size, orders=orders),
        grid=(parts,),
        in_specs=[
            ANY,
            ANY,
            fixed(vectors.shape),
            fixed(up_bias.shape),
            once(o_parts.shape),
            once(g_turned.shape),
        ]
        + [ANY] * 16,
        out_specs=[ANY] * 7 + [fixed((16, width)), ANY] + [ANY] * 2,
        out_shape=[array(rows, width)] * 2
        + [array(width // 2, hid)] * 4
        + [array(2, width // 4, hid)]
        + [jax.ShapeDtypeStruct((16, width), f32), array(cols, x.shape[0])]
        + [array(width, 256)] * 2,
        scratch_shapes=[
            pltpu.VMEM((rows, width), bf16),
            pltpu.VMEM((rows, width), bf16),
            pltpu.VMEM((parts, cols, width), bf16),
            pltpu.VMEM((parts, width, hid), bf16),
            pltpu.VMEM((parts, hid, width), bf16),
            pltpu.VMEM((rows, width), f32),
            pltpu.VMEM((rows, width), bf16),
            pltpu.VMEM((rows, width), f32),
            pltpu.VMEM((rows, width), f32),
            pltpu.VMEM((width, rows), bf16),
            pltpu.VMEM((rows, hid), bf16),
            pltpu.VMEM((rows, hid), bf16),
            pltpu.VMEM((parts, width, 2 * hid), bf16),
            pltpu.VMEM((2, width, 2 * hid), bf16),
            pltpu.VMEM((parts, cols, rows), bf16),
            pltpu.VMEM((2, width // 2, hid), bf16),
            pltpu.VMEM((2, width // 4, hid), bf16),
            pltpu.VMEM((2, 2, width, 256), bf16),
            pltpu.VMEM((2, width, 256), bf16),
            pltpu.SemaphoreType.DMA((5, 12)),
            pltpu.SemaphoreType.DMA((2, 10)),
        ],
        compiler_params=pltpu.CompilerParams(collective_id=4, has_side_effects=True, vmem_limit_bytes=VMEM),
        cost_estimate=cost(12 * rows * width * hid * parts, 8 * parts * width * hid, rows * hid * parts),
        name="own_rows",
    )(x, g, vectors, up_bias, o_parts, g_turned, *wo, *up, *down, *quarters[0], *quarters[1])
    return out[0], out[1], out[2:4], out[4:6], out[6], out[7], out[8], out[9:11]


def greet(partners):
    barrier = pltpu.get_barrier_semaphore()
    for partner in partners:
        pl.semaphore_signal(barrier, inc=1, device_id=partner, device_id_type=pl.DeviceIdType.MESH)
    pl.semaphore_wait(barrier, len(partners))


def send(source, target, sems, index, partner):
    return pltpu.make_async_remote_copy(
        src_ref=source,
        dst_ref=target,
        send_sem=sems.at[0, index],
        recv_sem=sems.at[1, index],
        device_id=partner,
        device_id_type=pl.DeviceIdType.MESH,
    )


def out_kernel(*refs, parts, dp_size, order):
    refs = list(refs)
    take = lambda count: [refs.pop(0) for _ in range(count)]
    o_ref, bias_ref, g_any = take(3)
    shards, pieces = take(3), take(3)
    o_all, bias_all, g_t = take(3)
    shards_to, pieces_to, across, across_to = take(3), take(3), take(2), take(2)
    own_o, own_bias, g_own, sems, local = refs
    dp, me = lax.axis_index("dp"), lax.axis_index("tensor")
    rows = o_all.shape[2]
    partners = [(dp, me ^ r) for r in range(parts)]
    beside, along = (dp ^ 1, me), (dp ^ 2, me)
    greet(partners[1:] + [beside, along])
    copies = []

    def start(source, target, partner):
        copies.append(send(source, target, sems, len(copies), partner))
        copies[-1].start()

    split = across[0].shape[0]
    start(pieces[1].at[pl.ds(0, split)], across[0], along)
    start(pieces[2].at[pl.ds(split, across[1].shape[0])], across[1], beside)
    for r in range(parts - 1, 0, -1):
        source = o_ref.at[:, pl.ds(pl.multiple_of((me ^ r) * rows, rows), rows)]
        start(source, o_all.at[r], partners[r])
        start(bias_ref, bias_all.at[r], partners[r])
    for source, target in zip(shards + pieces, shards_to + pieces_to):
        start(source, target, partners[1])
    mine = o_ref.at[:, pl.ds(pl.multiple_of(me * rows, rows), rows)]
    g_here = g_any.at[pl.ds(pl.multiple_of(me * rows, rows), rows)]
    loads = [
        pltpu.make_async_copy(mine, own_o, local.at[0]),
        pltpu.make_async_copy(bias_ref, own_bias, local.at[1]),
        pltpu.make_async_copy(g_here, g_own, local.at[2]),
    ]
    for load in loads:
        load.start()
    for load in loads:
        load.wait()
    stores = [
        pltpu.make_async_copy(own_o, o_all.at[0], local.at[0]),
        pltpu.make_async_copy(own_bias, bias_all.at[0], local.at[1]),
    ]
    for store in stores:
        store.start()
    g_t[...] = dot(halving_order(order, g_own.shape[1], dp_size), g_own[...], NT).astype(bf16)
    for index in range(2):
        copies[index].wait_recv()
        start(across[index], across_to[index], partners[1])
    for index, copy in enumerate(copies):
        if index < 2:
            copy.wait_send()
        else:
            copy.wait()
    for store in stores:
        store.wait()


def exchange_out(o, bias, g, shards, pieces, parts, dp_size, order):
    cols, rows = o.shape
    split = pieces[0].shape[0] - shards[2].shape[0] // 4
    like = lambda x, count=None: jax.ShapeDtypeStruct((count or x.shape[0],) + x.shape[1:], x.dtype)
    halves = [like(pieces[0], split), like(pieces[0], pieces[0].shape[0] - split)]
    shapes = [
        jax.ShapeDtypeStruct((parts, cols, rows // parts), bf16),
        jax.ShapeDtypeStruct((parts,) + bias.shape, f32),
        jax.ShapeDtypeStruct((g.shape[1], rows // parts), bf16),
        *map(like, shards),
        *map(like, pieces),
        *halves,
        *halves,
    ]
    out = pl.pallas_call(
        functools.partial(out_kernel, parts=parts, dp_size=dp_size, order=order),
        in_specs=[ANY] * 9,
        out_specs=[ANY] * 2 + [pl.BlockSpec(memory_space=pltpu.VMEM)] + [ANY] * (len(shapes) - 3),
        out_shape=shapes,
        scratch_shapes=[
            pltpu.VMEM((cols, rows // parts), bf16),
            pltpu.VMEM(bias.shape, f32),
            pltpu.VMEM((rows // parts, g.shape[1]), bf16),
            pltpu.SemaphoreType.DMA((2, 18)),
            pltpu.SemaphoreType.DMA((3,)),
        ],
        compiler_params=pltpu.CompilerParams(collective_id=1, has_side_effects=True, vmem_limit_bytes=VMEM),
        cost_estimate=cost(15 * 10**9, 10**7),
        name="exchange_out",
    )(o, bias, g, *shards, *pieces)
    return out[0], out[1], out[2], out[3:6], out[6:9], out[9:11], out[11:13]


def pick_kernel(*refs):
    *sources, target, sems = refs
    quarter = lax.axis_index("dp") % 4
    copies, at = [], 0
    for index, source in enumerate(sources):
        size = source.shape[0] // 4
        piece = source.at[pl.ds(pl.multiple_of(quarter * size, size), size)]
        copies.append(pltpu.make_async_copy(piece, target.at[pl.ds(at, size)], sems.at[index]))
        copies[index].start()
        at += size
    for copy in copies:
        copy.wait()


def pick_quarter(shards):
    rows = sum(shard.shape[0] for shard in shards) // 4
    return pl.pallas_call(
        pick_kernel,
        in_specs=[ANY] * len(shards),
        out_specs=pl.BlockSpec(memory_space=pltpu.VMEM),
        out_shape=jax.ShapeDtypeStruct((rows, shards[0].shape[1]), bf16),
        scratch_shapes=[pltpu.SemaphoreType.DMA((len(shards),))],
        name="pick_quarter",
    )(*shards)


def finish_kernel(
    own_any, mid_any, far_own_any, mid_keep_any, mid_came_any, x_any, dh_any, vec_ref, late_ref, bias_ref, early_ref, *refs,
    dp_size, tracks,
):
    bits = dp_size.bit_length() - 1
    refs = list(refs)
    take = lambda count: [refs.pop(0) for _ in range(count)]
    weights = [take(1), take(1), take(2), take(2), take(2)]
    (out_ref,) = take(1)
    weights_out = take(len(tracks))
    (sums_out,) = take(1)
    held, other, far_own, mid_keep, mid_came, far_mid, x_v, dh_v = take(8)
    sent = [take(len(order)) for order in tracks]
    got = [take(len(order)) for order in tracks]
    totals = take(len(tracks))
    sums, got_s, sems, w_sems, local = refs
    dp, me = lax.axis_index("dp"), lax.axis_index("tensor")
    core, side = me % 2, me // 2
    rows, width = out_ref.shape
    image_len = own_any.shape[0]
    half = image_len // 2
    x_own = x_any.at[pl.ds(pl.multiple_of(me * rows, rows), rows)]
    at_own = side * half
    at_mid = (1 - side) * image_len
    across = [(dp, me ^ 1), (dp, me ^ 2)]
    along = [(dp ^ (1 << bit), me) for bit in range(bits)]
    greet(across + along)

    loads = [
        pltpu.make_async_copy(own_any, held.at[pl.ds(pl.multiple_of(at_own, half), image_len)], local.at[0]),
        pltpu.make_async_copy(mid_any, held.at[pl.ds(pl.multiple_of(at_mid, half), half)], local.at[1]),
        pltpu.make_async_copy(far_own_any, far_own, local.at[2]),
        pltpu.make_async_copy(mid_keep_any, mid_keep, local.at[3]),
        pltpu.make_async_copy(mid_came_any, mid_came, local.at[6]),
        pltpu.make_async_copy(x_own, x_v, local.at[4]),
        pltpu.make_async_copy(dh_any, dh_v, local.at[5]),
    ]
    for load in loads:
        load.start()
    mid_load = loads.pop(4)
    mid_load.wait()
    loads[3].wait()
    mid_keep[...] = (mid_keep[...].astype(f32) + mid_came[...].astype(f32)).astype(bf16)

    copies = [[] for _ in tracks]
    tall = [totals[track].shape[0] for track in range(len(tracks))]

    def first(track, here):
        terms = [term[here, :].astype(f32) for term in weights[track]]
        return terms[0] + terms[1] if len(terms) > 1 else terms[0]

    def send_weight(track, step):
        target = sent[track][step]
        span = tall[track] // 2
        if step == 0:
            target[...] = first(track, slice(span, 2 * span)).astype(target.dtype)
        else:
            target[...] = totals[track][span : 2 * span, :].astype(target.dtype)
        route = along[tracks[track][step]]
        index = sum(len(order) for order in tracks[:track]) + step
        copies[track].append(send(target, got[track][step], w_sems, index, route))
        copies[track][step].start()

    def add_weight(track, step):
        copies[track][step].wait()
        tall[track] //= 2
        span = tall[track]
        kept = totals[track][0:span, :] if step else first(track, slice(0, span))
        totals[track][0:span, :] = kept + got[track][step][...].astype(f32)

    for track in range(len(tracks)):
        if tracks[track]:
            send_weight(track, 0)
    mid_copy = send(mid_keep, far_mid, sems, 14, across[1])

    sums[...] = early_ref[...]
    sums[0:2, :] = late_ref[0:2, :]
    sums[12:13, 0 : bias_ref.shape[1]] = bias_ref[0:1, :]
    routes = across + along
    s_copies = []

    def send_sums(step):
        s_copies.append(send(sums, got_s.at[step], sems, step, routes[step]))
        s_copies[step].start()

    def add_sums(step):
        s_copies[step].wait()
        if step < 2:
            sums[0:6, :] += got_s[step, 0:6, :]
            new = [sums[8 + r : 9 + r, :] + got_s[step, 8 + (r ^ (1 << step)) : 9 + (r ^ (1 << step)), :] for r in range(4)]
            for r in range(4):
                sums[8 + r : 9 + r, :] = new[r]
        else:
            sums[...] += got_s[step]

    def turn(track, step):
        add_weight(track, step)
        if step + 1 < len(tracks[track]):
            send_weight(track, step + 1)

    mid_copy.start()
    send_sums(0)
    for load in loads[:3]:
        load.wait()
    here = pl.ds(pl.multiple_of(at_own + core * half, half), half)
    held[here, :] = (held[here, :].astype(f32) + far_own[...].astype(f32)).astype(bf16)
    turn(0, 0)
    add_sums(0)
    send_sums(1)
    turn(1, 0)
    turn(2, 0)
    add_sums(1)
    send_sums(2)
    turn(0, 1)
    mid_copy.wait()

    here = pl.ds(pl.multiple_of(at_mid + core * (half // 2), half // 2), half // 2)
    held[here, :] = (held[here, :].astype(f32) + far_mid[...].astype(f32)).astype(bf16)
    theirs = held.at[pl.ds(pl.multiple_of((1 - core) * rows, rows), rows)]
    da_copy = send(theirs, other, sems, 15, across[0])
    da_copy.start()
    turn(1, 1)
    turn(2, 1)
    add_sums(2)
    if bits > 1:
        send_sums(3)
    for load in loads[4:]:
        load.wait()
    da_copy.wait()
    gain = vec_ref[0:1, :].astype(f32)
    step = 256
    for start in range(0, rows, step):
        piece = slice(start, start + step)
        unit, inverse = unit_rows(x_v[piece, :].astype(f32))
        mine = held[pl.ds(pl.multiple_of(core * rows + start, step), step), :].astype(f32)
        da = mine + other[piece, :].astype(f32)
        out_ref[piece, :] = (dh_v[piece, :].astype(f32) + norm_back(da, gain, unit, inverse)).astype(bf16)

    for step in range(2, bits):
        for track in range(3):
            turn(track, step)
        add_sums(1 + step)
        if step < bits:
            send_sums(2 + step)
    add_sums(1 + bits)
    for step in range(bits):
        for track in (3, 4):
            if step < len(tracks[track]):
                turn(track, step)
    for track in range(len(tracks)):
        if tracks[track]:
            weights_out[track][...] = totals[track][0 : weights_out[track].shape[0], :]
        else:
            weights_out[track][...] = first(track, slice(None))
    sums_out[...] = sums[...]


def unpack_kernel(out_ref, dw_one, dw_two, wo_in, down_ref, up_ref, sums_ref, out_to, qkv_to, wo_to, down_to, up_to, bias_to):
    out_to[...] = out_ref[...]
    down_to[...] = down_ref[...]
    up_to[...] = up_ref[...]
    cols = wo_to.shape[0]
    dw_ref = jnp.concatenate([dw_one[...], dw_two[...]], axis=1)
    for index, at in enumerate((2, 0, 1)):
        qkv_to[index] = dw_ref[:, at * cols : (at + 1) * cols]
    wo_to[...] = jnp.transpose(wo_in[...])[0:cols]
    for index, at in enumerate((2, 1)):
        bias_to[index : index + 1, :] = sums_ref[12:13, at * cols : (at + 1) * cols]


def unpack(out, dw_one, dw_two, wo, down, up, sums, cols):
    rows = dw_one.shape[0]
    vmem = pl.BlockSpec(memory_space=pltpu.VMEM)
    array = lambda *shape: jax.ShapeDtypeStruct(shape, f32)
    return pl.pallas_call(
        unpack_kernel,
        in_specs=[vmem] * 7,
        out_specs=[vmem] * 6,
        out_shape=[
            jax.ShapeDtypeStruct(out.shape, bf16),
            array(3, rows, cols),
            array(cols, rows),
            array(*down.shape),
            array(*up.shape),
            array(2, cols),
        ],
        compiler_params=pltpu.CompilerParams(vmem_limit_bytes=VMEM),
        name="unpack",
    )(out, dw_one, dw_two, wo, down, up, sums)


def finish(own, mid, far_own, mid_keep, mid_came, x, dh, vectors, late, bias, early, weights, tracks, dp_size):
    rows, width = dh.shape
    bits = dp_size.bit_length() - 1
    buffers, totals = [], []
    for group, order in zip(weights, tracks):
        tall, wide = group[0].shape[-2:]
        totals.append(pltpu.VMEM((tall, wide), f32))
        for bit in order:
            tall //= 2
            buffers.append(pltpu.VMEM((tall, wide), bf16 if tall % 16 == 0 else f32))
    count = sum(len(order) for order in tracks)
    flat = [weight for group in weights for weight in group]
    vmem = pl.BlockSpec(memory_space=pltpu.VMEM)
    return pl.pallas_call(
        functools.partial(finish_kernel, dp_size=dp_size, tracks=tracks),
        in_specs=[ANY] * 7 + [vmem] * (4 + len(flat)),
        out_specs=[vmem] * (2 + len(tracks)),
        out_shape=[jax.ShapeDtypeStruct((rows, width), bf16)]
        + [jax.ShapeDtypeStruct((width // dp_size, group[0].shape[-1]), f32) for group in weights]
        + [jax.ShapeDtypeStruct((16, width), f32)],
        scratch_shapes=[
            pltpu.VMEM((2 * rows, width), bf16),
            pltpu.VMEM((rows, width), bf16),
            pltpu.VMEM(far_own.shape, bf16),
            pltpu.VMEM(mid_keep.shape, bf16),
            pltpu.VMEM(mid_keep.shape, bf16),
            pltpu.VMEM(mid_keep.shape, bf16),
            pltpu.VMEM((rows, width), bf16),
            pltpu.VMEM((rows, width), bf16),
        ]
        + buffers * 2
        + totals
        + [
            pltpu.VMEM((16, width), f32),
            pltpu.VMEM((2 + bits, 16, width), f32),
            pltpu.SemaphoreType.DMA((2, 16)),
            pltpu.SemaphoreType.DMA((2, count)),
            pltpu.SemaphoreType.DMA((7,)),
        ],
        compiler_params=pltpu.CompilerParams(
            collective_id=3, has_side_effects=True, vmem_limit_bytes=VMEM
        ),
        name="finish",
    )(own, mid, far_own, mid_keep, mid_came, x, dh, vectors, late, bias, early, *flat)


def on_device(
    dp_size, tokens, buckets, norm1_gain, norm1_bias, qkv_weight, qkv_bias, out_weight, out_bias,
    norm2_gain, norm2_bias, up_weight, up_bias, down_weight, down_bias, cotangent,
):
    parts = 4
    dp_bits = dp_size.bit_length() - 1
    me = lax.axis_index("tensor")
    token_rows, width = tokens.shape
    share = token_rows // parts
    hid = up_weight.shape[1]
    cols = qkv_weight.shape[2]

    def over_tensor(values, mask):
        return lax.ppermute(values, "tensor", [(i, i ^ mask) for i in range(parts)])

    def over_dp(values, mask):
        return lax.ppermute(values, "dp", [(i, i ^ mask) for i in range(dp_size)])

    def add(*terms):
        total = terms[0].astype(f32)
        for term in terms[1:]:
            total = total + term.astype(f32)
        return total.astype(bf16)

    shards = (out_weight, up_weight, down_weight)
    near = over_tensor(pick_quarter(shards), 2)
    blank = jnp.zeros_like(norm1_gain)
    vectors = jnp.stack(
        [norm1_gain, norm1_bias, norm2_gain, norm2_bias, out_bias, down_bias, blank, blank]
    )
    up_bias_rows = jnp.broadcast_to(up_bias.astype(f32)[None], (8, hid))
    orders = [list(range(dp_bits)), [1, 0] + list(range(2, dp_bits))]
    turned_weight = jnp.swapaxes(qkv_weight, 1, 2)
    kvq, bound = project(tokens, vectors, turned_weight, qkv_bias)
    near, kvq = lax.optimization_barrier((near, kvq))
    beside, along = over_dp(near, 1), over_dp(near, 2)
    o, lse = attend(buckets, kvq, bound)
    near, beside, along, o = lax.optimization_barrier((near, beside, along, o))
    mine = [near, beside, along]
    o_parts, bias_parts, g_turned, shards_to, other, across, across_to = exchange_out(
        o, up_bias_rows, cotangent, shards, mine, parts, dp_size, orders[0]
    )
    wo, up, down = zip(shards, shards_to)
    quarters = [[*mine, *across], [*other, *across_to]]
    layer_out, e, kept, sent, far, early, grad_o, grad_wo = own_rows(
        tokens, cotangent, vectors, bias_parts, o_parts, g_turned, wo, up, down, quarters, dp_size, orders
    )

    tie = lax.optimization_barrier
    got = [over_dp(half, 1 << order[0]) for half, order in zip(sent, orders)]
    crossed, wo_far = over_tensor(far, 2), over_tensor(grad_wo[1], 2)

    side = me // 2
    order = [2 - 2 * side, jnp.ones_like(side), 2 * side]
    run = lambda stage, old, o: image_back(
        stage, buckets, order[stage].reshape(1).astype(jnp.int32), kvq, lse, o, grad_o, vectors, tokens, turned_weight,
        dp_size, orders, old,
    )
    da_keep, da_send, *old = run(0, [], o)
    came, first_keep = over_tensor(da_send, 1), da_keep
    *got, o = tie((*got, o, *old))[:3]
    split = width // 4
    sent = [add(k[split:], g[split:]) for k, g in zip(kept, got)]
    kept = [add(k[:split], g[:split]) for k, g in zip(kept, got)]
    got = [over_dp(half, 1 << order[1]) for half, order in zip(sent, orders)]
    mid_keep, da_send, mid, *old = run(1, old, o)
    came, o, crossed, *got = tie((came, o, crossed, *got, *old))[:5]
    far_own = over_tensor(add(first_keep, came), 2)
    mid_came = over_tensor(da_send, 1)
    split //= 2
    terms = list(zip(kept, got, crossed))
    sent = jnp.stack([add(*[t[split:] for t in group]) for group in terms])
    kept = [add(*[t[:split] for t in group]) for group in terms]
    got = over_dp(sent, 1 << orders[0][2])
    own, *dw, late, bias_sums = run(2, old, o)
    got, far_own, mid_came, own, wo_far = tie((got, far_own, mid_came, own, wo_far))
    weights = [dw[:1], dw[1:], [grad_wo[0], wo_far]] + [[k, g] for k, g in zip(kept, got)]
    tracks = [orders[0], orders[1], orders[0], orders[0][3:], orders[1][3:]]
    out, dw_one, dw_two, wo_out, down_out, grad_up, sums = finish(
        own, mid, far_own, mid_keep, mid_came, tokens, e, vectors, late, bias_sums, early, weights, tracks, dp_size
    )
    input_grad, grad_qkv_weight, grad_out, down_out, grad_up, grad_qkv_bias = unpack(
        out, dw_one, dw_two, wo_out, down_out, grad_up, sums, cols
    )
    grad_down = down_out.T
    return (
        layer_out,
        input_grad,
        sums[0],
        sums[1],
        grad_qkv_weight,
        grad_qkv_bias,
        grad_out,
        sums[4],
        sums[2],
        sums[3],
        grad_up,
        sums[8],
        grad_down,
        sums[5],
    )


def solution(mesh):
    return jax.shard_map(
        functools.partial(on_device, mesh.shape["dp"]),
        mesh=mesh,
        in_specs=(
            P("dp", None),
            P("dp"),
            P(),
            P(),
            P(None, None, "tensor"),
            P(None, "tensor"),
            P("tensor", None),
            P(),
            P(),
            P(),
            P(None, "tensor"),
            P("tensor"),
            P("tensor", None),
            P(),
            P("dp", None),
        ),
        out_specs=(
            P(("dp", "tensor"), None),
            P(("dp", "tensor"), None),
            P(),
            P(),
            P(None, "dp", "tensor"),
            P(None, "tensor"),
            P("tensor", "dp"),
            P(),
            P(),
            P(),
            P("dp", "tensor"),
            P("tensor"),
            P("tensor", "dp"),
            P(),
        ),
        check_vma=False,
    )
```

```python
import functools

import jax
import jax.numpy as jnp
from jax import lax
from jax.experimental import pallas as pl
from jax.experimental.pallas import tpu as pltpu
from jax.sharding import PartitionSpec as P

DH = 64
NORM_EPSILON = 1e-06
GRID_SIXTEENTHS = (16, 15, 15, 12, 12, 8, 8, 6, 6)
GELU_SCALE = 0.7978845608028654
GELU_CUBE = 0.044715
VMEM = 60 << 20
NN = (((1,), (0,)), ((), ()))
NT = (((1,), (1,)), ((), ()))
TN = (((0,), (0,)), ((), ()))
bf16 = jnp.bfloat16
f32 = jnp.float32
ANY = pl.BlockSpec(memory_space=pl.ANY)


def dot(left, right, dims=NN):
    return lax.dot_general(left, right, dims, preferred_element_type=f32)


def lanes(rows, width):
    return lax.broadcasted_iota(jnp.int32, (rows, width), 1)


def live_lengths(image_len):
    return sorted({image_len * s // 16 for s in GRID_SIXTEENTHS})


def live_length(bucket, image_len):
    length = jnp.int32(0)
    for index, sixteenths in enumerate(GRID_SIXTEENTHS):
        length = jnp.where(bucket == index, image_len * sixteenths // 16, length)
    return length


def cost(flops, nbytes, transcendentals=0):
    return pl.CostEstimate(flops=flops, bytes_accessed=nbytes, transcendentals=transcendentals)


def split3(values):
    high = values.astype(bf16).astype(f32)
    middle = (values - high).astype(bf16).astype(f32)
    return high, middle, values - high - middle


def halving_order(order, width, dp_size):
    bits = dp_size.bit_length() - 1
    size = width // dp_size
    place = lax.broadcasted_iota(jnp.int32, (width, 128), 0)
    block = jnp.zeros_like(place)
    for index in range(1, dp_size):
        block = block + (place >= index * size).astype(jnp.int32)
    turned = jnp.zeros_like(block)
    for step, bit in enumerate(order):
        turned = turned | (((block >> (bits - 1 - step)) & 1) << bit)
    source = (turned ^ lax.axis_index("dp")) * size + (place - block * size)
    lane = lanes(width, 128)
    return jnp.concatenate(
        [jnp.where(source == lane + start, 1.0, 0.0).astype(bf16) for start in range(0, width, 128)], axis=1
    )


def unit_rows(values):
    centred = values - jnp.mean(values, axis=-1, keepdims=True)
    spread = jnp.mean(centred * centred, axis=-1, keepdims=True)
    inverse = lax.rsqrt(spread + NORM_EPSILON)
    return centred * inverse, inverse


def norm_back(grad, gain, unit, inverse):
    scaled = grad * gain
    mean_one = jnp.mean(scaled, axis=-1, keepdims=True)
    mean_two = jnp.mean(scaled * unit, axis=-1, keepdims=True)
    return inverse * (scaled - mean_one - unit * mean_two)


def project_kernel(x_ref, vec_ref, w_ref, bias_ref, out_ref, bound_ref, w_all):
    cols = w_ref.shape[1]

    @pl.when(pl.program_id(0) == 0)
    def _():
        for index, source in enumerate((1, 2, 0)):
            w_all[index * cols : (index + 1) * cols, :] = w_ref[source]

    gain, shift = vec_ref[0:1, :].astype(f32), vec_ref[1:2, :].astype(f32)
    bias = bias_ref[...].astype(f32)
    bias = jnp.concatenate([jnp.zeros((1, cols), f32), bias[1:2], bias[0:1]], axis=1)
    rows, step = x_ref.shape[0], 128
    row = lax.broadcasted_iota(jnp.int32, (3 * cols, 128), 0)
    pick = jnp.where(row // DH == lanes(3 * cols, 128), 1.0, 0.0).astype(bf16)

    def normed(start):
        unit, _ = unit_rows(x_ref[start : start + step, :].astype(f32))
        return (unit * gain + shift).astype(bf16)

    largest = None
    ready = normed(0)
    for start in range(0, rows, step):
        following = normed(start + step) if start + step < rows else None
        values = (dot(ready, w_all[...], NT) + bias).astype(bf16)
        out_ref[start : start + step, :] = values
        squares = jnp.max(dot(values * values, pick), axis=0, keepdims=True)
        largest = squares if largest is None else jnp.maximum(largest, squares)
        ready = following
    bound_ref[0] = jnp.broadcast_to(largest, (8, 128))


def project(tokens, vectors, weight, bias):
    rows, width = tokens.shape
    cols = weight.shape[1]
    block = 512
    fixed = lambda shape: pl.BlockSpec(shape, lambda i: (0,) * len(shape))
    return pl.pallas_call(
        project_kernel,
        grid=(rows // block,),
        in_specs=[
            pl.BlockSpec((block, width), lambda i: (i, 0)),
            fixed(vectors.shape),
            fixed(weight.shape),
            fixed(bias.shape),
        ],
        out_specs=[
            pl.BlockSpec((block, 3 * cols), lambda i: (i, 0)),
            pl.BlockSpec((1, 8, 128), lambda i: (i, 0, 0)),
        ],
        out_shape=[
            jax.ShapeDtypeStruct((rows, 3 * cols), bf16),
            jax.ShapeDtypeStruct((rows // block, 8, 128), f32),
        ],
        scratch_shapes=[pltpu.VMEM((3 * cols, width), bf16)],
        compiler_params=pltpu.CompilerParams(vmem_limit_bytes=VMEM),
        cost_estimate=cost(6 * rows * width * cols, 2 * rows * (width + 3 * cols)),
        name="project",
    )(tokens, vectors, weight, bias)


def attend_kernel(bucket_ref, kvq_ref, bound_ref, o_ref, lse_ref, kx, vt, *, block):
    cols, image_len = o_ref.shape
    heads = cols // DH
    at_q = 2 * cols
    length = live_length(bucket_ref[pl.program_id(0)], image_len)
    squares = jnp.max(bound_ref[...], axis=0)
    lane = lanes(8, 128)
    largest_key = jnp.max(jnp.where(lane < heads, squares, 0.0))
    of_query = (lane >= 2 * heads) & (lane < 3 * heads)
    largest_query = jnp.max(jnp.where(of_query, squares, 0.0))
    small = largest_key * largest_query <= (8.0 * 60.0) ** 2

    def run(live, subtract):
        scaled = kvq_ref[0:live, 0:192] * jnp.asarray(0.125, bf16)
        flipped = jnp.transpose(kvq_ref[0:live, 128:384])
        lane = lanes(live, 128)
        for h in range(heads):
            if h < 2:
                keep = (lane < DH) if h == 0 else (lane >= DH)
                kx[h, 0:live, :] = jnp.where(keep, scaled[:, 0:128], jnp.zeros((), bf16))
            else:
                kx[h, 0:live, 0:DH] = scaled[:, 128:192]
            vt[h, 0:DH, 0:live] = flipped[DH * (h + 1) : DH * (h + 2)]
            vt[h, DH:128, 0:live] = jnp.ones((DH, live), bf16)

        def scores(h, start):
            here = slice(start, start + block)
            if h < 2:
                return dot(kx[h, 0:live, :], kvq_ref[here, at_q : at_q + 128], NT)
            return dot(kx[h, 0:live, 0:DH], kvq_ref[here, at_q + 128 : at_q + 192], NT)

        parts = {}

        def finish(h, start, score):
            offset = 0.0
            if subtract:
                key = lax.broadcasted_iota(jnp.int32, score.shape, 0)
                score = jnp.where(key < length, score, -1e30)
                offset = jnp.max(score, axis=0, keepdims=True)
                score = score - offset
            mixed = dot(vt[h, :, 0:live], jnp.exp(score).astype(bf16))
            total = mixed[DH : DH + 1]
            here = slice(start, start + block)
            parts[h] = -(offset + jnp.log(total))
            o_ref[DH * h : DH * (h + 1), here] = (mixed[:DH] * (1.0 / total)).astype(bf16)
            if h == heads - 1:
                rows = [parts[i] for i in range(heads)]
                lse_ref[:, here] = jnp.concatenate(rows + [jnp.zeros((8 - heads, block), f32)], axis=0)

        items = [(h, s) for s in range(0, image_len, block) for h in range(heads)]
        score = scores(*items[0])
        for index, item in enumerate(items):
            following = scores(*items[index + 1]) if index + 1 < len(items) else None
            finish(*item, score)
            score = following

    for live in live_lengths(image_len):
        pl.when(small & (length == live))(functools.partial(run, live, False))
    pl.when(jnp.logical_not(small))(functools.partial(run, image_len, True))


def attend(buckets, kvq, bound):
    rows = kvq.shape[0]
    cols = kvq.shape[1] // 3
    images = buckets.shape[0]
    image_len = rows // images
    heads = cols // DH
    by_rows = lambda w: pl.BlockSpec((image_len, w), lambda i, b: (i, 0))
    by_cols = lambda w: pl.BlockSpec((w, image_len), lambda i, b: (0, i))
    return pl.pallas_call(
        functools.partial(attend_kernel, block=512),
        grid_spec=pltpu.PrefetchScalarGridSpec(
            num_scalar_prefetch=1,
            grid=(images,),
            in_specs=[by_rows(3 * cols), pl.BlockSpec(bound.shape, lambda i, b: (0, 0, 0))],
            out_specs=[by_cols(cols), by_cols(8)],
            scratch_shapes=[
                pltpu.VMEM((heads, image_len, 128), bf16),
                pltpu.VMEM((heads, 128, image_len), bf16),
            ],
        ),
        out_shape=[
            jax.ShapeDtypeStruct((cols, rows), bf16),
            jax.ShapeDtypeStruct((8, rows), f32),
        ],
        compiler_params=pltpu.CompilerParams(vmem_limit_bytes=VMEM),
        cost_estimate=cost(16 * rows * image_len * cols, 12 * rows * cols, rows * image_len * heads),
        name="attend",
    )(buckets, kvq, bound)


def image_back_kernel(bucket_ref, which_ref, kvq_ref, lse_ref, o_ref, do_ref, vec_ref, *refs, block, stage, dp_size, orders):
    refs = list(refs)
    take = lambda count: [refs.pop(0) for _ in range(count)]
    x_any, w_any = take(2)
    old = take(3) if stage else None
    outs = take((2, 3, 1)[stage])
    dw_outs = take(2 if stage == 2 else 1)
    small_out, bias_out = take(2)
    dox, dot_t, qx, q_t, kx, vx, k_t, grad_q, grads, x, w_all, da_s, normed, dw, sems = take(15)
    cols, image_len = o_ref.shape
    heads = cols // DH
    image = which_ref[0]
    loads = [
        pltpu.make_async_copy(x_any.at[pl.ds(image * image_len, image_len)], x, sems.at[0]),
    ]
    for index, source in enumerate((1, 2, 0)):
        target = w_all.at[pl.ds(index * cols, cols)]
        loads.append(pltpu.make_async_copy(w_any.at[source], target, sems.at[7 + index]))
    if stage:
        loads.append(pltpu.make_async_copy(old[0], dw, sems.at[3]))
    for load in loads:
        load.start()
    length = live_length(bucket_ref[image], image_len)
    inner = []
    for h in range(heads):
        own = slice(DH * h, DH * (h + 1))
        product = do_ref[own, :].astype(f32) * o_ref[own, :].astype(f32)
        inner += list(split3(-jnp.sum(product, axis=0, keepdims=True)))
    blank = [jnp.zeros((DH - 3 * heads, image_len), f32)]
    dot_t[0:cols, :] = do_ref[...]
    dot_t[cols:, :] = jnp.concatenate(inner + blank, axis=0).astype(bf16)
    dox[...] = jnp.transpose(dot_t[...])
    outer = [part for h in range(heads) for part in split3(lse_ref[h : h + 1, :])]
    row = lax.broadcasted_iota(jnp.int32, (DH - 3 * heads, image_len), 0)
    outer = jnp.concatenate(outer + [jnp.where(row == 0, 1.0, 0.0)], axis=0).astype(bf16)
    q = kvq_ref[:, 2 * cols : 3 * cols]
    q_t[0:cols, :] = jnp.transpose(q)
    q_t[cols:, :] = outer
    qx[...] = jnp.concatenate([q, jnp.transpose(outer)], axis=1)
    scaled = kvq_ref[:, 0:cols] * jnp.asarray(0.125, bf16)
    values = kvq_ref[:, cols : 2 * cols]
    k_t[0:cols, :] = jnp.transpose(scaled)
    lane, side = lanes(image_len, cols), lanes(image_len, DH)
    key = lax.broadcasted_iota(jnp.int32, (image_len, DH), 0)
    zero = jnp.zeros((), bf16)
    for h in range(heads):
        keep = (lane >= DH * h) & (lane < DH * (h + 1))
        ones = jnp.where((side >= 3 * h) & (side < 3 * h + 3), 1.0, 0.0)
        dead = jnp.where((side == 3 * heads) & (key >= length), -1e30, ones).astype(bf16)
        kx[h] = jnp.concatenate([jnp.where(keep, scaled, zero), dead], axis=1)
        vx[h] = jnp.concatenate([jnp.where(keep, values, zero), ones.astype(bf16)], axis=1)
    grads[:, 0 : 2 * cols] = jnp.zeros((image_len, 2 * cols), bf16)
    grad_q[...] = jnp.zeros_like(grad_q)

    def key_block(index, carry):
        here = pl.ds(pl.multiple_of(index * block, block), block)
        parts = {}
        for h in range(heads):
            probs = jnp.exp(dot(kx[h, here, :], qx[...], NT))
            grad_probs = dot(vx[h, here, :], dox[...], NT)
            grad_scores = (probs * grad_probs).astype(bf16)
            pair = slice(0, 128) if h < 2 else slice(128, 256)
            own = slice(DH * (h % 2), DH * (h % 2) + DH)
            grad_v = dot(dot_t[pair, :], probs.astype(bf16), NT)[own]
            grad_k = dot(q_t[pair, :], grad_scores, NT)[own]
            parts[h] = (grad_k * 0.125, grad_v)
            grad_q[DH * h : DH * (h + 1), :] += dot(k_t[pair, here], grad_scores)[own]
        stack = [parts[h][j] for j in range(2) for h in range(heads)]
        grads[here, 0 : 2 * cols] = jnp.transpose(jnp.concatenate(stack, axis=0).astype(bf16))
        return carry

    lax.fori_loop(0, (length + block - 1) // block, key_block, 0)
    grads[:, 2 * cols : 3 * cols] = jnp.transpose(grad_q[...].astype(bf16))

    for load in loads:
        load.wait()
    gain, shift = vec_ref[0:1, :].astype(f32), vec_ref[1:2, :].astype(f32)
    step = 256
    sums = [jnp.zeros((1, 1), f32)] * 3
    if stage:
        sums = [old[1][0:1, :], old[1][1:2, :], old[2][0:1, :]]
    for start in range(0, image_len, step):
        here = slice(start, start + step)
        unit, _ = unit_rows(x[here, :].astype(f32))
        normed[here, :] = (unit * gain + shift).astype(bf16)
        part = grads[here, :]
        da = dot(part, w_all[...])
        da_s[here, :] = da.astype(bf16)
        more = [da * unit, da, part.astype(f32)]
        sums = [old_sum + jnp.sum(new, axis=0, keepdims=True) for old_sum, new in zip(sums, more)]
    me = lax.axis_index("tensor")
    core, side = me % 2, me // 2
    if stage == 0:
        half = image_len // 2
        spans = [(core * half, half), ((1 - core) * half, half)]
    elif stage == 1:
        half = image_len // 4
        far = (1 - side) * 2 * half
        spans = [(far + core * half, half), (far + (1 - core) * half, half), (side * 2 * half, 2 * half)]
    else:
        spans = [(0, image_len)]
    stores = []
    for index, (start, size) in enumerate(spans):
        source = da_s.at[pl.ds(pl.multiple_of(start, 256), size)] if size < image_len else da_s
        stores.append(pltpu.make_async_copy(source, outs[index], sems.at[4 + index]))
        stores[-1].start()
    fresh = dot(normed[...], grads[...], TN)
    if stage:
        fresh = fresh + dw[...]
    if stage == 2:
        fresh = fresh.astype(bf16)
        at = 0
        for order, target in zip(orders, dw_outs):
            piece = fresh[:, at : at + target.shape[1]]
            at += target.shape[1]
            target[...] = dot(halving_order(order, fresh.shape[0], dp_size), piece).astype(bf16)
    else:
        dw_outs[0][...] = fresh
    small_out[...] = jnp.concatenate([sums[0], sums[1], jnp.zeros((6, sums[0].shape[1]), f32)], axis=0)
    bias_out[...] = jnp.broadcast_to(sums[2], bias_out.shape)
    for store in stores:
        store.wait()


def image_back(stage, buckets, which, kvq, lse, o, grad_o, vectors, tokens, weight, dp_size, orders, old):
    rows, width = tokens.shape
    cols = o.shape[0]
    images = buckets.shape[0]
    image_len = rows // images
    heads = cols // DH
    half = image_len // 2
    da_rows = [[half, half], [half // 2, half // 2, half], [image_len]][stage]
    picked = lambda w: pl.BlockSpec((image_len, w), lambda i, b, s: (s[0], 0))
    across = lambda w: pl.BlockSpec((w, image_len), lambda i, b, s: (0, s[0]))
    fixed = lambda shape: pl.BlockSpec(shape, lambda i, b, s: (0,) * len(shape))
    if stage == 2:
        dw_shapes = [((width, n), bf16) for n in (256, 3 * cols - 256)]
    else:
        dw_shapes = [((width, 3 * cols), f32)]
    return pl.pallas_call(
        functools.partial(image_back_kernel, block=256, stage=stage, dp_size=dp_size, orders=orders),
        grid_spec=pltpu.PrefetchScalarGridSpec(
            num_scalar_prefetch=2,
            grid=(1,),
            in_specs=[picked(3 * cols), across(8), across(cols), across(cols), fixed(vectors.shape)]
            + [ANY] * 2
            + ([ANY, fixed((8, width)), fixed((8, 3 * cols))] if stage else []),
            out_specs=[ANY] * len(da_rows)
            + [fixed(shape) for shape, _ in dw_shapes]
            + [fixed((8, width)), fixed((8, 3 * cols))],
            scratch_shapes=[
                pltpu.VMEM((image_len, 256), bf16),
                pltpu.VMEM((256, image_len), bf16),
                pltpu.VMEM((image_len, 256), bf16),
                pltpu.VMEM((256, image_len), bf16),
                pltpu.VMEM((heads, image_len, 256), bf16),
                pltpu.VMEM((heads, image_len, 256), bf16),
                pltpu.VMEM((256, image_len), bf16),
                pltpu.VMEM((cols, image_len), f32),
                pltpu.VMEM((image_len, 3 * cols), bf16),
                pltpu.VMEM((image_len, width), bf16),
                pltpu.VMEM((3 * cols, width), bf16),
                pltpu.VMEM((image_len, width), bf16),
                pltpu.VMEM((image_len, width), bf16),
                pltpu.VMEM((width, 3 * cols), f32),
                pltpu.SemaphoreType.DMA((10,)),
            ],
        ),
        out_shape=[jax.ShapeDtypeStruct((n, width), bf16) for n in da_rows]
        + [
            *[jax.ShapeDtypeStruct(*shape) for shape in dw_shapes],
            jax.ShapeDtypeStruct((8, width), f32),
            jax.ShapeDtypeStruct((8, 3 * cols), f32),
        ],
        compiler_params=pltpu.CompilerParams(vmem_limit_bytes=VMEM),
        cost_estimate=cost(10**6, 10**4),
        name=f"image_back_{stage}",
    )(buckets, which, kvq, lse, o, grad_o, vectors, tokens, weight, *old)


def rows_kernel(*refs, parts, dp_size, orders):
    refs = list(refs)
    take = lambda count: [refs.pop(0) for _ in range(count)]
    x_any, g_any, vec_ref, bias_any, o_any = take(5)
    shards, pieces = take(3), take(3)
    y_ref, e_ref, kept, sent, far_out, small_ref, do_out, wo_refs = *take(2), take(2), take(2), *take(3), take(2)
    pieces_to, across, across_to = take(3), take(2), take(2)
    quarters = [pieces + across, pieces_to + across_to]
    x_ref, g_ref, wo_w, up_w, down_w, hidden, normed, mixed, back, c_t, z_s, du_s, grads, came, do_s = take(15)
    far_came, far_next, wo_made, wo_came, o_in, bias_ref, g_t, dz_s, sems, far_sems, out_sems = take(11)
    rows, width = x_ref.shape
    hid = up_w.shape[2]
    step_index = pl.program_id(0)
    part = step_index ^ 2
    dp, me = lax.axis_index("dp"), lax.axis_index("tensor")
    quarter = dp % 4
    here = pl.ds(pl.multiple_of(me * rows, rows), rows)
    inputs = [
        pltpu.make_async_copy(x_any.at[here], x_ref, sems.at[4, 0]),
        pltpu.make_async_copy(g_any.at[here], g_ref, sems.at[4, 1]),
        pltpu.make_async_copy(o_any.at[:, here], o_in.at[0], sems.at[4, 7]),
        pltpu.make_async_copy(bias_any, bias_ref.at[0], sems.at[4, 8]),
    ]
    half, fourth = width // 2, width // 4
    partners = [(dp, me ^ r) for r in range(parts)]
    along = [(dp ^ (1 << order[0]), me) for order in orders]
    core = [send(grads.at[3 - 2 * i], came.at[i], far_sems, i, partners[1]) for i in range(2)]
    columns = [pl.ds(0, hid), pl.ds(hid, hid)]
    fars = [
        send(grads.at[2, pl.ds(half, half), columns[at]], far_came.at[at], far_sems, 2 + at, along[at]) for at in range(2)
    ]
    nexts = [
        send(grads.at[2, pl.ds(fourth, fourth), columns[at]], far_next.at[at], far_sems, 4 + at, along[1 - at])
        for at in range(2)
    ]
    mine = do_out.at[:, here]
    do_copies = [send(do_s.at[r], mine, far_sems, 5 + r, partners[r]) for r in range(parts - 1, 0, -1)]
    do_copies.append(pltpu.make_async_copy(do_s.at[0], mine, sems.at[4, 2]))
    results = [pltpu.make_async_copy(z_s, e_ref, sems.at[4, 3]), pltpu.make_async_copy(du_s, y_ref, sems.at[4, 4])]
    wo_copy = send(wo_made.at[1], wo_came, far_sems, 9, partners[1])

    beside, beyond = (dp ^ 1, me), (dp ^ 2, me)
    size = across[0].shape[0]
    across_in = [
        send(pieces[1].at[pl.ds(0, size)], across[0], out_sems, 0, beyond),
        send(pieces[2].at[pl.ds(size, across[1].shape[0])], across[1], out_sems, 1, beside),
    ]
    across_on = [send(across[i], across_to[i], out_sems, 2 + i, partners[1]) for i in range(2)]
    pieces_on = [send(pieces[i], pieces_to[i], out_sems, 4 + i, partners[1]) for i in range(3)]
    weights = (wo_w, up_w, down_w)
    shards_on = [send(shards[i], weights[i].at[1], out_sems, 7 + i, partners[1]) for i in range(3)]
    heads_in = []
    for r in range(parts - 1, 0, -1):
        theirs = pl.ds(pl.multiple_of((me ^ r) * rows, rows), rows)
        heads_in.append(send(o_any.at[:, theirs], o_in.at[r], out_sems, 9 + r, partners[r]))
        heads_in.append(send(bias_any, bias_ref.at[r], out_sems, 12 + r, partners[r]))

    def wide(block):
        return block.astype(f32)

    def add_into(target, source, count, columns=slice(None)):
        for start in range(0, count, 64):
            piece = slice(start, start + 64)
            target[piece, columns] = (wide(target[piece, columns]) + wide(source[piece, :])).astype(bf16)

    def loads(index, at):
        target, row = weights[index], index
        found = [[pltpu.make_async_copy(shards[index], target.at[0], sems.at[row, 0])], []]
        size = target.shape[1] // 4
        for r in (2, 3):
            found.append([])
            for i in range(4):
                piece, start = quarters[r - 2][i], at
                if i == 3 and at >= split:
                    piece, start = quarters[r - 2][4], at - split
                place = target.at[r, pl.ds(pl.multiple_of((quarter ^ i) * size, size), size)]
                sem = sems.at[row, 2 + 4 * (r - 2) + i]
                found[r].append(pltpu.make_async_copy(piece.at[pl.ds(start, size)], place, sem))
        return found

    mixed_cols = o_in.shape[1]
    split = (mixed_cols + hid) // 4
    groups = [loads(0, 0), loads(1, mixed_cols // 4), loads(2, split)]
    wo_loads, up_loads, down_loads = groups
    gain, shift = vec_ref[2:3, :].astype(f32), vec_ref[3:4, :].astype(f32)

    def store_own():
        return [
            pltpu.make_async_copy(
                grads.at[0, pl.ds(side * half, half), columns[at]], group[at], sems.at[3, 2 * side + at]
            )
            for side, group in enumerate((kept, sent))
            for at in range(2)
        ]

    def store_far():
        return [
            pltpu.make_async_copy(grads.at[2, pl.ds(0, fourth), columns[at]], far_out.at[at], sems.at[3, 4 + at])
            for at in range(2)
        ]

    def hidden_grads(r):
        for load in (down_loads[r] if r != 1 else shards_on[2:]):
            load.wait()
        for start in range(0, hid, 256):
            cols = slice(start, start + 256)
            dz_s[r, :, cols] = dot(g_ref[...], down_w[r, cols, :], NT).astype(bf16)

    @pl.when(step_index == 0)
    def _():
        for load in inputs:
            load.start()
        greet(partners[1:] + along)
        for copy in across_in + heads_in + shards_on[:1] + pieces_on + shards_on[1:]:
            copy.start()
        for group in groups:
            for load in group[0] + group[2][:3]:
                load.start()
        for load in inputs:
            load.wait()
        g_t[...] = dot(halving_order(orders[0], width, dp_size), g_ref[...], NT).astype(bf16)
        hidden_grads(0)
        for i in range(2):
            across_in[i].wait_recv()
            across_on[i].start()
        for group in groups:
            group[2][3].start()
        for i in range(3):
            pieces_on[i].wait()
        for group in groups:
            for load in group[3][:3]:
                load.start()
        hidden_grads(1)
        hidden_grads(2)
        for i in range(2):
            across_in[i].wait_send()
            across_on[i].wait()
        for group in groups:
            group[3][3].start()
        hidden_grads(3)
        shards_on[0].wait()
        for group in wo_loads:
            for load in group:
                load.wait()
        for copy in heads_in:
            copy.wait()
        for start in range(0, rows, 256):
            piece = slice(start, start + 256)
            attended = dot(o_in[0, :, piece], wo_w[0], TN)
            for r in range(1, parts):
                attended += dot(o_in[r, :, piece], wo_w[r], TN)
            h1 = x_ref[piece, :].astype(f32) + attended + vec_ref[4:5, :].astype(f32)
            hidden[piece, :] = h1
            unit, _ = unit_rows(h1)
            normed[piece, :] = (unit * gain + shift).astype(bf16)
        c_t[...] = dot(halving_order(orders[1], width, dp_size), normed[...], NT).astype(bf16)
        mixed[...] = jnp.zeros_like(mixed)
        back[...] = jnp.zeros_like(back)
        small_ref[...] = jnp.zeros_like(small_ref)

    for r in range(parts):

        @pl.when(part == r)
        def _():
            for load in (up_loads[r] if r != 1 else shards_on[1:2]):
                load.wait()

    step = 256
    chunks = [slice(s, s + step) for s in range(0, hid, step)]

    def first(cols):
        u = dot(normed[...], up_w[part, :, cols]) + bias_ref[part, 0:1, cols]
        return u, wide(dz_s[part, :, cols])

    def bend(cols, u, dz):
        square = u * u
        scaled = u * GELU_SCALE
        gate = 0.5 + 0.5 * jnp.tanh(scaled * (1.0 + GELU_CUBE * square))
        z_s[:, cols] = (u * gate).astype(bf16)
        slope = gate + (2.0 * gate) * (1.0 - gate) * scaled * (1.0 + (3.0 * GELU_CUBE) * square)
        du = (dz * slope).astype(bf16)
        du_s[:, cols] = du
        small_ref[pl.ds(8 + part, 1), cols] = jnp.sum(du.astype(f32), axis=0, keepdims=True)

    def weigh(cols):
        grads[part, :, cols] = dot(g_t[...], z_s[:, cols]).astype(bf16)
        later = slice(hid + cols.start, hid + cols.stop)
        grads[part, :, later] = dot(c_t[...], du_s[:, cols]).astype(bf16)

    ready = first(chunks[0])
    for index, cols in enumerate(chunks):
        following = first(chunks[index + 1]) if index + 1 < len(chunks) else None
        bend(cols, *ready)
        if index:
            weigh(chunks[index - 1])
        ready = following
    mixed[...] += dot(z_s[...], down_w[part])
    weigh(chunks[-1])
    back[...] += dot(du_s[...], up_w[part], NT)
    @pl.when(part == 3)
    def _():
        core[0].start()

    @pl.when(part == 0)
    def _():
        core[0].wait()
        add_into(grads.at[2], came.at[0], width)
        for copy in fars:
            copy.start()

    @pl.when(part == 1)
    def _():
        core[1].start()
        totals = [jnp.zeros((1, width), f32)] * 4
        for start in range(0, rows, 256):
            piece = slice(start, start + 256)
            h1 = hidden[piece, :]
            unit, inverse = unit_rows(h1)
            dc = back[piece, :]
            wide_g = wide(g_ref[piece, :])
            dh = wide_g + norm_back(dc, gain, unit, inverse)
            z_s[piece, :] = dh.astype(bf16)
            du_s[piece, :] = (h1 + mixed[piece, :] + vec_ref[5:6, :].astype(f32)).astype(bf16)
            news = [jnp.sum(values, axis=0, keepdims=True) for values in (dc * unit, dc, dh, wide_g)]
            totals = [old + new for old, new in zip(totals, news)]
        for index, values in enumerate(totals):
            small_ref[2 + index : 3 + index, :] = values
        results[1].start()
        e = z_s[...]
        results[0].start()
        for r in range(parts):
            do_s[r] = dot(wo_w[r], e, NT).astype(bf16)
        for copy in do_copies:
            copy.start()
        for at in range(2):
            fars[at].wait()
            add_into(grads.at[2], far_came.at[at], half, columns[at])
            nexts[at].start()
        e_t = dot(halving_order(orders[0], width, dp_size), e, NT).astype(bf16)
        blank = jnp.zeros((width, 256 - mixed_cols), bf16)
        for r in range(parts):
            wo_made[r % 2, r // 2] = jnp.concatenate([dot(e_t, o_in[r], NT).astype(bf16), blank], axis=1)
        wo_copy.start()
        core[1].wait()
        add_into(grads.at[0], came.at[1], width)
        for copy in store_own():
            copy.start()
        for at in range(2):
            nexts[at].wait()
            add_into(grads.at[2], far_next.at[at], fourth, columns[at])
        for copy in store_far():
            copy.start()
        wo_copy.wait()
        for index in range(2):
            add_into(wo_made.at[0, index], wo_came.at[index], width)
        wo_stores = [
            pltpu.make_async_copy(wo_made.at[0, index], wo_refs[index], sems.at[4, 5 + index]) for index in range(2)
        ]
        for copy in wo_stores:
            copy.start()
        for copy in store_own() + store_far() + do_copies + results + wo_stores:
            copy.wait()


def own_rows(x, g, vectors, up_bias, o, shards, pieces, parts, dp_size, orders):
    cols = o.shape[0]
    rows = x.shape[0] // parts
    width = x.shape[1]
    hid = shards[1].shape[1]
    tall = pieces[0].shape[0]
    split = tall - hid // 4
    fixed = lambda shape: pl.BlockSpec(shape, lambda r: (0,) * len(shape))
    array = lambda *shape: jax.ShapeDtypeStruct(shape, bf16)
    out = pl.pallas_call(
        functools.partial(rows_kernel, parts=parts, dp_size=dp_size, orders=orders),
        grid=(parts,),
        in_specs=[
            ANY,
            ANY,
            fixed(vectors.shape),
        ]
        + [ANY] * 8,
        out_specs=[ANY] * 7 + [fixed((16, width)), ANY] + [ANY] * 9,
        out_shape=[array(rows, width)] * 2
        + [array(width // 2, hid)] * 4
        + [array(2, width // 4, hid)]
        + [jax.ShapeDtypeStruct((16, width), f32), array(cols, x.shape[0])]
        + [array(width, 256)] * 2
        + [array(tall, width)] * 3
        + [array(split, width), array(tall - split, width)] * 2,
        scratch_shapes=[
            pltpu.VMEM((rows, width), bf16),
            pltpu.VMEM((rows, width), bf16),
            pltpu.VMEM((parts, cols, width), bf16),
            pltpu.VMEM((parts, width, hid), bf16),
            pltpu.VMEM((parts, hid, width), bf16),
            pltpu.VMEM((rows, width), f32),
            pltpu.VMEM((rows, width), bf16),
            pltpu.VMEM((rows, width), f32),
            pltpu.VMEM((rows, width), f32),
            pltpu.VMEM((width, rows), bf16),
            pltpu.VMEM((rows, hid), bf16),
            pltpu.VMEM((rows, hid), bf16),
            pltpu.VMEM((parts, width, 2 * hid), bf16),
            pltpu.VMEM((2, width, 2 * hid), bf16),
            pltpu.VMEM((parts, cols, rows), bf16),
            pltpu.VMEM((2, width // 2, hid), bf16),
            pltpu.VMEM((2, width // 4, hid), bf16),
            pltpu.VMEM((2, 2, width, 256), bf16),
            pltpu.VMEM((2, width, 256), bf16),
            pltpu.VMEM((parts, cols, rows), bf16),
            pltpu.VMEM((parts,) + up_bias.shape, f32),
            pltpu.VMEM((width, rows), bf16),
            pltpu.VMEM((parts, rows, hid), bf16),
            pltpu.SemaphoreType.DMA((5, 12)),
            pltpu.SemaphoreType.DMA((2, 10)),
            pltpu.SemaphoreType.DMA((2, 16)),
        ],
        compiler_params=pltpu.CompilerParams(collective_id=4, has_side_effects=True, vmem_limit_bytes=VMEM),
        cost_estimate=cost(12 * rows * width * hid * parts, 8 * parts * width * hid, rows * hid * parts),
        name="own_rows",
    )(x, g, vectors, up_bias, o, *shards, *pieces)
    return out[0], out[1], out[2:4], out[4:6], out[6], out[7], out[8], out[9:11]


def greet(partners):
    barrier = pltpu.get_barrier_semaphore()
    for partner in partners:
        pl.semaphore_signal(barrier, inc=1, device_id=partner, device_id_type=pl.DeviceIdType.MESH)
    pl.semaphore_wait(barrier, len(partners))


def send(source, target, sems, index, partner):
    return pltpu.make_async_remote_copy(
        src_ref=source,
        dst_ref=target,
        send_sem=sems.at[0, index],
        recv_sem=sems.at[1, index],
        device_id=partner,
        device_id_type=pl.DeviceIdType.MESH,
    )


def pick_kernel(*refs):
    *sources, target, sems = refs
    quarter = lax.axis_index("dp") % 4
    copies, at = [], 0
    for index, source in enumerate(sources):
        size = source.shape[0] // 4
        piece = source.at[pl.ds(pl.multiple_of(quarter * size, size), size)]
        copies.append(pltpu.make_async_copy(piece, target.at[pl.ds(at, size)], sems.at[index]))
        copies[index].start()
        at += size
    for copy in copies:
        copy.wait()


def pick_quarter(shards):
    rows = sum(shard.shape[0] for shard in shards) // 4
    return pl.pallas_call(
        pick_kernel,
        in_specs=[ANY] * len(shards),
        out_specs=pl.BlockSpec(memory_space=pltpu.VMEM),
        out_shape=jax.ShapeDtypeStruct((rows, shards[0].shape[1]), bf16),
        scratch_shapes=[pltpu.SemaphoreType.DMA((len(shards),))],
        name="pick_quarter",
    )(*shards)


def finish_kernel(
    own_any, mid_any, far_own_any, mid_keep_any, mid_came_any, x_any, dh_any, vec_ref, late_ref, bias_ref, early_ref, *refs,
    dp_size, tracks,
):
    bits = dp_size.bit_length() - 1
    refs = list(refs)
    take = lambda count: [refs.pop(0) for _ in range(count)]
    weights = [take(1), take(1), take(2), take(2), take(2)]
    (out_ref,) = take(1)
    weights_out = take(len(tracks))
    (sums_out,) = take(1)
    held, other, far_own, mid_keep, mid_came, far_mid, x_v, dh_v = take(8)
    sent = [take(len(order)) for order in tracks]
    got = [take(len(order)) for order in tracks]
    totals = take(len(tracks))
    sums, got_s, sems, w_sems, local = refs
    dp, me = lax.axis_index("dp"), lax.axis_index("tensor")
    core, side = me % 2, me // 2
    rows, width = out_ref.shape
    image_len = own_any.shape[0]
    half = image_len // 2
    x_own = x_any.at[pl.ds(pl.multiple_of(me * rows, rows), rows)]
    at_own = side * half
    at_mid = (1 - side) * image_len
    across = [(dp, me ^ 1), (dp, me ^ 2)]
    along = [(dp ^ (1 << bit), me) for bit in range(bits)]
    greet(across + along)

    loads = [
        pltpu.make_async_copy(own_any, held.at[pl.ds(pl.multiple_of(at_own, half), image_len)], local.at[0]),
        pltpu.make_async_copy(mid_any, held.at[pl.ds(pl.multiple_of(at_mid, half), half)], local.at[1]),
        pltpu.make_async_copy(far_own_any, far_own, local.at[2]),
        pltpu.make_async_copy(mid_keep_any, mid_keep, local.at[3]),
        pltpu.make_async_copy(mid_came_any, mid_came, local.at[6]),
        pltpu.make_async_copy(x_own, x_v, local.at[4]),
        pltpu.make_async_copy(dh_any, dh_v, local.at[5]),
    ]
    for load in loads:
        load.start()
    mid_load = loads.pop(4)
    mid_load.wait()
    loads[3].wait()
    mid_keep[...] = (mid_keep[...].astype(f32) + mid_came[...].astype(f32)).astype(bf16)

    copies = [[] for _ in tracks]
    tall = [totals[track].shape[0] for track in range(len(tracks))]

    def first(track, here):
        terms = [term[here, :].astype(f32) for term in weights[track]]
        return terms[0] + terms[1] if len(terms) > 1 else terms[0]

    def send_weight(track, step):
        target = sent[track][step]
        span = tall[track] // 2
        if step == 0:
            target[...] = first(track, slice(span, 2 * span)).astype(target.dtype)
        else:
            target[...] = totals[track][span : 2 * span, :].astype(target.dtype)
        route = along[tracks[track][step]]
        index = sum(len(order) for order in tracks[:track]) + step
        copies[track].append(send(target, got[track][step], w_sems, index, route))
        copies[track][step].start()

    def add_weight(track, step):
        copies[track][step].wait()
        tall[track] //= 2
        span = tall[track]
        kept = totals[track][0:span, :] if step else first(track, slice(0, span))
        totals[track][0:span, :] = kept + got[track][step][...].astype(f32)

    for track in range(len(tracks)):
        if tracks[track]:
            send_weight(track, 0)
    mid_copy = send(mid_keep, far_mid, sems, 14, across[1])

    sums[...] = early_ref[...]
    sums[0:2, :] = late_ref[0:2, :]
    sums[12:13, 0 : bias_ref.shape[1]] = bias_ref[0:1, :]
    routes = across + along
    s_copies = []

    def send_sums(step):
        s_copies.append(send(sums, got_s.at[step], sems, step, routes[step]))
        s_copies[step].start()

    def add_sums(step):
        s_copies[step].wait()
        if step < 2:
            sums[0:6, :] += got_s[step, 0:6, :]
            new = [sums[8 + r : 9 + r, :] + got_s[step, 8 + (r ^ (1 << step)) : 9 + (r ^ (1 << step)), :] for r in range(4)]
            for r in range(4):
                sums[8 + r : 9 + r, :] = new[r]
        else:
            sums[...] += got_s[step]

    def turn(track, step):
        add_weight(track, step)
        if step + 1 < len(tracks[track]):
            send_weight(track, step + 1)

    mid_copy.start()
    send_sums(0)
    for load in loads[:3]:
        load.wait()
    here = pl.ds(pl.multiple_of(at_own + core * half, half), half)
    held[here, :] = (held[here, :].astype(f32) + far_own[...].astype(f32)).astype(bf16)
    turn(0, 0)
    add_sums(0)
    send_sums(1)
    turn(1, 0)
    turn(2, 0)
    add_sums(1)
    send_sums(2)
    turn(0, 1)
    mid_copy.wait()

    here = pl.ds(pl.multiple_of(at_mid + core * (half // 2), half // 2), half // 2)
    held[here, :] = (held[here, :].astype(f32) + far_mid[...].astype(f32)).astype(bf16)
    theirs = held.at[pl.ds(pl.multiple_of((1 - core) * rows, rows), rows)]
    da_copy = send(theirs, other, sems, 15, across[0])
    da_copy.start()
    turn(1, 1)
    turn(2, 1)
    add_sums(2)
    if bits > 1:
        send_sums(3)
    for load in loads[4:]:
        load.wait()
    da_copy.wait()
    gain = vec_ref[0:1, :].astype(f32)
    step = 256
    for start in range(0, rows, step):
        piece = slice(start, start + step)
        unit, inverse = unit_rows(x_v[piece, :].astype(f32))
        mine = held[pl.ds(pl.multiple_of(core * rows + start, step), step), :].astype(f32)
        da = mine + other[piece, :].astype(f32)
        out_ref[piece, :] = (dh_v[piece, :].astype(f32) + norm_back(da, gain, unit, inverse)).astype(bf16)

    for step in range(2, bits):
        for track in range(3):
            turn(track, step)
        add_sums(1 + step)
        if step < bits:
            send_sums(2 + step)
    add_sums(1 + bits)
    for step in range(bits):
        for track in (3, 4):
            if step < len(tracks[track]):
                turn(track, step)
    for track in range(len(tracks)):
        if tracks[track]:
            weights_out[track][...] = totals[track][0 : weights_out[track].shape[0], :]
        else:
            weights_out[track][...] = first(track, slice(None))
    sums_out[...] = sums[...]


def unpack_kernel(out_ref, dw_one, dw_two, wo_in, down_ref, up_ref, sums_ref, out_to, qkv_to, wo_to, down_to, up_to, bias_to):
    out_to[...] = out_ref[...]
    down_to[...] = down_ref[...]
    up_to[...] = up_ref[...]
    cols = wo_to.shape[0]
    dw_ref = jnp.concatenate([dw_one[...], dw_two[...]], axis=1)
    for index, at in enumerate((2, 0, 1)):
        qkv_to[index] = dw_ref[:, at * cols : (at + 1) * cols]
    wo_to[...] = jnp.transpose(wo_in[...])[0:cols]
    for index, at in enumerate((2, 1)):
        bias_to[index : index + 1, :] = sums_ref[12:13, at * cols : (at + 1) * cols]


def unpack(out, dw_one, dw_two, wo, down, up, sums, cols):
    rows = dw_one.shape[0]
    vmem = pl.BlockSpec(memory_space=pltpu.VMEM)
    array = lambda *shape: jax.ShapeDtypeStruct(shape, f32)
    return pl.pallas_call(
        unpack_kernel,
        in_specs=[vmem] * 7,
        out_specs=[vmem] * 6,
        out_shape=[
            jax.ShapeDtypeStruct(out.shape, bf16),
            array(3, rows, cols),
            array(cols, rows),
            array(*down.shape),
            array(*up.shape),
            array(2, cols),
        ],
        compiler_params=pltpu.CompilerParams(vmem_limit_bytes=VMEM),
        name="unpack",
    )(out, dw_one, dw_two, wo, down, up, sums)


def finish(own, mid, far_own, mid_keep, mid_came, x, dh, vectors, late, bias, early, weights, tracks, dp_size):
    rows, width = dh.shape
    bits = dp_size.bit_length() - 1
    buffers, totals = [], []
    for group, order in zip(weights, tracks):
        tall, wide = group[0].shape[-2:]
        totals.append(pltpu.VMEM((tall, wide), f32))
        for bit in order:
            tall //= 2
            buffers.append(pltpu.VMEM((tall, wide), bf16 if tall % 16 == 0 else f32))
    count = sum(len(order) for order in tracks)
    flat = [weight for group in weights for weight in group]
    vmem = pl.BlockSpec(memory_space=pltpu.VMEM)
    return pl.pallas_call(
        functools.partial(finish_kernel, dp_size=dp_size, tracks=tracks),
        in_specs=[ANY] * 7 + [vmem] * (4 + len(flat)),
        out_specs=[vmem] * (2 + len(tracks)),
        out_shape=[jax.ShapeDtypeStruct((rows, width), bf16)]
        + [jax.ShapeDtypeStruct((width // dp_size, group[0].shape[-1]), f32) for group in weights]
        + [jax.ShapeDtypeStruct((16, width), f32)],
        scratch_shapes=[
            pltpu.VMEM((2 * rows, width), bf16),
            pltpu.VMEM((rows, width), bf16),
            pltpu.VMEM(far_own.shape, bf16),
            pltpu.VMEM(mid_keep.shape, bf16),
            pltpu.VMEM(mid_keep.shape, bf16),
            pltpu.VMEM(mid_keep.shape, bf16),
            pltpu.VMEM((rows, width), bf16),
            pltpu.VMEM((rows, width), bf16),
        ]
        + buffers * 2
        + totals
        + [
            pltpu.VMEM((16, width), f32),
            pltpu.VMEM((2 + bits, 16, width), f32),
            pltpu.SemaphoreType.DMA((2, 16)),
            pltpu.SemaphoreType.DMA((2, count)),
            pltpu.SemaphoreType.DMA((7,)),
        ],
        compiler_params=pltpu.CompilerParams(
            collective_id=3, has_side_effects=True, vmem_limit_bytes=VMEM
        ),
        name="finish",
    )(own, mid, far_own, mid_keep, mid_came, x, dh, vectors, late, bias, early, *flat)


def on_device(
    dp_size, tokens, buckets, norm1_gain, norm1_bias, qkv_weight, qkv_bias, out_weight, out_bias,
    norm2_gain, norm2_bias, up_weight, up_bias, down_weight, down_bias, cotangent,
):
    parts = 4
    dp_bits = dp_size.bit_length() - 1
    me = lax.axis_index("tensor")
    token_rows, width = tokens.shape
    share = token_rows // parts
    hid = up_weight.shape[1]
    cols = qkv_weight.shape[2]

    def over_tensor(values, mask):
        return lax.ppermute(values, "tensor", [(i, i ^ mask) for i in range(parts)])

    def over_dp(values, mask):
        return lax.ppermute(values, "dp", [(i, i ^ mask) for i in range(dp_size)])

    def add(*terms):
        total = terms[0].astype(f32)
        for term in terms[1:]:
            total = total + term.astype(f32)
        return total.astype(bf16)

    shards = (out_weight, up_weight, down_weight)
    near = over_tensor(pick_quarter(shards), 2)
    blank = jnp.zeros_like(norm1_gain)
    vectors = jnp.stack(
        [norm1_gain, norm1_bias, norm2_gain, norm2_bias, out_bias, down_bias, blank, blank]
    )
    up_bias_rows = jnp.broadcast_to(up_bias.astype(f32)[None], (8, hid))
    orders = [list(range(dp_bits)), [1, 0] + list(range(2, dp_bits))]
    turned_weight = jnp.swapaxes(qkv_weight, 1, 2)
    kvq, bound = project(tokens, vectors, turned_weight, qkv_bias)
    near, kvq = lax.optimization_barrier((near, kvq))
    beside, along = over_dp(near, 1), over_dp(near, 2)
    o, lse = attend(buckets, kvq, bound)
    near, beside, along, o = lax.optimization_barrier((near, beside, along, o))
    layer_out, e, kept, sent, far, early, grad_o, grad_wo = own_rows(
        tokens, cotangent, vectors, up_bias_rows, o, shards, (near, beside, along), parts, dp_size, orders
    )

    tie = lax.optimization_barrier
    got = [over_dp(half, 1 << order[0]) for half, order in zip(sent, orders)]
    crossed, wo_far = over_tensor(far, 2), over_tensor(grad_wo[1], 2)

    side = me // 2
    order = [2 - 2 * side, jnp.ones_like(side), 2 * side]
    run = lambda stage, old, o: image_back(
        stage, buckets, order[stage].reshape(1).astype(jnp.int32), kvq, lse, o, grad_o, vectors, tokens, turned_weight,
        dp_size, orders, old,
    )
    da_keep, da_send, *old = run(0, [], o)
    came, first_keep = over_tensor(da_send, 1), da_keep
    *got, o = tie((*got, o, *old))[:3]
    split = width // 4
    sent = [add(k[split:], g[split:]) for k, g in zip(kept, got)]
    kept = [add(k[:split], g[:split]) for k, g in zip(kept, got)]
    got = [over_dp(half, 1 << order[1]) for half, order in zip(sent, orders)]
    mid_keep, da_send, mid, *old = run(1, old, o)
    came, o, wo_far, crossed, *got = tie((came, o, wo_far, crossed, *got, *old))[:6]
    far_own = over_tensor(add(first_keep, came), 2)
    mid_came = over_tensor(da_send, 1)
    split //= 2
    terms = list(zip(kept, got, crossed))
    sent = jnp.stack([add(*[t[split:] for t in group]) for group in terms])
    kept = [add(*[t[:split] for t in group]) for group in terms]
    got = over_dp(sent, 1 << orders[0][2])
    own, *dw, late, bias_sums = run(2, old, o)
    got, far_own, mid_came, own, wo_far = tie((got, far_own, mid_came, own, wo_far))
    weights = [dw[:1], dw[1:], [grad_wo[0], wo_far]] + [[k, g] for k, g in zip(kept, got)]
    tracks = [orders[0], orders[1], orders[0], orders[0][3:], orders[1][3:]]
    out, dw_one, dw_two, wo_out, down_out, grad_up, sums = finish(
        own, mid, far_own, mid_keep, mid_came, tokens, e, vectors, late, bias_sums, early, weights, tracks, dp_size
    )
    input_grad, grad_qkv_weight, grad_out, down_out, grad_up, grad_qkv_bias = unpack(
        out, dw_one, dw_two, wo_out, down_out, grad_up, sums, cols
    )
    grad_down = down_out.T
    return (
        layer_out,
        input_grad,
        sums[0],
        sums[1],
        grad_qkv_weight,
        grad_qkv_bias,
        grad_out,
        sums[4],
        sums[2],
        sums[3],
        grad_up,
        sums[8],
        grad_down,
        sums[5],
    )


def solution(mesh):
    return jax.shard_map(
        functools.partial(on_device, mesh.shape["dp"]),
        mesh=mesh,
        in_specs=(
            P("dp", None),
            P("dp"),
            P(),
            P(),
            P(None, None, "tensor"),
            P(None, "tensor"),
            P("tensor", None),
            P(),
            P(),
            P(),
            P(None, "tensor"),
            P("tensor"),
            P("tensor", None),
            P(),
            P("dp", None),
        ),
        out_specs=(
            P(("dp", "tensor"), None),
            P(("dp", "tensor"), None),
            P(),
            P(),
            P(None, "dp", "tensor"),
            P(None, "tensor"),
            P("tensor", "dp"),
            P(),
            P(),
            P(),
            P("dp", "tensor"),
            P("tensor"),
            P("tensor", "dp"),
            P(),
        ),
        check_vma=False,
    )
```

```python
import functools

import jax
import jax.numpy as jnp
from jax import lax
from jax.experimental import pallas as pl
from jax.experimental.pallas import tpu as pltpu
from jax.sharding import PartitionSpec as P

DH = 64
NORM_EPSILON = 1e-06
GRID_SIXTEENTHS = (16, 15, 15, 12, 12, 8, 8, 6, 6)
GELU_SCALE = 0.7978845608028654
GELU_CUBE = 0.044715
VMEM = 60 << 20
NN = (((1,), (0,)), ((), ()))
NT = (((1,), (1,)), ((), ()))
TN = (((0,), (0,)), ((), ()))
bf16 = jnp.bfloat16
f32 = jnp.float32
ANY = pl.BlockSpec(memory_space=pl.ANY)


def dot(left, right, dims=NN):
    return lax.dot_general(left, right, dims, preferred_element_type=f32)


def lanes(rows, width):
    return lax.broadcasted_iota(jnp.int32, (rows, width), 1)


def live_lengths(image_len):
    return sorted({image_len * s // 16 for s in GRID_SIXTEENTHS})


def live_length(bucket, image_len):
    length = jnp.int32(0)
    for index, sixteenths in enumerate(GRID_SIXTEENTHS):
        length = jnp.where(bucket == index, image_len * sixteenths // 16, length)
    return length


def cost(flops, nbytes, transcendentals=0):
    return pl.CostEstimate(flops=flops, bytes_accessed=nbytes, transcendentals=transcendentals)


def split3(values):
    high = values.astype(bf16).astype(f32)
    middle = (values - high).astype(bf16).astype(f32)
    return high, middle, values - high - middle


def halving_order(order, width, dp_size):
    bits = dp_size.bit_length() - 1
    size = width // dp_size
    place = lax.broadcasted_iota(jnp.int32, (width, 128), 0)
    block = jnp.zeros_like(place)
    for index in range(1, dp_size):
        block = block + (place >= index * size).astype(jnp.int32)
    turned = jnp.zeros_like(block)
    for step, bit in enumerate(order):
        turned = turned | (((block >> (bits - 1 - step)) & 1) << bit)
    source = (turned ^ lax.axis_index("dp")) * size + (place - block * size)
    lane = lanes(width, 128)
    return jnp.concatenate(
        [jnp.where(source == lane + start, 1.0, 0.0).astype(bf16) for start in range(0, width, 128)], axis=1
    )


def unit_rows(values):
    centred = values - jnp.mean(values, axis=-1, keepdims=True)
    spread = jnp.mean(centred * centred, axis=-1, keepdims=True)
    inverse = lax.rsqrt(spread + NORM_EPSILON)
    return centred * inverse, inverse


def norm_back(grad, gain, unit, inverse):
    scaled = grad * gain
    mean_one = jnp.mean(scaled, axis=-1, keepdims=True)
    mean_two = jnp.mean(scaled * unit, axis=-1, keepdims=True)
    return inverse * (scaled - mean_one - unit * mean_two)


def project_kernel(x_ref, vec_ref, w_ref, bias_ref, out_ref, bound_ref, w_all):
    cols = w_ref.shape[1]

    @pl.when(pl.program_id(0) == 0)
    def _():
        for index, source in enumerate((1, 2, 0)):
            w_all[index * cols : (index + 1) * cols, :] = w_ref[source]

    gain, shift = vec_ref[0:1, :].astype(f32), vec_ref[1:2, :].astype(f32)
    bias = bias_ref[...].astype(f32)
    bias = jnp.concatenate([jnp.zeros((1, cols), f32), bias[1:2], bias[0:1]], axis=1)
    rows, step = x_ref.shape[0], 128
    row = lax.broadcasted_iota(jnp.int32, (3 * cols, 128), 0)
    pick = jnp.where(row // DH == lanes(3 * cols, 128), 1.0, 0.0).astype(bf16)

    def normed(start):
        unit, _ = unit_rows(x_ref[start : start + step, :].astype(f32))
        return (unit * gain + shift).astype(bf16)

    largest = None
    ready = normed(0)
    for start in range(0, rows, step):
        following = normed(start + step) if start + step < rows else None
        values = (dot(ready, w_all[...], NT) + bias).astype(bf16)
        out_ref[start : start + step, :] = values
        squares = jnp.max(dot(values * values, pick), axis=0, keepdims=True)
        largest = squares if largest is None else jnp.maximum(largest, squares)
        ready = following
    bound_ref[0] = jnp.broadcast_to(largest, (8, 128))


def project(tokens, vectors, weight, bias):
    rows, width = tokens.shape
    cols = weight.shape[1]
    block = 512
    fixed = lambda shape: pl.BlockSpec(shape, lambda i: (0,) * len(shape))
    return pl.pallas_call(
        project_kernel,
        grid=(rows // block,),
        in_specs=[
            pl.BlockSpec((block, width), lambda i: (i, 0)),
            fixed(vectors.shape),
            fixed(weight.shape),
            fixed(bias.shape),
        ],
        out_specs=[
            pl.BlockSpec((block, 3 * cols), lambda i: (i, 0)),
            pl.BlockSpec((1, 8, 128), lambda i: (i, 0, 0)),
        ],
        out_shape=[
            jax.ShapeDtypeStruct((rows, 3 * cols), bf16),
            jax.ShapeDtypeStruct((rows // block, 8, 128), f32),
        ],
        scratch_shapes=[pltpu.VMEM((3 * cols, width), bf16)],
        compiler_params=pltpu.CompilerParams(vmem_limit_bytes=VMEM),
        cost_estimate=cost(6 * rows * width * cols, 2 * rows * (width + 3 * cols)),
        name="project",
    )(tokens, vectors, weight, bias)


def attend_kernel(bucket_ref, kvq_ref, bound_ref, o_ref, lse_ref, kx, vt, *, block):
    cols, image_len = o_ref.shape
    heads = cols // DH
    at_q = 2 * cols
    length = live_length(bucket_ref[pl.program_id(0)], image_len)
    squares = jnp.max(bound_ref[...], axis=0)
    lane = lanes(8, 128)
    largest_key = jnp.max(jnp.where(lane < heads, squares, 0.0))
    of_query = (lane >= 2 * heads) & (lane < 3 * heads)
    largest_query = jnp.max(jnp.where(of_query, squares, 0.0))
    small = largest_key * largest_query <= (8.0 * 60.0) ** 2

    def run(live, subtract):
        scaled = kvq_ref[0:live, 0:192] * jnp.asarray(0.125, bf16)
        flipped = jnp.transpose(kvq_ref[0:live, 128:384])
        lane = lanes(live, 128)
        for h in range(heads):
            if h < 2:
                keep = (lane < DH) if h == 0 else (lane >= DH)
                kx[h, 0:live, :] = jnp.where(keep, scaled[:, 0:128], jnp.zeros((), bf16))
            else:
                kx[h, 0:live, 0:DH] = scaled[:, 128:192]
            vt[h, 0:DH, 0:live] = flipped[DH * (h + 1) : DH * (h + 2)]
            vt[h, DH:128, 0:live] = jnp.ones((DH, live), bf16)

        def scores(h, start):
            here = slice(start, start + block)
            if h < 2:
                return dot(kx[h, 0:live, :], kvq_ref[here, at_q : at_q + 128], NT)
            return dot(kx[h, 0:live, 0:DH], kvq_ref[here, at_q + 128 : at_q + 192], NT)

        parts = {}

        def finish(h, start, score):
            offset = 0.0
            if subtract:
                key = lax.broadcasted_iota(jnp.int32, score.shape, 0)
                score = jnp.where(key < length, score, -1e30)
                offset = jnp.max(score, axis=0, keepdims=True)
                score = score - offset
            mixed = dot(vt[h, :, 0:live], jnp.exp(score).astype(bf16))
            total = mixed[DH : DH + 1]
            here = slice(start, start + block)
            parts[h] = -(offset + jnp.log(total))
            o_ref[DH * h : DH * (h + 1), here] = (mixed[:DH] * (1.0 / total)).astype(bf16)
            if h == heads - 1:
                rows = [parts[i] for i in range(heads)]
                lse_ref[:, here] = jnp.concatenate(rows + [jnp.zeros((8 - heads, block), f32)], axis=0)

        items = [(h, s) for s in range(0, image_len, block) for h in range(heads)]
        score = scores(*items[0])
        for index, item in enumerate(items):
            following = scores(*items[index + 1]) if index + 1 < len(items) else None
            finish(*item, score)
            score = following

    for live in live_lengths(image_len):
        pl.when(small & (length == live))(functools.partial(run, live, False))
    pl.when(jnp.logical_not(small))(functools.partial(run, image_len, True))


def attend(buckets, kvq, bound):
    rows = kvq.shape[0]
    cols = kvq.shape[1] // 3
    images = buckets.shape[0]
    image_len = rows // images
    heads = cols // DH
    by_rows = lambda w: pl.BlockSpec((image_len, w), lambda i, b: (i, 0))
    by_cols = lambda w: pl.BlockSpec((w, image_len), lambda i, b: (0, i))
    return pl.pallas_call(
        functools.partial(attend_kernel, block=512),
        grid_spec=pltpu.PrefetchScalarGridSpec(
            num_scalar_prefetch=1,
            grid=(images,),
            in_specs=[by_rows(3 * cols), pl.BlockSpec(bound.shape, lambda i, b: (0, 0, 0))],
            out_specs=[by_cols(cols), by_cols(8)],
            scratch_shapes=[
                pltpu.VMEM((heads, image_len, 128), bf16),
                pltpu.VMEM((heads, 128, image_len), bf16),
            ],
        ),
        out_shape=[
            jax.ShapeDtypeStruct((cols, rows), bf16),
            jax.ShapeDtypeStruct((8, rows), f32),
        ],
        compiler_params=pltpu.CompilerParams(vmem_limit_bytes=VMEM),
        cost_estimate=cost(16 * rows * image_len * cols, 12 * rows * cols, rows * image_len * heads),
        name="attend",
    )(buckets, kvq, bound)


def image_back_kernel(bucket_ref, which_ref, kvq_ref, lse_ref, o_ref, do_ref, vec_ref, *refs, block, stage, dp_size, orders):
    refs = list(refs)
    take = lambda count: [refs.pop(0) for _ in range(count)]
    x_any, w_any = take(2)
    old = take(3) if stage else None
    outs = take((2, 3, 1)[stage])
    dw_outs = take(2 if stage == 2 else 1)
    small_out, bias_out = take(2)
    dox, dot_t, qx, q_t, kx, vx, k_t, grad_q, grads, x, w_all, da_s, normed, dw, sems = take(15)
    cols, image_len = o_ref.shape
    heads = cols // DH
    image = which_ref[0]
    loads = [
        pltpu.make_async_copy(x_any.at[pl.ds(image * image_len, image_len)], x, sems.at[0]),
    ]
    for index, source in enumerate((1, 2, 0)):
        target = w_all.at[pl.ds(index * cols, cols)]
        loads.append(pltpu.make_async_copy(w_any.at[source], target, sems.at[7 + index]))
    if stage:
        loads.append(pltpu.make_async_copy(old[0], dw, sems.at[3]))
    for load in loads:
        load.start()
    length = live_length(bucket_ref[image], image_len)
    inner = []
    for h in range(heads):
        own = slice(DH * h, DH * (h + 1))
        product = do_ref[own, :].astype(f32) * o_ref[own, :].astype(f32)
        inner += list(split3(-jnp.sum(product, axis=0, keepdims=True)))
    blank = [jnp.zeros((DH - 3 * heads, image_len), f32)]
    dot_t[0:cols, :] = do_ref[...]
    dot_t[cols:, :] = jnp.concatenate(inner + blank, axis=0).astype(bf16)
    dox[...] = jnp.transpose(dot_t[...])
    outer = [part for h in range(heads) for part in split3(lse_ref[h : h + 1, :])]
    row = lax.broadcasted_iota(jnp.int32, (DH - 3 * heads, image_len), 0)
    outer = jnp.concatenate(outer + [jnp.where(row == 0, 1.0, 0.0)], axis=0).astype(bf16)
    q = kvq_ref[:, 2 * cols : 3 * cols]
    q_t[0:cols, :] = jnp.transpose(q)
    q_t[cols:, :] = outer
    qx[...] = jnp.concatenate([q, jnp.transpose(outer)], axis=1)
    scaled = kvq_ref[:, 0:cols] * jnp.asarray(0.125, bf16)
    values = kvq_ref[:, cols : 2 * cols]
    k_t[0:cols, :] = jnp.transpose(scaled)
    lane, side = lanes(image_len, cols), lanes(image_len, DH)
    key = lax.broadcasted_iota(jnp.int32, (image_len, DH), 0)
    zero = jnp.zeros((), bf16)
    for h in range(heads):
        keep = (lane >= DH * h) & (lane < DH * (h + 1))
        ones = jnp.where((side >= 3 * h) & (side < 3 * h + 3), 1.0, 0.0)
        dead = jnp.where((side == 3 * heads) & (key >= length), -1e30, ones).astype(bf16)
        kx[h] = jnp.concatenate([jnp.where(keep, scaled, zero), dead], axis=1)
        vx[h] = jnp.concatenate([jnp.where(keep, values, zero), ones.astype(bf16)], axis=1)
    grads[:, 0 : 2 * cols] = jnp.zeros((image_len, 2 * cols), bf16)
    grad_q[...] = jnp.zeros_like(grad_q)

    def key_block(index, carry):
        here = pl.ds(pl.multiple_of(index * block, block), block)
        parts = {}
        for h in range(heads):
            probs = jnp.exp(dot(kx[h, here, :], qx[...], NT))
            grad_probs = dot(vx[h, here, :], dox[...], NT)
            grad_scores = (probs * grad_probs).astype(bf16)
            pair = slice(0, 128) if h < 2 else slice(128, 256)
            own = slice(DH * (h % 2), DH * (h % 2) + DH)
            grad_v = dot(dot_t[pair, :], probs.astype(bf16), NT)[own]
            grad_k = dot(q_t[pair, :], grad_scores, NT)[own]
            parts[h] = (grad_k * 0.125, grad_v)
            grad_q[DH * h : DH * (h + 1), :] += dot(k_t[pair, here], grad_scores)[own]
        stack = [parts[h][j] for j in range(2) for h in range(heads)]
        grads[here, 0 : 2 * cols] = jnp.transpose(jnp.concatenate(stack, axis=0).astype(bf16))
        return carry

    lax.fori_loop(0, (length + block - 1) // block, key_block, 0)
    grads[:, 2 * cols : 3 * cols] = jnp.transpose(grad_q[...].astype(bf16))

    for load in loads:
        load.wait()
    gain, shift = vec_ref[0:1, :].astype(f32), vec_ref[1:2, :].astype(f32)
    step = 256
    sums = [jnp.zeros((1, 1), f32)] * 3
    if stage:
        sums = [old[1][0:1, :], old[1][1:2, :], old[2][0:1, :]]
    for start in range(0, image_len, step):
        here = slice(start, start + step)
        unit, _ = unit_rows(x[here, :].astype(f32))
        normed[here, :] = (unit * gain + shift).astype(bf16)
        part = grads[here, :]
        da = dot(part, w_all[...])
        da_s[here, :] = da.astype(bf16)
        more = [da * unit, da, part.astype(f32)]
        sums = [old_sum + jnp.sum(new, axis=0, keepdims=True) for old_sum, new in zip(sums, more)]
    me = lax.axis_index("tensor")
    core, side = me % 2, me // 2
    if stage == 0:
        half = image_len // 2
        spans = [(core * half, half), ((1 - core) * half, half)]
    elif stage == 1:
        half = image_len // 4
        far = (1 - side) * 2 * half
        spans = [(far + core * half, half), (far + (1 - core) * half, half), (side * 2 * half, 2 * half)]
    else:
        spans = [(0, image_len)]
    stores = []
    for index, (start, size) in enumerate(spans):
        source = da_s.at[pl.ds(pl.multiple_of(start, 256), size)] if size < image_len else da_s
        stores.append(pltpu.make_async_copy(source, outs[index], sems.at[4 + index]))
        stores[-1].start()
    fresh = dot(normed[...], grads[...], TN)
    if stage:
        fresh = fresh + dw[...]
    if stage == 2:
        fresh = fresh.astype(bf16)
        at = 0
        for order, target in zip(orders, dw_outs):
            piece = fresh[:, at : at + target.shape[1]]
            at += target.shape[1]
            target[...] = dot(halving_order(order, fresh.shape[0], dp_size), piece).astype(bf16)
    else:
        dw_outs[0][...] = fresh
    small_out[...] = jnp.concatenate([sums[0], sums[1], jnp.zeros((6, sums[0].shape[1]), f32)], axis=0)
    bias_out[...] = jnp.broadcast_to(sums[2], bias_out.shape)
    for store in stores:
        store.wait()


def image_back(stage, buckets, which, kvq, lse, o, grad_o, vectors, tokens, weight, dp_size, orders, old):
    rows, width = tokens.shape
    cols = o.shape[0]
    images = buckets.shape[0]
    image_len = rows // images
    heads = cols // DH
    half = image_len // 2
    da_rows = [[half, half], [half // 2, half // 2, half], [image_len]][stage]
    picked = lambda w: pl.BlockSpec((image_len, w), lambda i, b, s: (s[0], 0))
    across = lambda w: pl.BlockSpec((w, image_len), lambda i, b, s: (0, s[0]))
    fixed = lambda shape: pl.BlockSpec(shape, lambda i, b, s: (0,) * len(shape))
    if stage == 2:
        dw_shapes = [((width, n), bf16) for n in (256, 3 * cols - 256)]
    else:
        dw_shapes = [((width, 3 * cols), f32)]
    return pl.pallas_call(
        functools.partial(image_back_kernel, block=256, stage=stage, dp_size=dp_size, orders=orders),
        grid_spec=pltpu.PrefetchScalarGridSpec(
            num_scalar_prefetch=2,
            grid=(1,),
            in_specs=[picked(3 * cols), across(8), across(cols), across(cols), fixed(vectors.shape)]
            + [ANY] * 2
            + ([ANY, fixed((8, width)), fixed((8, 3 * cols))] if stage else []),
            out_specs=[ANY] * len(da_rows)
            + [fixed(shape) for shape, _ in dw_shapes]
            + [fixed((8, width)), fixed((8, 3 * cols))],
            scratch_shapes=[
                pltpu.VMEM((image_len, 256), bf16),
                pltpu.VMEM((256, image_len), bf16),
                pltpu.VMEM((image_len, 256), bf16),
                pltpu.VMEM((256, image_len), bf16),
                pltpu.VMEM((heads, image_len, 256), bf16),
                pltpu.VMEM((heads, image_len, 256), bf16),
                pltpu.VMEM((256, image_len), bf16),
                pltpu.VMEM((cols, image_len), f32),
                pltpu.VMEM((image_len, 3 * cols), bf16),
                pltpu.VMEM((image_len, width), bf16),
                pltpu.VMEM((3 * cols, width), bf16),
                pltpu.VMEM((image_len, width), bf16),
                pltpu.VMEM((image_len, width), bf16),
                pltpu.VMEM((width, 3 * cols), f32),
                pltpu.SemaphoreType.DMA((10,)),
            ],
        ),
        out_shape=[jax.ShapeDtypeStruct((n, width), bf16) for n in da_rows]
        + [
            *[jax.ShapeDtypeStruct(*shape) for shape in dw_shapes],
            jax.ShapeDtypeStruct((8, width), f32),
            jax.ShapeDtypeStruct((8, 3 * cols), f32),
        ],
        compiler_params=pltpu.CompilerParams(vmem_limit_bytes=VMEM),
        cost_estimate=cost(10**6, 10**4),
        name=f"image_back_{stage}",
    )(buckets, which, kvq, lse, o, grad_o, vectors, tokens, weight, *old)


def rows_kernel(*refs, parts, dp_size, orders):
    refs = list(refs)
    take = lambda count: [refs.pop(0) for _ in range(count)]
    x_any, g_any, vec_ref, bias_any, o_any = take(5)
    shards, pieces = take(3), take(3)
    y_ref, e_ref, kept, sent, far_out, small_ref, do_out, wo_refs = *take(2), take(2), take(2), *take(3), take(2)
    pieces_to, across, across_to = take(3), take(2), take(2)
    quarters = [pieces + across, pieces_to + across_to]
    x_ref, g_ref, wo_w, up_w, down_w, hidden, normed, mixed, back, c_t, z_s, du_s, grads, came, do_s = take(15)
    far_came, far_next, wo_made, wo_came, o_in, bias_ref, g_t, dz_s, sems, far_sems, out_sems = take(11)
    rows, width = x_ref.shape
    hid = up_w.shape[2]
    step_index = pl.program_id(0)
    part = step_index ^ 2
    dp, me = lax.axis_index("dp"), lax.axis_index("tensor")
    quarter = dp % 4
    here = pl.ds(pl.multiple_of(me * rows, rows), rows)
    inputs = [
        pltpu.make_async_copy(x_any.at[here], x_ref, sems.at[4, 0]),
        pltpu.make_async_copy(g_any.at[here], g_ref, sems.at[4, 1]),
        pltpu.make_async_copy(o_any.at[:, here], o_in.at[0], sems.at[4, 7]),
        pltpu.make_async_copy(bias_any, bias_ref.at[0], sems.at[4, 8]),
    ]
    half, fourth = width // 2, width // 4
    partners = [(dp, me ^ r) for r in range(parts)]
    along = [(dp ^ (1 << order[0]), me) for order in orders]
    core = [send(grads.at[3 - 2 * i], came.at[i], far_sems, i, partners[1]) for i in range(2)]
    columns = [pl.ds(0, hid), pl.ds(hid, hid)]
    fars = [
        send(grads.at[2, pl.ds(half, half), columns[at]], far_came.at[at], far_sems, 2 + at, along[at]) for at in range(2)
    ]
    nexts = [
        send(grads.at[2, pl.ds(fourth, fourth), columns[at]], far_next.at[at], far_sems, 4 + at, along[1 - at])
        for at in range(2)
    ]
    mine = do_out.at[:, here]
    do_copies = [send(do_s.at[r], mine, far_sems, 5 + r, partners[r]) for r in range(parts - 1, 0, -1)]
    do_copies.append(pltpu.make_async_copy(do_s.at[0], mine, sems.at[4, 2]))
    results = [pltpu.make_async_copy(z_s, e_ref, sems.at[4, 3]), pltpu.make_async_copy(du_s, y_ref, sems.at[4, 4])]
    wo_copy = send(wo_made.at[1], wo_came, far_sems, 9, partners[1])

    beside, beyond = (dp ^ 1, me), (dp ^ 2, me)
    size = across[0].shape[0]
    across_in = [
        send(pieces[1].at[pl.ds(0, size)], across[0], out_sems, 0, beyond),
        send(pieces[2].at[pl.ds(size, across[1].shape[0])], across[1], out_sems, 1, beside),
    ]
    across_on = [send(across[i], across_to[i], out_sems, 2 + i, partners[1]) for i in range(2)]
    pieces_on = [send(pieces[i], pieces_to[i], out_sems, 4 + i, partners[1]) for i in range(3)]
    weights = (wo_w, up_w, down_w)
    shards_on = [send(shards[i], weights[i].at[1], out_sems, 7 + i, partners[1]) for i in range(3)]
    heads_in = []
    for r in range(parts - 1, 0, -1):
        theirs = pl.ds(pl.multiple_of((me ^ r) * rows, rows), rows)
        heads_in.append(send(o_any.at[:, theirs], o_in.at[r], out_sems, 9 + r, partners[r]))
        heads_in.append(send(bias_any, bias_ref.at[r], out_sems, 12 + r, partners[r]))

    def wide(block):
        return block.astype(f32)

    def add_into(target, source, count, columns=slice(None)):
        for start in range(0, count, 64):
            piece = slice(start, start + 64)
            target[piece, columns] = (wide(target[piece, columns]) + wide(source[piece, :])).astype(bf16)

    def loads(index, at):
        target, row = weights[index], index
        found = [[pltpu.make_async_copy(shards[index], target.at[0], sems.at[row, 0])], []]
        size = target.shape[1] // 4
        for r in (2, 3):
            found.append([])
            for i in range(4):
                piece, start = quarters[r - 2][i], at
                if i == 3 and at >= split:
                    piece, start = quarters[r - 2][4], at - split
                place = target.at[r, pl.ds(pl.multiple_of((quarter ^ i) * size, size), size)]
                sem = sems.at[row, 2 + 4 * (r - 2) + i]
                found[r].append(pltpu.make_async_copy(piece.at[pl.ds(start, size)], place, sem))
        return found

    mixed_cols = o_in.shape[1]
    split = (mixed_cols + hid) // 4
    groups = [loads(0, 0), loads(1, mixed_cols // 4), loads(2, split)]
    wo_loads, up_loads, down_loads = groups
    gain, shift = vec_ref[2:3, :].astype(f32), vec_ref[3:4, :].astype(f32)

    def store_own():
        return [
            pltpu.make_async_copy(
                grads.at[0, pl.ds(side * half, half), columns[at]], group[at], sems.at[3, 2 * side + at]
            )
            for side, group in enumerate((kept, sent))
            for at in range(2)
        ]

    def store_far():
        return [
            pltpu.make_async_copy(grads.at[2, pl.ds(0, fourth), columns[at]], far_out.at[at], sems.at[3, 4 + at])
            for at in range(2)
        ]

    def hidden_grads(r):
        for load in (down_loads[r] if r != 1 else shards_on[2:]):
            load.wait()
        for start in range(0, hid, 256):
            cols = slice(start, start + 256)
            dz_s[r, :, cols] = dot(g_ref[...], down_w[r, cols, :], NT).astype(bf16)

    @pl.when(step_index == 0)
    def _():
        for load in inputs:
            load.start()
        greet(partners[1:] + along)
        for copy in across_in + heads_in + shards_on[:1] + pieces_on + shards_on[1:]:
            copy.start()
        for group in groups:
            for load in group[0] + group[2][:3]:
                load.start()
        for load in inputs:
            load.wait()
        g_t[...] = dot(halving_order(orders[0], width, dp_size), g_ref[...], NT).astype(bf16)
        hidden_grads(0)
        for i in range(2):
            across_in[i].wait_recv()
            across_on[i].start()
        for group in groups:
            group[2][3].start()
        for i in range(3):
            pieces_on[i].wait()
        for group in groups:
            for load in group[3][:3]:
                load.start()
        hidden_grads(1)
        hidden_grads(2)
        for i in range(2):
            across_in[i].wait_send()
            across_on[i].wait()
        for group in groups:
            group[3][3].start()
        hidden_grads(3)
        shards_on[0].wait()
        for group in wo_loads:
            for load in group:
                load.wait()
        for copy in heads_in:
            copy.wait()
        for start in range(0, rows, 256):
            piece = slice(start, start + 256)
            attended = dot(o_in[0, :, piece], wo_w[0], TN)
            for r in range(1, parts):
                attended += dot(o_in[r, :, piece], wo_w[r], TN)
            h1 = x_ref[piece, :].astype(f32) + attended + vec_ref[4:5, :].astype(f32)
            hidden[piece, :] = h1
            unit, _ = unit_rows(h1)
            normed[piece, :] = (unit * gain + shift).astype(bf16)
        c_t[...] = dot(halving_order(orders[1], width, dp_size), normed[...], NT).astype(bf16)
        mixed[...] = jnp.zeros_like(mixed)
        back[...] = jnp.zeros_like(back)
        small_ref[...] = jnp.zeros_like(small_ref)

    for r in range(parts):

        @pl.when(part == r)
        def _():
            for load in (up_loads[r] if r != 1 else shards_on[1:2]):
                load.wait()

    step = 256
    chunks = [slice(s, s + step) for s in range(0, hid, step)]

    def first(cols):
        u = dot(normed[...], up_w[part, :, cols]) + bias_ref[part, 0:1, cols]
        return u, wide(dz_s[part, :, cols])

    def bend(cols, u, dz):
        square = u * u
        scaled = u * GELU_SCALE
        gate = 0.5 + 0.5 * jnp.tanh(scaled * (1.0 + GELU_CUBE * square))
        z_s[:, cols] = (u * gate).astype(bf16)
        slope = gate + (2.0 * gate) * (1.0 - gate) * scaled * (1.0 + (3.0 * GELU_CUBE) * square)
        du = (dz * slope).astype(bf16)
        du_s[:, cols] = du
        small_ref[pl.ds(8 + part, 1), cols] = jnp.sum(du.astype(f32), axis=0, keepdims=True)

    def weigh(cols):
        grads[part, :, cols] = dot(g_t[...], z_s[:, cols]).astype(bf16)
        later = slice(hid + cols.start, hid + cols.stop)
        grads[part, :, later] = dot(c_t[...], du_s[:, cols]).astype(bf16)

    ready = first(chunks[0])
    for index, cols in enumerate(chunks):
        following = first(chunks[index + 1]) if index + 1 < len(chunks) else None
        bend(cols, *ready)
        if index:
            weigh(chunks[index - 1])
        ready = following
    mixed[...] += dot(z_s[...], down_w[part])
    weigh(chunks[-1])
    back[...] += dot(du_s[...], up_w[part], NT)
    @pl.when(part == 3)
    def _():
        core[0].start()

    @pl.when(part == 0)
    def _():
        core[0].wait()
        add_into(grads.at[2], came.at[0], width)
        for copy in fars:
            copy.start()

    @pl.when(part == 1)
    def _():
        core[1].start()
        totals = [jnp.zeros((1, width), f32)] * 4
        for start in range(0, rows, 256):
            piece = slice(start, start + 256)
            h1 = hidden[piece, :]
            unit, inverse = unit_rows(h1)
            dc = back[piece, :]
            wide_g = wide(g_ref[piece, :])
            dh = wide_g + norm_back(dc, gain, unit, inverse)
            z_s[piece, :] = dh.astype(bf16)
            du_s[piece, :] = (h1 + mixed[piece, :] + vec_ref[5:6, :].astype(f32)).astype(bf16)
            news = [jnp.sum(values, axis=0, keepdims=True) for values in (dc * unit, dc, dh, wide_g)]
            totals = [old + new for old, new in zip(totals, news)]
        for index, values in enumerate(totals):
            small_ref[2 + index : 3 + index, :] = values
        results[1].start()
        e = z_s[...]
        results[0].start()
        for r, copy in zip(range(parts - 1, -1, -1), do_copies):
            do_s[r] = dot(wo_w[r], e, NT).astype(bf16)
            copy.start()
        for at in range(2):
            fars[at].wait()
            add_into(grads.at[2], far_came.at[at], half, columns[at])
            nexts[at].start()
        e_t = dot(halving_order(orders[0], width, dp_size), e, NT).astype(bf16)
        blank = jnp.zeros((width, 256 - mixed_cols), bf16)
        for r in range(parts):
            wo_made[r % 2, r // 2] = jnp.concatenate([dot(e_t, o_in[r], NT).astype(bf16), blank], axis=1)
        wo_copy.start()
        core[1].wait()
        add_into(grads.at[0], came.at[1], width)
        for copy in store_own():
            copy.start()
        for at in range(2):
            nexts[at].wait()
            add_into(grads.at[2], far_next.at[at], fourth, columns[at])
        for copy in store_far():
            copy.start()
        wo_copy.wait()
        for index in range(2):
            add_into(wo_made.at[0, index], wo_came.at[index], width)
        wo_stores = [
            pltpu.make_async_copy(wo_made.at[0, index], wo_refs[index], sems.at[4, 5 + index]) for index in range(2)
        ]
        for copy in wo_stores:
            copy.start()
        for copy in store_own() + store_far() + do_copies + results + wo_stores:
            copy.wait()


def own_rows(x, g, vectors, up_bias, o, shards, pieces, parts, dp_size, orders):
    cols = o.shape[0]
    rows = x.shape[0] // parts
    width = x.shape[1]
    hid = shards[1].shape[1]
    tall = pieces[0].shape[0]
    split = tall - hid // 4
    fixed = lambda shape: pl.BlockSpec(shape, lambda r: (0,) * len(shape))
    array = lambda *shape: jax.ShapeDtypeStruct(shape, bf16)
    out = pl.pallas_call(
        functools.partial(rows_kernel, parts=parts, dp_size=dp_size, orders=orders),
        grid=(parts,),
        in_specs=[
            ANY,
            ANY,
            fixed(vectors.shape),
        ]
        + [ANY] * 8,
        out_specs=[ANY] * 7 + [fixed((16, width)), ANY] + [ANY] * 9,
        out_shape=[array(rows, width)] * 2
        + [array(width // 2, hid)] * 4
        + [array(2, width // 4, hid)]
        + [jax.ShapeDtypeStruct((16, width), f32), array(cols, x.shape[0])]
        + [array(width, 256)] * 2
        + [array(tall, width)] * 3
        + [array(split, width), array(tall - split, width)] * 2,
        scratch_shapes=[
            pltpu.VMEM((rows, width), bf16),
            pltpu.VMEM((rows, width), bf16),
            pltpu.VMEM((parts, cols, width), bf16),
            pltpu.VMEM((parts, width, hid), bf16),
            pltpu.VMEM((parts, hid, width), bf16),
            pltpu.VMEM((rows, width), f32),
            pltpu.VMEM((rows, width), bf16),
            pltpu.VMEM((rows, width), f32),
            pltpu.VMEM((rows, width), f32),
            pltpu.VMEM((width, rows), bf16),
            pltpu.VMEM((rows, hid), bf16),
            pltpu.VMEM((rows, hid), bf16),
            pltpu.VMEM((parts, width, 2 * hid), bf16),
            pltpu.VMEM((2, width, 2 * hid), bf16),
            pltpu.VMEM((parts, cols, rows), bf16),
            pltpu.VMEM((2, width // 2, hid), bf16),
            pltpu.VMEM((2, width // 4, hid), bf16),
            pltpu.VMEM((2, 2, width, 256), bf16),
            pltpu.VMEM((2, width, 256), bf16),
            pltpu.VMEM((parts, cols, rows), bf16),
            pltpu.VMEM((parts,) + up_bias.shape, f32),
            pltpu.VMEM((width, rows), bf16),
            pltpu.VMEM((parts, rows, hid), bf16),
            pltpu.SemaphoreType.DMA((5, 12)),
            pltpu.SemaphoreType.DMA((2, 10)),
            pltpu.SemaphoreType.DMA((2, 16)),
        ],
        compiler_params=pltpu.CompilerParams(collective_id=4, has_side_effects=True, vmem_limit_bytes=VMEM),
        cost_estimate=cost(12 * rows * width * hid * parts, 8 * parts * width * hid, rows * hid * parts),
        name="own_rows",
    )(x, g, vectors, up_bias, o, *shards, *pieces)
    return out[0], out[1], out[2:4], out[4:6], out[6], out[7], out[8], out[9:11]


def greet(partners):
    barrier = pltpu.get_barrier_semaphore()
    for partner in partners:
        pl.semaphore_signal(barrier, inc=1, device_id=partner, device_id_type=pl.DeviceIdType.MESH)
    pl.semaphore_wait(barrier, len(partners))


def send(source, target, sems, index, partner):
    return pltpu.make_async_remote_copy(
        src_ref=source,
        dst_ref=target,
        send_sem=sems.at[0, index],
        recv_sem=sems.at[1, index],
        device_id=partner,
        device_id_type=pl.DeviceIdType.MESH,
    )


def pick_kernel(*refs):
    *sources, target, sems = refs
    quarter = lax.axis_index("dp") % 4
    copies, at = [], 0
    for index, source in enumerate(sources):
        size = source.shape[0] // 4
        piece = source.at[pl.ds(pl.multiple_of(quarter * size, size), size)]
        copies.append(pltpu.make_async_copy(piece, target.at[pl.ds(at, size)], sems.at[index]))
        copies[index].start()
        at += size
    for copy in copies:
        copy.wait()


def pick_quarter(shards):
    rows = sum(shard.shape[0] for shard in shards) // 4
    return pl.pallas_call(
        pick_kernel,
        in_specs=[ANY] * len(shards),
        out_specs=pl.BlockSpec(memory_space=pltpu.VMEM),
        out_shape=jax.ShapeDtypeStruct((rows, shards[0].shape[1]), bf16),
        scratch_shapes=[pltpu.SemaphoreType.DMA((len(shards),))],
        name="pick_quarter",
    )(*shards)


def finish_kernel(
    own_any, mid_any, far_own_any, mid_keep_any, mid_came_any, x_any, dh_any, vec_ref, late_ref, bias_ref, early_ref, *refs,
    dp_size, tracks,
):
    bits = dp_size.bit_length() - 1
    refs = list(refs)
    take = lambda count: [refs.pop(0) for _ in range(count)]
    weights = [take(1), take(1), take(2)]
    kept_one, kept_two, came = take(3)
    weights += [[kept_one, came.at[0]], [kept_two, came.at[1]]]
    (out_ref,) = take(1)
    weights_out = take(len(tracks))
    (sums_out,) = take(1)
    held, other, far_own, mid_keep, mid_came, far_mid, x_v, dh_v = take(8)
    sent = [take(len(order)) for order in tracks]
    got = [take(len(order)) for order in tracks]
    totals = take(len(tracks))
    sums, got_s, sems, w_sems, local = refs
    dp, me = lax.axis_index("dp"), lax.axis_index("tensor")
    core, side = me % 2, me // 2
    rows, width = out_ref.shape
    image_len = own_any.shape[0]
    half = image_len // 2
    x_own = x_any.at[pl.ds(pl.multiple_of(me * rows, rows), rows)]
    at_own = side * half
    at_mid = (1 - side) * image_len
    across = [(dp, me ^ 1), (dp, me ^ 2)]
    along = [(dp ^ (1 << bit), me) for bit in range(bits)]
    greet(across + along)

    loads = [
        pltpu.make_async_copy(own_any, held.at[pl.ds(pl.multiple_of(at_own, half), image_len)], local.at[0]),
        pltpu.make_async_copy(mid_any, held.at[pl.ds(pl.multiple_of(at_mid, half), half)], local.at[1]),
        pltpu.make_async_copy(far_own_any, far_own, local.at[2]),
        pltpu.make_async_copy(mid_keep_any, mid_keep, local.at[3]),
        pltpu.make_async_copy(mid_came_any, mid_came, local.at[6]),
        pltpu.make_async_copy(x_own, x_v, local.at[4]),
        pltpu.make_async_copy(dh_any, dh_v, local.at[5]),
    ]
    for load in loads:
        load.start()
    copies = [[] for _ in tracks]
    tall = [totals[track].shape[0] for track in range(len(tracks))]

    def first(track, here):
        terms = [term[here, :].astype(f32) for term in weights[track]]
        return terms[0] + terms[1] if len(terms) > 1 else terms[0]

    def send_weight(track, step):
        target = sent[track][step]
        span = tall[track] // 2
        if step == 0:
            target[...] = first(track, slice(span, 2 * span)).astype(target.dtype)
        else:
            target[...] = totals[track][span : 2 * span, :].astype(target.dtype)
        route = along[tracks[track][step]]
        index = sum(len(order) for order in tracks[:track]) + step
        copies[track].append(send(target, got[track][step], w_sems, index, route))
        copies[track][step].start()

    def add_weight(track, step):
        copies[track][step].wait()
        tall[track] //= 2
        span = tall[track]
        kept = totals[track][0:span, :] if step else first(track, slice(0, span))
        totals[track][0:span, :] = kept + got[track][step][...].astype(f32)

    for track in range(len(tracks)):
        if tracks[track]:
            send_weight(track, 0)
    mid_load = loads.pop(4)
    mid_load.wait()
    loads[3].wait()
    mid_keep[...] = (mid_keep[...].astype(f32) + mid_came[...].astype(f32)).astype(bf16)
    mid_copy = send(mid_keep, far_mid, sems, 14, across[1])

    sums[...] = early_ref[...]
    sums[0:2, :] = late_ref[0:2, :]
    sums[12:13, 0 : bias_ref.shape[1]] = bias_ref[0:1, :]
    routes = across + along
    s_copies = []

    def send_sums(step):
        s_copies.append(send(sums, got_s.at[step], sems, step, routes[step]))
        s_copies[step].start()

    def add_sums(step):
        s_copies[step].wait()
        if step < 2:
            sums[0:6, :] += got_s[step, 0:6, :]
            new = [sums[8 + r : 9 + r, :] + got_s[step, 8 + (r ^ (1 << step)) : 9 + (r ^ (1 << step)), :] for r in range(4)]
            for r in range(4):
                sums[8 + r : 9 + r, :] = new[r]
        else:
            sums[...] += got_s[step]

    def turn(track, step):
        add_weight(track, step)
        if step + 1 < len(tracks[track]):
            send_weight(track, step + 1)

    mid_copy.start()
    send_sums(0)
    for load in loads[:3]:
        load.wait()
    here = pl.ds(pl.multiple_of(at_own + core * half, half), half)
    held[here, :] = (held[here, :].astype(f32) + far_own[...].astype(f32)).astype(bf16)
    turn(0, 0)
    add_sums(0)
    send_sums(1)
    turn(1, 0)
    turn(2, 0)
    add_sums(1)
    send_sums(2)
    turn(0, 1)
    mid_copy.wait()

    here = pl.ds(pl.multiple_of(at_mid + core * (half // 2), half // 2), half // 2)
    held[here, :] = (held[here, :].astype(f32) + far_mid[...].astype(f32)).astype(bf16)
    theirs = held.at[pl.ds(pl.multiple_of((1 - core) * rows, rows), rows)]
    da_copy = send(theirs, other, sems, 15, across[0])
    da_copy.start()
    turn(1, 1)
    turn(2, 1)
    add_sums(2)
    if bits > 1:
        send_sums(3)
    for load in loads[4:]:
        load.wait()
    da_copy.wait()
    gain = vec_ref[0:1, :].astype(f32)
    step = 256
    for start in range(0, rows, step):
        piece = slice(start, start + step)
        unit, inverse = unit_rows(x_v[piece, :].astype(f32))
        mine = held[pl.ds(pl.multiple_of(core * rows + start, step), step), :].astype(f32)
        da = mine + other[piece, :].astype(f32)
        out_ref[piece, :] = (dh_v[piece, :].astype(f32) + norm_back(da, gain, unit, inverse)).astype(bf16)

    for step in range(2, bits):
        for track in range(3):
            turn(track, step)
        add_sums(1 + step)
        if step < bits:
            send_sums(2 + step)
    add_sums(1 + bits)
    for step in range(bits):
        for track in (3, 4):
            if step < len(tracks[track]):
                turn(track, step)
    for track in range(len(tracks)):
        if tracks[track]:
            weights_out[track][...] = totals[track][0 : weights_out[track].shape[0], :]
        else:
            weights_out[track][...] = first(track, slice(None))
    sums_out[...] = sums[...]


def unpack_kernel(out_ref, dw_one, dw_two, wo_in, down_ref, up_ref, sums_ref, out_to, qkv_to, wo_to, down_to, up_to, bias_to, *vectors_to):
    for index, target in zip((0, 1, 2, 3, 4, 5, 8), vectors_to):
        target[...] = sums_ref[index, :]
    out_to[...] = out_ref[...]
    down_to[...] = down_ref[...]
    up_to[...] = up_ref[...]
    cols = wo_to.shape[0]
    dw_ref = jnp.concatenate([dw_one[...], dw_two[...]], axis=1)
    for index, at in enumerate((2, 0, 1)):
        qkv_to[index] = dw_ref[:, at * cols : (at + 1) * cols]
    wo_to[...] = jnp.transpose(wo_in[...])[0:cols]
    for index, at in enumerate((2, 1)):
        bias_to[index : index + 1, :] = sums_ref[12:13, at * cols : (at + 1) * cols]


def unpack(out, dw_one, dw_two, wo, down, up, sums, cols):
    rows = dw_one.shape[0]
    vmem = pl.BlockSpec(memory_space=pltpu.VMEM)
    array = lambda *shape: jax.ShapeDtypeStruct(shape, f32)
    return pl.pallas_call(
        unpack_kernel,
        in_specs=[vmem] * 7,
        out_specs=[vmem] * 13,
        out_shape=[
            jax.ShapeDtypeStruct(out.shape, bf16),
            array(3, rows, cols),
            array(cols, rows),
            array(*down.shape),
            array(*up.shape),
            array(2, cols),
            *[array(sums.shape[1])] * 7,
        ],
        compiler_params=pltpu.CompilerParams(vmem_limit_bytes=VMEM),
        name="unpack",
    )(out, dw_one, dw_two, wo, down, up, sums)


def finish(own, mid, far_own, mid_keep, mid_came, x, dh, vectors, late, bias, early, weights, came, tracks, dp_size):
    rows, width = dh.shape
    bits = dp_size.bit_length() - 1
    buffers, totals = [], []
    for group, order in zip(weights, tracks):
        tall, wide = group[0].shape[-2:]
        totals.append(pltpu.VMEM((tall, wide), f32))
        for bit in order:
            tall //= 2
            buffers.append(pltpu.VMEM((tall, wide), bf16 if tall % 16 == 0 else f32))
    count = sum(len(order) for order in tracks)
    flat = [weight for group in weights for weight in group] + [came]
    vmem = pl.BlockSpec(memory_space=pltpu.VMEM)
    return pl.pallas_call(
        functools.partial(finish_kernel, dp_size=dp_size, tracks=tracks),
        in_specs=[ANY] * 7 + [vmem] * (4 + len(flat)),
        out_specs=[vmem] * (2 + len(tracks)),
        out_shape=[jax.ShapeDtypeStruct((rows, width), bf16)]
        + [jax.ShapeDtypeStruct((width // dp_size, group[0].shape[-1]), f32) for group in weights]
        + [jax.ShapeDtypeStruct((16, width), f32)],
        scratch_shapes=[
            pltpu.VMEM((2 * rows, width), bf16),
            pltpu.VMEM((rows, width), bf16),
            pltpu.VMEM(far_own.shape, bf16),
            pltpu.VMEM(mid_keep.shape, bf16),
            pltpu.VMEM(mid_keep.shape, bf16),
            pltpu.VMEM(mid_keep.shape, bf16),
            pltpu.VMEM((rows, width), bf16),
            pltpu.VMEM((rows, width), bf16),
        ]
        + buffers * 2
        + totals
        + [
            pltpu.VMEM((16, width), f32),
            pltpu.VMEM((2 + bits, 16, width), f32),
            pltpu.SemaphoreType.DMA((2, 16)),
            pltpu.SemaphoreType.DMA((2, count)),
            pltpu.SemaphoreType.DMA((7,)),
        ],
        compiler_params=pltpu.CompilerParams(
            collective_id=3, has_side_effects=True, vmem_limit_bytes=VMEM
        ),
        name="finish",
    )(own, mid, far_own, mid_keep, mid_came, x, dh, vectors, late, bias, early, *flat)


def on_device(
    dp_size, tokens, buckets, norm1_gain, norm1_bias, qkv_weight, qkv_bias, out_weight, out_bias,
    norm2_gain, norm2_bias, up_weight, up_bias, down_weight, down_bias, cotangent,
):
    parts = 4
    dp_bits = dp_size.bit_length() - 1
    me = lax.axis_index("tensor")
    token_rows, width = tokens.shape
    share = token_rows // parts
    hid = up_weight.shape[1]
    cols = qkv_weight.shape[2]

    def over_tensor(values, mask):
        return lax.ppermute(values, "tensor", [(i, i ^ mask) for i in range(parts)])

    def over_dp(values, mask):
        return lax.ppermute(values, "dp", [(i, i ^ mask) for i in range(dp_size)])

    def add(*terms):
        total = terms[0].astype(f32)
        for term in terms[1:]:
            total = total + term.astype(f32)
        return total.astype(bf16)

    shards = (out_weight, up_weight, down_weight)
    near = over_tensor(pick_quarter(shards), 2)
    blank = jnp.zeros_like(norm1_gain)
    vectors = jnp.stack(
        [norm1_gain, norm1_bias, norm2_gain, norm2_bias, out_bias, down_bias, blank, blank]
    )
    up_bias_rows = jnp.broadcast_to(up_bias.astype(f32)[None], (8, hid))
    orders = [list(range(dp_bits)), [1, 0] + list(range(2, dp_bits))]
    turned_weight = jnp.swapaxes(qkv_weight, 1, 2)
    kvq, bound = project(tokens, vectors, turned_weight, qkv_bias)
    near, kvq = lax.optimization_barrier((near, kvq))
    beside, along = over_dp(near, 1), over_dp(near, 2)
    o, lse = attend(buckets, kvq, bound)
    near, beside, along, o = lax.optimization_barrier((near, beside, along, o))
    layer_out, e, kept, sent, far, early, grad_o, grad_wo = own_rows(
        tokens, cotangent, vectors, up_bias_rows, o, shards, (near, beside, along), parts, dp_size, orders
    )

    tie = lax.optimization_barrier
    got = [over_dp(half, 1 << order[0]) for half, order in zip(sent, orders)]
    crossed, wo_far = over_tensor(far, 2), over_tensor(grad_wo[1], 2)

    side = me // 2
    order = [2 - 2 * side, jnp.ones_like(side), 2 * side]
    run = lambda stage, old, o: image_back(
        stage, buckets, order[stage].reshape(1).astype(jnp.int32), kvq, lse, o, grad_o, vectors, tokens, turned_weight,
        dp_size, orders, old,
    )
    da_keep, da_send, *old = run(0, [], o)
    came, first_keep = over_tensor(da_send, 1), da_keep
    *got, o = tie((*got, o, *old))[:3]
    split = width // 4
    sent = [add(k[split:], g[split:]) for k, g in zip(kept, got)]
    kept = [add(k[:split], g[:split]) for k, g in zip(kept, got)]
    got = [over_dp(half, 1 << order[1]) for half, order in zip(sent, orders)]
    mid_keep, da_send, mid, *old = run(1, old, o)
    came, o, wo_far, crossed, *got = tie((came, o, wo_far, crossed, *got, *old))[:6]
    far_own = over_tensor(add(first_keep, came), 2)
    mid_came = over_tensor(da_send, 1)
    split //= 2
    terms = list(zip(kept, got, crossed))
    sent = jnp.stack([add(*[t[split:] for t in group]) for group in terms])
    kept = [add(*[t[:split] for t in group]) for group in terms]
    got = over_dp(sent, 1 << orders[0][2])
    own, *dw, late, bias_sums = run(2, old, o)
    got, far_own, mid_came, own, wo_far = tie((got, far_own, mid_came, own, wo_far))
    weights = [dw[:1], dw[1:], [grad_wo[0], wo_far]] + [[k] for k in kept]
    tracks = [orders[0], orders[1], orders[0], orders[0][3:], orders[1][3:]]
    out, dw_one, dw_two, wo_out, down_out, grad_up, sums = finish(
        own, mid, far_own, mid_keep, mid_came, tokens, e, vectors, late, bias_sums, early, weights, got, tracks, dp_size
    )
    input_grad, grad_qkv_weight, grad_out, down_out, grad_up, grad_qkv_bias, *vectors_out = unpack(
        out, dw_one, dw_two, wo_out, down_out, grad_up, sums, cols
    )
    grad_down = down_out.T
    return (
        layer_out,
        input_grad,
        vectors_out[0],
        vectors_out[1],
        grad_qkv_weight,
        grad_qkv_bias,
        grad_out,
        vectors_out[4],
        vectors_out[2],
        vectors_out[3],
        grad_up,
        vectors_out[6],
        grad_down,
        vectors_out[5],
    )


def solution(mesh):
    return jax.shard_map(
        functools.partial(on_device, mesh.shape["dp"]),
        mesh=mesh,
        in_specs=(
            P("dp", None),
            P("dp"),
            P(),
            P(),
            P(None, None, "tensor"),
            P(None, "tensor"),
            P("tensor", None),
            P(),
            P(),
            P(),
            P(None, "tensor"),
            P("tensor"),
            P("tensor", None),
            P(),
            P("dp", None),
        ),
        out_specs=(
            P(("dp", "tensor"), None),
            P(("dp", "tensor"), None),
            P(),
            P(),
            P(None, "dp", "tensor"),
            P(None, "tensor"),
            P("tensor", "dp"),
            P(),
            P(),
            P(),
            P("dp", "tensor"),
            P("tensor"),
            P("tensor", "dp"),
            P(),
        ),
        check_vma=False,
    )
```

```python
import functools

import jax
import jax.numpy as jnp
from jax import lax
from jax.experimental import pallas as pl
from jax.experimental.pallas import tpu as pltpu
from jax.sharding import PartitionSpec as P

DH = 64
NORM_EPSILON = 1e-06
GRID_SIXTEENTHS = (16, 15, 15, 12, 12, 8, 8, 6, 6)
GELU_SCALE = 0.7978845608028654
GELU_CUBE = 0.044715
VMEM = 60 << 20
NN = (((1,), (0,)), ((), ()))
NT = (((1,), (1,)), ((), ()))
TN = (((0,), (0,)), ((), ()))
bf16 = jnp.bfloat16
f32 = jnp.float32
ANY = pl.BlockSpec(memory_space=pl.ANY)


def dot(left, right, dims=NN):
    return lax.dot_general(left, right, dims, preferred_element_type=f32)


def lanes(rows, width):
    return lax.broadcasted_iota(jnp.int32, (rows, width), 1)


def live_lengths(image_len):
    return sorted({image_len * s // 16 for s in GRID_SIXTEENTHS})


def live_length(bucket, image_len):
    length = jnp.int32(0)
    for index, sixteenths in enumerate(GRID_SIXTEENTHS):
        length = jnp.where(bucket == index, image_len * sixteenths // 16, length)
    return length


def cost(flops, nbytes, transcendentals=0):
    return pl.CostEstimate(flops=flops, bytes_accessed=nbytes, transcendentals=transcendentals)


def split3(values):
    high = values.astype(bf16).astype(f32)
    middle = (values - high).astype(bf16).astype(f32)
    return high, middle, values - high - middle


def halving_order(order, width, dp_size):
    bits = dp_size.bit_length() - 1
    size = width // dp_size
    place = lax.broadcasted_iota(jnp.int32, (width, 128), 0)
    block = jnp.zeros_like(place)
    for index in range(1, dp_size):
        block = block + (place >= index * size).astype(jnp.int32)
    turned = jnp.zeros_like(block)
    for step, bit in enumerate(order):
        turned = turned | (((block >> (bits - 1 - step)) & 1) << bit)
    source = (turned ^ lax.axis_index("dp")) * size + (place - block * size)
    lane = lanes(width, 128)
    return jnp.concatenate(
        [jnp.where(source == lane + start, 1.0, 0.0).astype(bf16) for start in range(0, width, 128)], axis=1
    )


def unit_rows(values):
    centred = values - jnp.mean(values, axis=-1, keepdims=True)
    spread = jnp.mean(centred * centred, axis=-1, keepdims=True)
    inverse = lax.rsqrt(spread + NORM_EPSILON)
    return centred * inverse, inverse


def norm_back(grad, gain, unit, inverse):
    scaled = grad * gain
    mean_one = jnp.mean(scaled, axis=-1, keepdims=True)
    mean_two = jnp.mean(scaled * unit, axis=-1, keepdims=True)
    return inverse * (scaled - mean_one - unit * mean_two)


def project_kernel(x_ref, vec_ref, w_ref, bias_ref, out_ref, bound_ref, w_all):
    cols = w_ref.shape[1]

    @pl.when(pl.program_id(0) == 0)
    def _():
        for index, source in enumerate((1, 2, 0)):
            w_all[index * cols : (index + 1) * cols, :] = w_ref[source]

    gain, shift = vec_ref[0:1, :].astype(f32), vec_ref[1:2, :].astype(f32)
    bias = bias_ref[...].astype(f32)
    bias = jnp.concatenate([jnp.zeros((1, cols), f32), bias[1:2], bias[0:1]], axis=1)
    rows, step = x_ref.shape[0], 128
    row = lax.broadcasted_iota(jnp.int32, (3 * cols, 128), 0)
    pick = jnp.where(row // DH == lanes(3 * cols, 128), 1.0, 0.0).astype(bf16)

    def normed(start):
        unit, _ = unit_rows(x_ref[start : start + step, :].astype(f32))
        return (unit * gain + shift).astype(bf16)

    largest = None
    ready = normed(0)
    for start in range(0, rows, step):
        following = normed(start + step) if start + step < rows else None
        values = (dot(ready, w_all[...], NT) + bias).astype(bf16)
        out_ref[start : start + step, :] = values
        squares = jnp.max(dot(values * values, pick), axis=0, keepdims=True)
        largest = squares if largest is None else jnp.maximum(largest, squares)
        ready = following
    bound_ref[0] = jnp.broadcast_to(largest, (8, 128))


def project(tokens, vectors, weight, bias):
    rows, width = tokens.shape
    cols = weight.shape[1]
    block = 512
    fixed = lambda shape: pl.BlockSpec(shape, lambda i: (0,) * len(shape))
    return pl.pallas_call(
        project_kernel,
        grid=(rows // block,),
        in_specs=[
            pl.BlockSpec((block, width), lambda i: (i, 0)),
            fixed(vectors.shape),
            fixed(weight.shape),
            fixed(bias.shape),
        ],
        out_specs=[
            pl.BlockSpec((block, 3 * cols), lambda i: (i, 0)),
            pl.BlockSpec((1, 8, 128), lambda i: (i, 0, 0)),
        ],
        out_shape=[
            jax.ShapeDtypeStruct((rows, 3 * cols), bf16),
            jax.ShapeDtypeStruct((rows // block, 8, 128), f32),
        ],
        scratch_shapes=[pltpu.VMEM((3 * cols, width), bf16)],
        compiler_params=pltpu.CompilerParams(vmem_limit_bytes=VMEM),
        cost_estimate=cost(6 * rows * width * cols, 2 * rows * (width + 3 * cols)),
        name="project",
    )(tokens, vectors, weight, bias)


def attend_kernel(bucket_ref, kvq_ref, bound_ref, o_ref, lse_ref, kx, vt, *, block):
    cols, image_len = o_ref.shape
    heads = cols // DH
    at_q = 2 * cols
    length = live_length(bucket_ref[pl.program_id(0)], image_len)
    squares = jnp.max(bound_ref[...], axis=0)
    lane = lanes(8, 128)
    largest_key = jnp.max(jnp.where(lane < heads, squares, 0.0))
    of_query = (lane >= 2 * heads) & (lane < 3 * heads)
    largest_query = jnp.max(jnp.where(of_query, squares, 0.0))
    small = largest_key * largest_query <= (8.0 * 60.0) ** 2

    def run(live, subtract):
        scaled = kvq_ref[0:live, 0:192] * jnp.asarray(0.125, bf16)
        flipped = jnp.transpose(kvq_ref[0:live, 128:384])
        lane = lanes(live, 128)
        for h in range(heads):
            if h < 2:
                keep = (lane < DH) if h == 0 else (lane >= DH)
                kx[h, 0:live, :] = jnp.where(keep, scaled[:, 0:128], jnp.zeros((), bf16))
            else:
                kx[h, 0:live, 0:DH] = scaled[:, 128:192]
            vt[h, 0:DH, 0:live] = flipped[DH * (h + 1) : DH * (h + 2)]
            vt[h, DH:128, 0:live] = jnp.ones((DH, live), bf16)

        def scores(h, start):
            here = slice(start, start + block)
            if h < 2:
                return dot(kx[h, 0:live, :], kvq_ref[here, at_q : at_q + 128], NT)
            return dot(kx[h, 0:live, 0:DH], kvq_ref[here, at_q + 128 : at_q + 192], NT)

        parts = {}

        def finish(h, start, score):
            offset = 0.0
            if subtract:
                key = lax.broadcasted_iota(jnp.int32, score.shape, 0)
                score = jnp.where(key < length, score, -1e30)
                offset = jnp.max(score, axis=0, keepdims=True)
                score = score - offset
            mixed = dot(vt[h, :, 0:live], jnp.exp(score).astype(bf16))
            total = mixed[DH : DH + 1]
            here = slice(start, start + block)
            parts[h] = -(offset + jnp.log(total))
            o_ref[DH * h : DH * (h + 1), here] = (mixed[:DH] * (1.0 / total)).astype(bf16)
            if h == heads - 1:
                rows = [parts[i] for i in range(heads)]
                lse_ref[:, here] = jnp.concatenate(rows + [jnp.zeros((8 - heads, block), f32)], axis=0)

        items = [(h, s) for s in range(0, image_len, block) for h in range(heads)]
        score = scores(*items[0])
        for index, item in enumerate(items):
            following = scores(*items[index + 1]) if index + 1 < len(items) else None
            finish(*item, score)
            score = following

    for live in live_lengths(image_len):
        pl.when(small & (length == live))(functools.partial(run, live, False))
    pl.when(jnp.logical_not(small))(functools.partial(run, image_len, True))


def attend(buckets, kvq, bound):
    rows = kvq.shape[0]
    cols = kvq.shape[1] // 3
    images = buckets.shape[0]
    image_len = rows // images
    heads = cols // DH
    by_rows = lambda w: pl.BlockSpec((image_len, w), lambda i, b: (i, 0))
    by_cols = lambda w: pl.BlockSpec((w, image_len), lambda i, b: (0, i))
    return pl.pallas_call(
        functools.partial(attend_kernel, block=512),
        grid_spec=pltpu.PrefetchScalarGridSpec(
            num_scalar_prefetch=1,
            grid=(images,),
            in_specs=[by_rows(3 * cols), pl.BlockSpec(bound.shape, lambda i, b: (0, 0, 0))],
            out_specs=[by_cols(cols), by_cols(8)],
            scratch_shapes=[
                pltpu.VMEM((heads, image_len, 128), bf16),
                pltpu.VMEM((heads, 128, image_len), bf16),
            ],
        ),
        out_shape=[
            jax.ShapeDtypeStruct((cols, rows), bf16),
            jax.ShapeDtypeStruct((8, rows), f32),
        ],
        compiler_params=pltpu.CompilerParams(vmem_limit_bytes=VMEM),
        cost_estimate=cost(16 * rows * image_len * cols, 12 * rows * cols, rows * image_len * heads),
        name="attend",
    )(buckets, kvq, bound)


def image_back_kernel(bucket_ref, which_ref, kvq_ref, lse_ref, o_ref, do_ref, vec_ref, *refs, block, stage, dp_size, orders):
    refs = list(refs)
    take = lambda count: [refs.pop(0) for _ in range(count)]
    x_any, w_any = take(2)
    old = take(3) if stage else None
    outs = take((2, 3, 1)[stage])
    dw_outs = take(2 if stage == 2 else 1)
    small_out, bias_out = take(2)
    dox, dot_t, qx, q_t, kx, vx, k_t, grad_q, grads, x, w_all, da_s, normed, dw, sems = take(15)
    cols, image_len = o_ref.shape
    heads = cols // DH
    image = which_ref[0]
    loads = [
        pltpu.make_async_copy(x_any.at[pl.ds(image * image_len, image_len)], x, sems.at[0]),
    ]
    for index, source in enumerate((1, 2, 0)):
        target = w_all.at[pl.ds(index * cols, cols)]
        loads.append(pltpu.make_async_copy(w_any.at[source], target, sems.at[7 + index]))
    if stage:
        loads.append(pltpu.make_async_copy(old[0], dw, sems.at[3]))
    for load in loads:
        load.start()
    length = live_length(bucket_ref[image], image_len)
    inner = []
    for h in range(heads):
        own = slice(DH * h, DH * (h + 1))
        product = do_ref[own, :].astype(f32) * o_ref[own, :].astype(f32)
        inner += list(split3(-jnp.sum(product, axis=0, keepdims=True)))
    blank = [jnp.zeros((DH - 3 * heads, image_len), f32)]
    dot_t[0:cols, :] = do_ref[...]
    dot_t[cols:, :] = jnp.concatenate(inner + blank, axis=0).astype(bf16)
    dox[...] = jnp.transpose(dot_t[...])
    outer = [part for h in range(heads) for part in split3(lse_ref[h : h + 1, :])]
    row = lax.broadcasted_iota(jnp.int32, (DH - 3 * heads, image_len), 0)
    outer = jnp.concatenate(outer + [jnp.where(row == 0, 1.0, 0.0)], axis=0).astype(bf16)
    q = kvq_ref[:, 2 * cols : 3 * cols]
    q_t[0:cols, :] = jnp.transpose(q)
    q_t[cols:, :] = outer
    qx[...] = jnp.concatenate([q, jnp.transpose(outer)], axis=1)
    scaled = kvq_ref[:, 0:cols] * jnp.asarray(0.125, bf16)
    values = kvq_ref[:, cols : 2 * cols]
    k_t[0:cols, :] = jnp.transpose(scaled)
    lane, side = lanes(image_len, cols), lanes(image_len, DH)
    key = lax.broadcasted_iota(jnp.int32, (image_len, DH), 0)
    zero = jnp.zeros((), bf16)
    for h in range(heads):
        keep = (lane >= DH * h) & (lane < DH * (h + 1))
        ones = jnp.where((side >= 3 * h) & (side < 3 * h + 3), 1.0, 0.0)
        dead = jnp.where((side == 3 * heads) & (key >= length), -1e30, ones).astype(bf16)
        kx[h] = jnp.concatenate([jnp.where(keep, scaled, zero), dead], axis=1)
        vx[h] = jnp.concatenate([jnp.where(keep, values, zero), ones.astype(bf16)], axis=1)
    grads[:, 0 : 2 * cols] = jnp.zeros((image_len, 2 * cols), bf16)
    grad_q[...] = jnp.zeros_like(grad_q)

    def key_block(index, carry):
        here = pl.ds(pl.multiple_of(index * block, block), block)
        parts = {}
        for h in range(heads):
            probs = jnp.exp(dot(kx[h, here, :], qx[...], NT))
            grad_probs = dot(vx[h, here, :], dox[...], NT)
            grad_scores = (probs * grad_probs).astype(bf16)
            pair = slice(0, 128) if h < 2 else slice(128, 256)
            own = slice(DH * (h % 2), DH * (h % 2) + DH)
            grad_v = dot(dot_t[pair, :], probs.astype(bf16), NT)[own]
            grad_k = dot(q_t[pair, :], grad_scores, NT)[own]
            parts[h] = (grad_k * 0.125, grad_v)
            grad_q[DH * h : DH * (h + 1), :] += dot(k_t[pair, here], grad_scores)[own]
        stack = [parts[h][j] for j in range(2) for h in range(heads)]
        grads[here, 0 : 2 * cols] = jnp.transpose(jnp.concatenate(stack, axis=0).astype(bf16))
        return carry

    lax.fori_loop(0, (length + block - 1) // block, key_block, 0)
    grads[:, 2 * cols : 3 * cols] = jnp.transpose(grad_q[...].astype(bf16))

    for load in loads:
        load.wait()
    gain, shift = vec_ref[0:1, :].astype(f32), vec_ref[1:2, :].astype(f32)
    step = 256
    sums = [jnp.zeros((1, 1), f32)] * 3
    if stage:
        sums = [old[1][0:1, :], old[1][1:2, :], old[2][0:1, :]]
    for start in range(0, image_len, step):
        here = slice(start, start + step)
        unit, _ = unit_rows(x[here, :].astype(f32))
        normed[here, :] = (unit * gain + shift).astype(bf16)
        part = grads[here, :]
        da = dot(part, w_all[...])
        da_s[here, :] = da.astype(bf16)
        more = [da * unit, da, part.astype(f32)]
        sums = [old_sum + jnp.sum(new, axis=0, keepdims=True) for old_sum, new in zip(sums, more)]
    me = lax.axis_index("tensor")
    core, side = me % 2, me // 2
    if stage == 0:
        half = image_len // 2
        spans = [(core * half, half), ((1 - core) * half, half)]
    elif stage == 1:
        half = image_len // 4
        far = (1 - side) * 2 * half
        spans = [(far + core * half, half), (far + (1 - core) * half, half), (side * 2 * half, 2 * half)]
    else:
        spans = [(0, image_len)]
    stores = []
    for index, (start, size) in enumerate(spans):
        source = da_s.at[pl.ds(pl.multiple_of(start, 256), size)] if size < image_len else da_s
        stores.append(pltpu.make_async_copy(source, outs[index], sems.at[4 + index]))
        stores[-1].start()
    fresh = dot(normed[...], grads[...], TN)
    if stage:
        fresh = fresh + dw[...]
    if stage == 2:
        fresh = fresh.astype(bf16)
        at = 0
        for order, target in zip(orders, dw_outs):
            piece = fresh[:, at : at + target.shape[1]]
            at += target.shape[1]
            target[...] = dot(halving_order(order, fresh.shape[0], dp_size), piece).astype(bf16)
    else:
        dw_outs[0][...] = fresh
    small_out[...] = jnp.concatenate([sums[0], sums[1], jnp.zeros((6, sums[0].shape[1]), f32)], axis=0)
    bias_out[...] = jnp.broadcast_to(sums[2], bias_out.shape)
    for store in stores:
        store.wait()


def image_back(stage, buckets, which, kvq, lse, o, grad_o, vectors, tokens, weight, dp_size, orders, old):
    rows, width = tokens.shape
    cols = o.shape[0]
    images = buckets.shape[0]
    image_len = rows // images
    heads = cols // DH
    half = image_len // 2
    da_rows = [[half, half], [half // 2, half // 2, half], [image_len]][stage]
    picked = lambda w: pl.BlockSpec((image_len, w), lambda i, b, s: (s[0], 0))
    across = lambda w: pl.BlockSpec((w, image_len), lambda i, b, s: (0, s[0]))
    fixed = lambda shape: pl.BlockSpec(shape, lambda i, b, s: (0,) * len(shape))
    if stage == 2:
        dw_shapes = [((width, n), bf16) for n in (384, 3 * cols - 384)]
    else:
        dw_shapes = [((width, 3 * cols), f32)]
    return pl.pallas_call(
        functools.partial(image_back_kernel, block=256, stage=stage, dp_size=dp_size, orders=orders),
        grid_spec=pltpu.PrefetchScalarGridSpec(
            num_scalar_prefetch=2,
            grid=(1,),
            in_specs=[picked(3 * cols), across(8), across(cols), across(cols), fixed(vectors.shape)]
            + [ANY] * 2
            + ([ANY, fixed((8, width)), fixed((8, 3 * cols))] if stage else []),
            out_specs=[ANY] * len(da_rows)
            + [fixed(shape) for shape, _ in dw_shapes]
            + [fixed((8, width)), fixed((8, 3 * cols))],
            scratch_shapes=[
                pltpu.VMEM((image_len, 256), bf16),
                pltpu.VMEM((256, image_len), bf16),
                pltpu.VMEM((image_len, 256), bf16),
                pltpu.VMEM((256, image_len), bf16),
                pltpu.VMEM((heads, image_len, 256), bf16),
                pltpu.VMEM((heads, image_len, 256), bf16),
                pltpu.VMEM((256, image_len), bf16),
                pltpu.VMEM((cols, image_len), f32),
                pltpu.VMEM((image_len, 3 * cols), bf16),
                pltpu.VMEM((image_len, width), bf16),
                pltpu.VMEM((3 * cols, width), bf16),
                pltpu.VMEM((image_len, width), bf16),
                pltpu.VMEM((image_len, width), bf16),
                pltpu.VMEM((width, 3 * cols), f32),
                pltpu.SemaphoreType.DMA((10,)),
            ],
        ),
        out_shape=[jax.ShapeDtypeStruct((n, width), bf16) for n in da_rows]
        + [
            *[jax.ShapeDtypeStruct(*shape) for shape in dw_shapes],
            jax.ShapeDtypeStruct((8, width), f32),
            jax.ShapeDtypeStruct((8, 3 * cols), f32),
        ],
        compiler_params=pltpu.CompilerParams(vmem_limit_bytes=VMEM),
        cost_estimate=cost(10**6, 10**4),
        name=f"image_back_{stage}",
    )(buckets, which, kvq, lse, o, grad_o, vectors, tokens, weight, *old)


def rows_kernel(*refs, parts, dp_size, orders):
    refs = list(refs)
    take = lambda count: [refs.pop(0) for _ in range(count)]
    x_any, g_any, vec_ref, bias_any, o_any = take(5)
    shards, pieces = take(3), take(3)
    y_ref, e_ref, kept, sent, far_out, small_ref, do_out, wo_refs = *take(2), take(2), take(2), *take(3), take(2)
    pieces_to, across, across_to = take(3), take(2), take(2)
    quarters = [pieces + across, pieces_to + across_to]
    x_ref, g_ref, wo_w, up_w, down_w, hidden, normed, mixed, back, c_t, z_s, du_s, grads, came, do_s = take(15)
    far_came, far_next, wo_made, wo_came, o_in, bias_ref, g_t, dz_s, sems, far_sems, out_sems = take(11)
    rows, width = x_ref.shape
    hid = up_w.shape[2]
    step_index = pl.program_id(0)
    part = step_index ^ 2
    dp, me = lax.axis_index("dp"), lax.axis_index("tensor")
    quarter = dp % 4
    here = pl.ds(pl.multiple_of(me * rows, rows), rows)
    inputs = [
        pltpu.make_async_copy(x_any.at[here], x_ref, sems.at[4, 0]),
        pltpu.make_async_copy(g_any.at[here], g_ref, sems.at[4, 1]),
        pltpu.make_async_copy(o_any.at[:, here], o_in.at[0], sems.at[4, 7]),
        pltpu.make_async_copy(bias_any, bias_ref.at[0], sems.at[4, 8]),
    ]
    half, fourth = width // 2, width // 4
    partners = [(dp, me ^ r) for r in range(parts)]
    along = [(dp ^ (1 << order[0]), me) for order in orders]
    core = [send(grads.at[3 - 2 * i], came.at[i], far_sems, i, partners[1]) for i in range(2)]
    columns = [pl.ds(0, hid), pl.ds(hid, hid)]
    fars = [
        send(grads.at[2, pl.ds(half, half), columns[at]], far_came.at[at], far_sems, 2 + at, along[at]) for at in range(2)
    ]
    nexts = [
        send(grads.at[2, pl.ds(fourth, fourth), columns[at]], far_next.at[at], far_sems, 4 + at, along[1 - at])
        for at in range(2)
    ]
    mine = do_out.at[:, here]
    do_copies = [send(do_s.at[r], mine, far_sems, 5 + r, partners[r]) for r in range(parts - 1, 0, -1)]
    do_copies.append(pltpu.make_async_copy(do_s.at[0], mine, sems.at[4, 2]))
    results = [pltpu.make_async_copy(z_s, e_ref, sems.at[4, 3]), pltpu.make_async_copy(du_s, y_ref, sems.at[4, 4])]
    wo_copy = send(wo_made.at[1], wo_came, far_sems, 9, partners[1])

    beside, beyond = (dp ^ 1, me), (dp ^ 2, me)
    size = across[0].shape[0]
    across_in = [
        send(pieces[1].at[pl.ds(0, size)], across[0], out_sems, 0, beyond),
        send(pieces[2].at[pl.ds(size, across[1].shape[0])], across[1], out_sems, 1, beside),
    ]
    across_on = [send(across[i], across_to[i], out_sems, 2 + i, partners[1]) for i in range(2)]
    pieces_on = [send(pieces[i], pieces_to[i], out_sems, 4 + i, partners[1]) for i in range(3)]
    weights = (wo_w, up_w, down_w)
    shards_on = [send(shards[i], weights[i].at[1], out_sems, 7 + i, partners[1]) for i in range(3)]
    heads_in = []
    for r in range(parts - 1, 0, -1):
        theirs = pl.ds(pl.multiple_of((me ^ r) * rows, rows), rows)
        heads_in.append(send(o_any.at[:, theirs], o_in.at[r], out_sems, 9 + r, partners[r]))
        heads_in.append(send(bias_any, bias_ref.at[r], out_sems, 12 + r, partners[r]))

    def wide(block):
        return block.astype(f32)

    def add_into(target, source, count, columns=slice(None)):
        for start in range(0, count, 64):
            piece = slice(start, start + 64)
            target[piece, columns] = (wide(target[piece, columns]) + wide(source[piece, :])).astype(bf16)

    def loads(index, at):
        target, row = weights[index], index
        found = [[pltpu.make_async_copy(shards[index], target.at[0], sems.at[row, 0])], []]
        size = target.shape[1] // 4
        for r in (2, 3):
            found.append([])
            for i in range(4):
                piece, start = quarters[r - 2][i], at
                if i == 3 and at >= split:
                    piece, start = quarters[r - 2][4], at - split
                place = target.at[r, pl.ds(pl.multiple_of((quarter ^ i) * size, size), size)]
                sem = sems.at[row, 2 + 4 * (r - 2) + i]
                found[r].append(pltpu.make_async_copy(piece.at[pl.ds(start, size)], place, sem))
        return found

    mixed_cols = o_in.shape[1]
    split = (mixed_cols + hid) // 4
    groups = [loads(0, 0), loads(1, mixed_cols // 4), loads(2, split)]
    wo_loads, up_loads, down_loads = groups
    gain, shift = vec_ref[2:3, :].astype(f32), vec_ref[3:4, :].astype(f32)

    def store_own():
        return [
            pltpu.make_async_copy(
                grads.at[0, pl.ds(side * half, half), columns[at]], group[at], sems.at[3, 2 * side + at]
            )
            for side, group in enumerate((kept, sent))
            for at in range(2)
        ]

    def store_far():
        return [
            pltpu.make_async_copy(grads.at[2, pl.ds(0, fourth), columns[at]], far_out.at[at], sems.at[3, 4 + at])
            for at in range(2)
        ]

    def hidden_grads(r):
        for load in (down_loads[r] if r != 1 else shards_on[2:]):
            load.wait()
        for start in range(0, hid, 256):
            cols = slice(start, start + 256)
            dz_s[r, :, cols] = dot(g_ref[...], down_w[r, cols, :], NT).astype(bf16)

    @pl.when(step_index == 0)
    def _():
        for load in inputs:
            load.start()
        greet(partners[1:] + along)
        for copy in across_in + heads_in + shards_on[:1] + pieces_on + shards_on[1:]:
            copy.start()
        for group in groups:
            for load in group[0] + group[2][:3]:
                load.start()
        for load in inputs:
            load.wait()
        g_t[...] = dot(halving_order(orders[0], width, dp_size), g_ref[...], NT).astype(bf16)
        hidden_grads(0)
        for i in range(2):
            across_in[i].wait_recv()
            across_on[i].start()
        for group in groups:
            group[2][3].start()
        for i in range(3):
            pieces_on[i].wait()
        for group in groups:
            for load in group[3][:3]:
                load.start()
        hidden_grads(1)
        hidden_grads(2)
        for i in range(2):
            across_in[i].wait_send()
            across_on[i].wait()
        for group in groups:
            group[3][3].start()
        hidden_grads(3)
        shards_on[0].wait()
        for group in wo_loads:
            for load in group:
                load.wait()
        for copy in heads_in:
            copy.wait()
        for start in range(0, rows, 256):
            piece = slice(start, start + 256)
            attended = dot(o_in[0, :, piece], wo_w[0], TN)
            for r in range(1, parts):
                attended += dot(o_in[r, :, piece], wo_w[r], TN)
            h1 = x_ref[piece, :].astype(f32) + attended + vec_ref[4:5, :].astype(f32)
            hidden[piece, :] = h1
            unit, _ = unit_rows(h1)
            normed[piece, :] = (unit * gain + shift).astype(bf16)
        c_t[...] = dot(halving_order(orders[1], width, dp_size), normed[...], NT).astype(bf16)
        mixed[...] = jnp.zeros_like(mixed)
        back[...] = jnp.zeros_like(back)
        small_ref[...] = jnp.zeros_like(small_ref)

    for r in range(parts):

        @pl.when(part == r)
        def _():
            for load in (up_loads[r] if r != 1 else shards_on[1:2]):
                load.wait()

    step = 256
    chunks = [slice(s, s + step) for s in range(0, hid, step)]

    def first(cols):
        u = dot(normed[...], up_w[part, :, cols]) + bias_ref[part, 0:1, cols]
        return u, wide(dz_s[part, :, cols])

    def bend(cols, u, dz):
        square = u * u
        scaled = u * GELU_SCALE
        gate = 0.5 + 0.5 * jnp.tanh(scaled * (1.0 + GELU_CUBE * square))
        z_s[:, cols] = (u * gate).astype(bf16)
        slope = gate + (2.0 * gate) * (1.0 - gate) * scaled * (1.0 + (3.0 * GELU_CUBE) * square)
        du = (dz * slope).astype(bf16)
        du_s[:, cols] = du
        small_ref[pl.ds(8 + part, 1), cols] = jnp.sum(du.astype(f32), axis=0, keepdims=True)

    def weigh(cols):
        grads[part, :, cols] = dot(g_t[...], z_s[:, cols]).astype(bf16)
        later = slice(hid + cols.start, hid + cols.stop)
        grads[part, :, later] = dot(c_t[...], du_s[:, cols]).astype(bf16)

    ready = first(chunks[0])
    for index, cols in enumerate(chunks):
        following = first(chunks[index + 1]) if index + 1 < len(chunks) else None
        bend(cols, *ready)
        if index:
            weigh(chunks[index - 1])
        ready = following
    mixed[...] += dot(z_s[...], down_w[part])
    weigh(chunks[-1])
    back[...] += dot(du_s[...], up_w[part], NT)
    @pl.when(part == 3)
    def _():
        core[0].start()

    @pl.when(part == 0)
    def _():
        core[0].wait()
        add_into(grads.at[2], came.at[0], width)
        for copy in fars:
            copy.start()

    @pl.when(part == 1)
    def _():
        core[1].start()
        totals = [jnp.zeros((1, width), f32)] * 4
        for start in range(0, rows, 256):
            piece = slice(start, start + 256)
            h1 = hidden[piece, :]
            unit, inverse = unit_rows(h1)
            dc = back[piece, :]
            wide_g = wide(g_ref[piece, :])
            dh = wide_g + norm_back(dc, gain, unit, inverse)
            z_s[piece, :] = dh.astype(bf16)
            du_s[piece, :] = (h1 + mixed[piece, :] + vec_ref[5:6, :].astype(f32)).astype(bf16)
            news = [jnp.sum(values, axis=0, keepdims=True) for values in (dc * unit, dc, dh, wide_g)]
            totals = [old + new for old, new in zip(totals, news)]
        for index, values in enumerate(totals):
            small_ref[2 + index : 3 + index, :] = values
        results[1].start()
        e = z_s[...]
        results[0].start()
        for r, copy in zip(range(parts - 1, -1, -1), do_copies):
            do_s[r] = dot(wo_w[r], e, NT).astype(bf16)
            copy.start()
        for at in range(2):
            fars[at].wait()
            add_into(grads.at[2], far_came.at[at], half, columns[at])
            nexts[at].start()
        e_t = dot(halving_order(orders[0], width, dp_size), e, NT).astype(bf16)
        blank = jnp.zeros((width, 256 - mixed_cols), bf16)
        for r in range(parts):
            wo_made[r % 2, r // 2] = jnp.concatenate([dot(e_t, o_in[r], NT).astype(bf16), blank], axis=1)
        wo_copy.start()
        core[1].wait()
        add_into(grads.at[0], came.at[1], width)
        for copy in store_own():
            copy.start()
        for at in range(2):
            nexts[at].wait()
            add_into(grads.at[2], far_next.at[at], fourth, columns[at])
        for copy in store_far():
            copy.start()
        wo_copy.wait()
        for index in range(2):
            add_into(wo_made.at[0, index], wo_came.at[index], width)
        wo_stores = [
            pltpu.make_async_copy(wo_made.at[0, index], wo_refs[index], sems.at[4, 5 + index]) for index in range(2)
        ]
        for copy in wo_stores:
            copy.start()
        for copy in store_own() + store_far() + do_copies + results + wo_stores:
            copy.wait()


def own_rows(x, g, vectors, up_bias, o, shards, pieces, parts, dp_size, orders):
    cols = o.shape[0]
    rows = x.shape[0] // parts
    width = x.shape[1]
    hid = shards[1].shape[1]
    tall = pieces[0].shape[0]
    split = tall - hid // 4
    fixed = lambda shape: pl.BlockSpec(shape, lambda r: (0,) * len(shape))
    array = lambda *shape: jax.ShapeDtypeStruct(shape, bf16)
    out = pl.pallas_call(
        functools.partial(rows_kernel, parts=parts, dp_size=dp_size, orders=orders),
        grid=(parts,),
        in_specs=[
            ANY,
            ANY,
            fixed(vectors.shape),
        ]
        + [ANY] * 8,
        out_specs=[ANY] * 7 + [fixed((16, width)), ANY] + [ANY] * 9,
        out_shape=[array(rows, width)] * 2
        + [array(width // 2, hid)] * 4
        + [array(2, width // 4, hid)]
        + [jax.ShapeDtypeStruct((16, width), f32), array(cols, x.shape[0])]
        + [array(width, 256)] * 2
        + [array(tall, width)] * 3
        + [array(split, width), array(tall - split, width)] * 2,
        scratch_shapes=[
            pltpu.VMEM((rows, width), bf16),
            pltpu.VMEM((rows, width), bf16),
            pltpu.VMEM((parts, cols, width), bf16),
            pltpu.VMEM((parts, width, hid), bf16),
            pltpu.VMEM((parts, hid, width), bf16),
            pltpu.VMEM((rows, width), f32),
            pltpu.VMEM((rows, width), bf16),
            pltpu.VMEM((rows, width), f32),
            pltpu.VMEM((rows, width), f32),
            pltpu.VMEM((width, rows), bf16),
            pltpu.VMEM((rows, hid), bf16),
            pltpu.VMEM((rows, hid), bf16),
            pltpu.VMEM((parts, width, 2 * hid), bf16),
            pltpu.VMEM((2, width, 2 * hid), bf16),
            pltpu.VMEM((parts, cols, rows), bf16),
            pltpu.VMEM((2, width // 2, hid), bf16),
            pltpu.VMEM((2, width // 4, hid), bf16),
            pltpu.VMEM((2, 2, width, 256), bf16),
            pltpu.VMEM((2, width, 256), bf16),
            pltpu.VMEM((parts, cols, rows), bf16),
            pltpu.VMEM((parts,) + up_bias.shape, f32),
            pltpu.VMEM((width, rows), bf16),
            pltpu.VMEM((parts, rows, hid), bf16),
            pltpu.SemaphoreType.DMA((5, 12)),
            pltpu.SemaphoreType.DMA((2, 10)),
            pltpu.SemaphoreType.DMA((2, 16)),
        ],
        compiler_params=pltpu.CompilerParams(collective_id=4, has_side_effects=True, vmem_limit_bytes=VMEM),
        cost_estimate=cost(12 * rows * width * hid * parts, 8 * parts * width * hid, rows * hid * parts),
        name="own_rows",
    )(x, g, vectors, up_bias, o, *shards, *pieces)
    return out[0], out[1], out[2:4], out[4:6], out[6], out[7], out[8], out[9:11]


def greet(partners):
    barrier = pltpu.get_barrier_semaphore()
    for partner in partners:
        pl.semaphore_signal(barrier, inc=1, device_id=partner, device_id_type=pl.DeviceIdType.MESH)
    pl.semaphore_wait(barrier, len(partners))


def send(source, target, sems, index, partner):
    return pltpu.make_async_remote_copy(
        src_ref=source,
        dst_ref=target,
        send_sem=sems.at[0, index],
        recv_sem=sems.at[1, index],
        device_id=partner,
        device_id_type=pl.DeviceIdType.MESH,
    )


def pick_kernel(*refs):
    *sources, target, sems = refs
    quarter = lax.axis_index("dp") % 4
    copies, at = [], 0
    for index, source in enumerate(sources):
        size = source.shape[0] // 4
        piece = source.at[pl.ds(pl.multiple_of(quarter * size, size), size)]
        copies.append(pltpu.make_async_copy(piece, target.at[pl.ds(at, size)], sems.at[index]))
        copies[index].start()
        at += size
    for copy in copies:
        copy.wait()


def pick_quarter(shards):
    rows = sum(shard.shape[0] for shard in shards) // 4
    return pl.pallas_call(
        pick_kernel,
        in_specs=[ANY] * len(shards),
        out_specs=pl.BlockSpec(memory_space=pltpu.VMEM),
        out_shape=jax.ShapeDtypeStruct((rows, shards[0].shape[1]), bf16),
        scratch_shapes=[pltpu.SemaphoreType.DMA((len(shards),))],
        name="pick_quarter",
    )(*shards)


def finish_kernel(
    own_any, mid_any, far_own_any, mid_keep_any, mid_came_any, x_any, dh_any, vec_ref, late_ref, bias_ref, early_ref, *refs,
    dp_size, tracks,
):
    bits = dp_size.bit_length() - 1
    refs = list(refs)
    take = lambda count: [refs.pop(0) for _ in range(count)]
    weights = [take(1), take(1), take(2)]
    kept_one, kept_two, came = take(3)
    weights += [[kept_one, came.at[0]], [kept_two, came.at[1]]]
    (out_ref,) = take(1)
    weights_out = take(len(tracks))
    (sums_out,) = take(1)
    held, other, far_own, mid_keep, mid_came, far_mid, x_v, dh_v = take(8)
    sent = [take(len(order)) for order in tracks]
    got = [take(len(order)) for order in tracks]
    totals = take(len(tracks))
    sums, got_s, sems, w_sems, local = refs
    dp, me = lax.axis_index("dp"), lax.axis_index("tensor")
    core, side = me % 2, me // 2
    rows, width = out_ref.shape
    image_len = own_any.shape[0]
    half = image_len // 2
    x_own = x_any.at[pl.ds(pl.multiple_of(me * rows, rows), rows)]
    at_own = side * half
    at_mid = (1 - side) * image_len
    across = [(dp, me ^ 1), (dp, me ^ 2)]
    along = [(dp ^ (1 << bit), me) for bit in range(bits)]
    greet(across + along)

    loads = [
        pltpu.make_async_copy(own_any, held.at[pl.ds(pl.multiple_of(at_own, half), image_len)], local.at[0]),
        pltpu.make_async_copy(mid_any, held.at[pl.ds(pl.multiple_of(at_mid, half), half)], local.at[1]),
        pltpu.make_async_copy(far_own_any, far_own, local.at[2]),
        pltpu.make_async_copy(mid_keep_any, mid_keep, local.at[3]),
        pltpu.make_async_copy(mid_came_any, mid_came, local.at[6]),
        pltpu.make_async_copy(x_own, x_v, local.at[4]),
        pltpu.make_async_copy(dh_any, dh_v, local.at[5]),
    ]
    for load in loads:
        load.start()
    copies = [[] for _ in tracks]
    tall = [totals[track].shape[0] for track in range(len(tracks))]

    def first(track, here):
        terms = [term[here, :].astype(f32) for term in weights[track]]
        return terms[0] + terms[1] if len(terms) > 1 else terms[0]

    def send_weight(track, step):
        target = sent[track][step]
        span = tall[track] // 2
        if step == 0:
            target[...] = first(track, slice(span, 2 * span)).astype(target.dtype)
        else:
            target[...] = totals[track][span : 2 * span, :].astype(target.dtype)
        route = along[tracks[track][step]]
        index = sum(len(order) for order in tracks[:track]) + step
        copies[track].append(send(target, got[track][step], w_sems, index, route))
        copies[track][step].start()

    def add_weight(track, step):
        copies[track][step].wait()
        tall[track] //= 2
        span = tall[track]
        kept = totals[track][0:span, :] if step else first(track, slice(0, span))
        totals[track][0:span, :] = kept + got[track][step][...].astype(f32)

    for track in range(len(tracks)):
        if tracks[track]:
            send_weight(track, 0)
    mid_load = loads.pop(4)
    mid_load.wait()
    loads[3].wait()
    mid_keep[...] = (mid_keep[...].astype(f32) + mid_came[...].astype(f32)).astype(bf16)
    mid_copy = send(mid_keep, far_mid, sems, 14, across[1])

    sums[...] = early_ref[...]
    sums[0:2, :] = late_ref[0:2, :]
    sums[12:13, 0 : bias_ref.shape[1]] = bias_ref[0:1, :]
    routes = across + along
    s_copies = []

    def send_sums(step):
        s_copies.append(send(sums, got_s.at[step], sems, step, routes[step]))
        s_copies[step].start()

    def add_sums(step):
        s_copies[step].wait()
        if step < 2:
            sums[0:6, :] += got_s[step, 0:6, :]
            new = [sums[8 + r : 9 + r, :] + got_s[step, 8 + (r ^ (1 << step)) : 9 + (r ^ (1 << step)), :] for r in range(4)]
            for r in range(4):
                sums[8 + r : 9 + r, :] = new[r]
        else:
            sums[...] += got_s[step]

    def turn(track, step):
        add_weight(track, step)
        if step + 1 < len(tracks[track]):
            send_weight(track, step + 1)

    mid_copy.start()
    send_sums(0)
    for load in loads[:3]:
        load.wait()
    here = pl.ds(pl.multiple_of(at_own + core * half, half), half)
    held[here, :] = (held[here, :].astype(f32) + far_own[...].astype(f32)).astype(bf16)
    turn(0, 0)
    add_sums(0)
    send_sums(1)
    turn(1, 0)
    turn(2, 0)
    add_sums(1)
    send_sums(2)
    turn(0, 1)
    mid_copy.wait()

    here = pl.ds(pl.multiple_of(at_mid + core * (half // 2), half // 2), half // 2)
    held[here, :] = (held[here, :].astype(f32) + far_mid[...].astype(f32)).astype(bf16)
    theirs = held.at[pl.ds(pl.multiple_of((1 - core) * rows, rows), rows)]
    da_copy = send(theirs, other, sems, 15, across[0])
    da_copy.start()
    turn(1, 1)
    turn(2, 1)
    add_sums(2)
    if bits > 1:
        send_sums(3)
    for load in loads[4:]:
        load.wait()
    da_copy.wait()
    gain = vec_ref[0:1, :].astype(f32)
    step = 256
    for start in range(0, rows, step):
        piece = slice(start, start + step)
        unit, inverse = unit_rows(x_v[piece, :].astype(f32))
        mine = held[pl.ds(pl.multiple_of(core * rows + start, step), step), :].astype(f32)
        da = mine + other[piece, :].astype(f32)
        out_ref[piece, :] = (dh_v[piece, :].astype(f32) + norm_back(da, gain, unit, inverse)).astype(bf16)

    for step in range(2, bits):
        for track in range(3):
            turn(track, step)
        add_sums(1 + step)
        if step < bits:
            send_sums(2 + step)
    add_sums(1 + bits)
    for step in range(bits):
        for track in (3, 4):
            if step < len(tracks[track]):
                turn(track, step)
    for track in range(len(tracks)):
        if tracks[track]:
            weights_out[track][...] = totals[track][0 : weights_out[track].shape[0], :]
        else:
            weights_out[track][...] = first(track, slice(None))
    sums_out[...] = sums[...]


def unpack_kernel(out_ref, dw_one, dw_two, wo_in, down_ref, up_ref, sums_ref, out_to, qkv_to, wo_to, down_to, up_to, bias_to, *vectors_to):
    for index, target in zip((0, 1, 2, 3, 4, 5, 8), vectors_to):
        target[...] = sums_ref[index, :]
    out_to[...] = out_ref[...]
    down_to[...] = down_ref[...]
    up_to[...] = up_ref[...]
    cols = wo_to.shape[0]
    dw_ref = jnp.concatenate([dw_one[...], dw_two[...]], axis=1)
    for index, at in enumerate((2, 0, 1)):
        qkv_to[index] = dw_ref[:, at * cols : (at + 1) * cols]
    wo_to[...] = jnp.transpose(wo_in[...])[0:cols]
    for index, at in enumerate((2, 1)):
        bias_to[index : index + 1, :] = sums_ref[12:13, at * cols : (at + 1) * cols]


def unpack(out, dw_one, dw_two, wo, down, up, sums, cols):
    rows = dw_one.shape[0]
    vmem = pl.BlockSpec(memory_space=pltpu.VMEM)
    array = lambda *shape: jax.ShapeDtypeStruct(shape, f32)
    return pl.pallas_call(
        unpack_kernel,
        in_specs=[vmem] * 7,
        out_specs=[vmem] * 13,
        out_shape=[
            jax.ShapeDtypeStruct(out.shape, bf16),
            array(3, rows, cols),
            array(cols, rows),
            array(*down.shape),
            array(*up.shape),
            array(2, cols),
            *[array(sums.shape[1])] * 7,
        ],
        compiler_params=pltpu.CompilerParams(vmem_limit_bytes=VMEM),
        name="unpack",
    )(out, dw_one, dw_two, wo, down, up, sums)


def finish(own, mid, far_own, mid_keep, mid_came, x, dh, vectors, late, bias, early, weights, came, tracks, dp_size):
    rows, width = dh.shape
    bits = dp_size.bit_length() - 1
    buffers, totals = [], []
    for group, order in zip(weights, tracks):
        tall, wide = group[0].shape[-2:]
        totals.append(pltpu.VMEM((tall, wide), f32))
        for bit in order:
            tall //= 2
            buffers.append(pltpu.VMEM((tall, wide), bf16 if tall % 16 == 0 else f32))
    count = sum(len(order) for order in tracks)
    flat = [weight for group in weights for weight in group] + [came]
    vmem = pl.BlockSpec(memory_space=pltpu.VMEM)
    return pl.pallas_call(
        functools.partial(finish_kernel, dp_size=dp_size, tracks=tracks),
        in_specs=[ANY] * 7 + [vmem] * (4 + len(flat)),
        out_specs=[vmem] * (2 + len(tracks)),
        out_shape=[jax.ShapeDtypeStruct((rows, width), bf16)]
        + [jax.ShapeDtypeStruct((width // dp_size, group[0].shape[-1]), f32) for group in weights]
        + [jax.ShapeDtypeStruct((16, width), f32)],
        scratch_shapes=[
            pltpu.VMEM((2 * rows, width), bf16),
            pltpu.VMEM((rows, width), bf16),
            pltpu.VMEM(far_own.shape, bf16),
            pltpu.VMEM(mid_keep.shape, bf16),
            pltpu.VMEM(mid_keep.shape, bf16),
            pltpu.VMEM(mid_keep.shape, bf16),
            pltpu.VMEM((rows, width), bf16),
            pltpu.VMEM((rows, width), bf16),
        ]
        + buffers * 2
        + totals
        + [
            pltpu.VMEM((16, width), f32),
            pltpu.VMEM((2 + bits, 16, width), f32),
            pltpu.SemaphoreType.DMA((2, 16)),
            pltpu.SemaphoreType.DMA((2, count)),
            pltpu.SemaphoreType.DMA((7,)),
        ],
        compiler_params=pltpu.CompilerParams(
            collective_id=3, has_side_effects=True, vmem_limit_bytes=VMEM
        ),
        name="finish",
    )(own, mid, far_own, mid_keep, mid_came, x, dh, vectors, late, bias, early, *flat)


def on_device(
    dp_size, tokens, buckets, norm1_gain, norm1_bias, qkv_weight, qkv_bias, out_weight, out_bias,
    norm2_gain, norm2_bias, up_weight, up_bias, down_weight, down_bias, cotangent,
):
    parts = 4
    dp_bits = dp_size.bit_length() - 1
    me = lax.axis_index("tensor")
    token_rows, width = tokens.shape
    share = token_rows // parts
    hid = up_weight.shape[1]
    cols = qkv_weight.shape[2]

    def over_tensor(values, mask):
        return lax.ppermute(values, "tensor", [(i, i ^ mask) for i in range(parts)])

    def over_dp(values, mask):
        return lax.ppermute(values, "dp", [(i, i ^ mask) for i in range(dp_size)])

    def add(*terms):
        total = terms[0].astype(f32)
        for term in terms[1:]:
            total = total + term.astype(f32)
        return total.astype(bf16)

    shards = (out_weight, up_weight, down_weight)
    near = over_tensor(pick_quarter(shards), 2)
    blank = jnp.zeros_like(norm1_gain)
    vectors = jnp.stack(
        [norm1_gain, norm1_bias, norm2_gain, norm2_bias, out_bias, down_bias, blank, blank]
    )
    up_bias_rows = jnp.broadcast_to(up_bias.astype(f32)[None], (8, hid))
    orders = [list(range(dp_bits)), [1, 0] + list(range(2, dp_bits))]
    turned_weight = jnp.swapaxes(qkv_weight, 1, 2)
    kvq, bound = project(tokens, vectors, turned_weight, qkv_bias)
    near, kvq = lax.optimization_barrier((near, kvq))
    beside, along = over_dp(near, 1), over_dp(near, 2)
    o, lse = attend(buckets, kvq, bound)
    near, beside, along, o = lax.optimization_barrier((near, beside, along, o))
    layer_out, e, kept, sent, far, early, grad_o, grad_wo = own_rows(
        tokens, cotangent, vectors, up_bias_rows, o, shards, (near, beside, along), parts, dp_size, orders
    )

    tie = lax.optimization_barrier
    got = [over_dp(half, 1 << order[0]) for half, order in zip(sent, orders)]
    crossed, wo_far = over_tensor(far, 2), over_tensor(grad_wo[1], 2)

    side = me // 2
    order = [2 - 2 * side, jnp.ones_like(side), 2 * side]
    run = lambda stage, old, o: image_back(
        stage, buckets, order[stage].reshape(1).astype(jnp.int32), kvq, lse, o, grad_o, vectors, tokens, turned_weight,
        dp_size, orders, old,
    )
    da_keep, da_send, *old = run(0, [], o)
    came, first_keep = over_tensor(da_send, 1), da_keep
    *got, o = tie((*got, o, *old))[:3]
    split = width // 4
    sent = [add(k[split:], g[split:]) for k, g in zip(kept, got)]
    kept = [add(k[:split], g[:split]) for k, g in zip(kept, got)]
    got = [over_dp(half, 1 << order[1]) for half, order in zip(sent, orders)]
    mid_keep, da_send, mid, *old = run(1, old, o)
    came, o, wo_far, crossed, *got = tie((came, o, wo_far, crossed, *got, *old))[:6]
    far_own = over_tensor(add(first_keep, came), 2)
    mid_came = over_tensor(da_send, 1)
    split //= 2
    terms = list(zip(kept, got, crossed))
    sent = jnp.stack([add(*[t[split:] for t in group]) for group in terms])
    kept = [add(*[t[:split] for t in group]) for group in terms]
    got = over_dp(sent, 1 << orders[0][2])
    own, *dw, late, bias_sums = run(2, old, o)
    got, far_own, mid_came, own, wo_far = tie((got, far_own, mid_came, own, wo_far))
    weights = [dw[:1], dw[1:], [grad_wo[0], wo_far]] + [[k] for k in kept]
    tracks = [orders[0], orders[1], orders[0], orders[0][3:], orders[1][3:]]
    out, dw_one, dw_two, wo_out, down_out, grad_up, sums = finish(
        own, mid, far_own, mid_keep, mid_came, tokens, e, vectors, late, bias_sums, early, weights, got, tracks, dp_size
    )
    input_grad, grad_qkv_weight, grad_out, down_out, grad_up, grad_qkv_bias, *vectors_out = unpack(
        out, dw_one, dw_two, wo_out, down_out, grad_up, sums, cols
    )
    grad_down = down_out.T
    return (
        layer_out,
        input_grad,
        vectors_out[0],
        vectors_out[1],
        grad_qkv_weight,
        grad_qkv_bias,
        grad_out,
        vectors_out[4],
        vectors_out[2],
        vectors_out[3],
        grad_up,
        vectors_out[6],
        grad_down,
        vectors_out[5],
    )


def solution(mesh):
    return jax.shard_map(
        functools.partial(on_device, mesh.shape["dp"]),
        mesh=mesh,
        in_specs=(
            P("dp", None),
            P("dp"),
            P(),
            P(),
            P(None, None, "tensor"),
            P(None, "tensor"),
            P("tensor", None),
            P(),
            P(),
            P(),
            P(None, "tensor"),
            P("tensor"),
            P("tensor", None),
            P(),
            P("dp", None),
        ),
        out_specs=(
            P(("dp", "tensor"), None),
            P(("dp", "tensor"), None),
            P(),
            P(),
            P(None, "dp", "tensor"),
            P(None, "tensor"),
            P("tensor", "dp"),
            P(),
            P(),
            P(),
            P("dp", "tensor"),
            P("tensor"),
            P("tensor", "dp"),
            P(),
        ),
        check_vma=False,
    )
```
